128 devices in a mesh: seg: 8 (over y, core), col: 16 (over x, z).
Axes of the slice: x: 4, y: 4, z: 4, core: 2. Of those that a mesh axis runs over, the one named last changes fastest.
Arguments:
- segment_state: float32 [16, 2, 32, 32768], P('seg', None, None, 'col'), may hold values from -6 to 6
- light: float32 [16, 32, 32768], P('seg', None, 'col'), may hold values from 0.05 to 1
- mixing: float32 [16, 6, 32, 32768], P('seg', None, None, 'col'), may hold values from 0.04 to 0.3
- kappa: float32 [16, 32, 32768], P('seg', None, 'col'), may hold values from 0.05 to 2
- neighbour_columns: int32 [32768, 6], P('col'), may hold values from 0 to 32767, as said below
- wet_levels: int32 [32768], P('col'), may hold values from 1 to 32
- basis: float32 [4, 16, 2, 32, 32768], P(None, 'seg', None, None, 'col'), may hold values from -0.0009765625 to 0.0009765625
Outputs:
- residual: float32 [16, 2, 32, 32768], P('seg', None, None, 'col')
- new_vector: float32 [16, 2, 32, 32768], P('seg', None, None, 'col')
- coefficients: float32 [5], replicated
The draws below stay inside these ranges and needn't reach their ends.
Inputs may be any that keep to these rules, and one draw needn't show every extreme that they name: `neighbour_columns`: entry 0 of each row is the column itself; every entry lies within 512 columns of its own column, counted cyclically over all 32768 columns, and that distance is reached on both sides by the first and last column of every block of 2048 columns.
All inputs are finite; a program needn't handle non-finite values.
Results may differ from the reference program's by a relative error of at most 0.00013.
Values sent between devices are 32-bit elements; how exact they have to be, the bound alone decides.
No kernel may reach another device: no remote copies, remote signals or barrier semaphores. Data moves between devices by JAX's collectives and lax.ppermute only.
A program may use at most 128 MiB of HBM per device.

```python
import math
import jax
import jax.numpy as jnp
from jax import lax

TRACERS = 2
LEV = 32
NBR = 6
HALO = 512
BASIS = 4
COL_DEV = 2048
NSEG = 16
COLUMNS = 32768


def draw_neighbour_columns(key, part):
    key = jax.random.fold_in(key, 7)
    column = jnp.arange(COLUMNS, dtype=jnp.int32)
    offsets = jax.random.randint(key, (COLUMNS, NBR), -HALO, HALO + 1, dtype=jnp.int32)
    offsets = offsets.at[:, 0].set(0)
    inside = column % COL_DEV
    reach = jnp.where(inside == 0, -HALO, jnp.where(inside == COL_DEV - 1, HALO, offsets[:, 1]))
    offsets = offsets.at[:, 1].set(reach)
    offsets = offsets.at[:, 2].set(jnp.where(column == 0, -1, offsets[:, 2]))
    return ((column[:, None] + offsets) % COLUMNS).astype(jnp.int32)


def set_ends(values, stream_key, least, high):
    longest = values.shape.index(max(values.shape))
    spots = []
    for shift in (0, 1):
        where = [jax.random.randint(jax.random.fold_in(stream_key, axis), (), 0, length) for axis, length in enumerate(values.shape)]
        where[longest] = (where[longest] + shift) % values.shape[longest]
        spots.append(tuple(where))
    return values.at[spots[0]].set(least).at[spots[1]].set(high)


def levels(own_key, dims, pieces, low, largest):
    def one(position, blocks):
        draws = jax.random.uniform(jax.random.fold_in(jax.random.fold_in(own_key, 6), position), (blocks,), jnp.float32, low / len(pieces), largest / len(pieces))
        return jnp.repeat(jnp.exp(draws), dims[position] // blocks).reshape((-1,) + (1,) * (len(dims) - position - 1))

    level = one(*pieces[0])
    for cut in pieces[1:]:
        level = level * one(*cut)
    return level


def normal_values(stream_key, extent, scale, most, pieces=(), kind=jnp.bfloat16):
    values = scale * jax.random.normal(stream_key, extent, jnp.float32)
    if pieces:
        values = values * levels(stream_key, extent, pieces, -0.22, 0.18)
    return jnp.clip(values, -most, most).astype(kind)


def setup_inputs(seed: int = 0) -> dict:
    splits = jax.random.split(jax.random.key(seed), 8)
    segment_state = normal_values(splits[0], (NSEG, TRACERS, LEV, COLUMNS), 1.0, 6.0, ((0, 8), (3, 16)), jnp.float32)
    light = jnp.clip(jnp.exp(math.log(1.0) - 2.9957323 * jax.random.uniform(splits[1], (NSEG, LEV, COLUMNS), jnp.float32) ** levels(splits[1], (NSEG, LEV, COLUMNS), ((0, 8), (2, 16)), -0.2, 0.2)), 0.05, 1.0)
    mixing = jnp.clip(0.04 + 0.26000001 * jax.random.uniform(splits[2], (NSEG, NBR, LEV, COLUMNS), jnp.float32) ** levels(splits[2], (NSEG, NBR, LEV, COLUMNS), ((0, 8), (3, 16)), -0.2, 0.2), 0.04, 0.3)
    kappa = jnp.clip(jnp.exp(math.log(2.0) - 3.6888794 * jax.random.uniform(splits[3], (NSEG, LEV, COLUMNS), jnp.float32) ** levels(splits[3], (NSEG, LEV, COLUMNS), ((0, 8), (2, 16)), -0.2, 0.2)), 0.05, 2.0)
    neighbour_columns = draw_neighbour_columns(jax.random.fold_in(splits[7], 71), 0)
    wet_levels = set_ends(jax.random.randint(splits[5], (COLUMNS,), 1, LEV + 1), jax.random.fold_in(splits[5], 1), 1, LEV).astype(jnp.int32)
    basis = normal_values(splits[6], (BASIS, NSEG, TRACERS, LEV, COLUMNS), (NSEG * TRACERS * LEV * COLUMNS) ** -0.5, 0.0009765625, ((1, 8), (4, 16)), jnp.float32)
    return dict(segment_state=segment_state, light=light, mixing=mixing, kappa=kappa, neighbour_columns=neighbour_columns, wet_levels=wet_levels, basis=basis)


uptake_rate = 0.6
half_saturation = 0.3
remin_rate = 0.2
dissolved_share = 0.7
epsilon = 1e-06

def sources(field, light):
    phosphate = field[:, 0]
    organic = field[:, 1]
    squared = phosphate * phosphate
    uptake = uptake_rate * light * squared / (squared + half_saturation)
    return jnp.stack([remin_rate * organic - uptake, dissolved_share * uptake - remin_rate * organic], axis=1)

def couplings(kappa, wet_flags):
    depth_index = lax.broadcasted_iota(jnp.int32, wet_flags.shape, 0)
    upper = jnp.where((depth_index >= 1) & wet_flags, kappa, jnp.float32(0.0))
    lower = jnp.concatenate([upper[:, 1:], jnp.zeros_like(upper[:, :1])], axis=1)
    return (upper[:, None], lower[:, None])

def vertical_solve(source, upper, lower):
    number = source.shape[-2]
    diagonal = 1.0 + upper + lower
    ratio = -lower[..., 0, :] / diagonal[..., 0, :]
    value = source[..., 0, :] / diagonal[..., 0, :]
    ratios = [ratio]
    values = [value]
    for layer in range(1, number):
        pivot = diagonal[..., layer, :] + upper[..., layer, :] * ratio
        ratio = -lower[..., layer, :] / pivot
        value = (source[..., layer, :] + upper[..., layer, :] * value) / pivot
        ratios.append(ratio)
        values.append(value)
    result = values[-1]
    solved = [result]
    for layer in range(number - 2, -1, -1):
        result = values[layer] - ratios[layer] * result
        solved.append(result)
    return jnp.stack(solved[::-1], axis=-2)

def transport(extended, table, mixing):
    total = mixing[:, 0][:, None] * jnp.take(extended, table[:, 0], axis=3)
    for neighbour in range(1, table.shape[1]):
        total = total + mixing[:, neighbour][:, None] * jnp.take(extended, table[:, neighbour], axis=3)
    return total

def advance(field, extended, table, mixing, light, upper, lower, wet_float):
    sourced = transport(extended, table, mixing) + sources(field, light)
    return vertical_solve(sourced, upper, lower) * wet_float

def combine(weights, basis):
    return jnp.einsum('m,msjlc->sjlc', weights, basis, precision=lax.Precision.HIGHEST)

def projections(basis, vector):
    return lax.optimization_barrier(jnp.sum(basis * vector[None], axis=(1, 2, 3, 4)))

def reference(segment_state, light, mixing, kappa, neighbour_columns, wet_levels, basis):
    depth_index = lax.broadcasted_iota(jnp.int32, (LEV, COLUMNS), 0)
    wet_flags = depth_index < wet_levels[None, :]
    wet_float = wet_flags.astype(jnp.float32)
    upper, lower = couplings(kappa, wet_flags)
    field = segment_state
    for turn in range(2):
        field = advance(field, field, neighbour_columns, mixing, light, upper, lower, wet_float)
    previous = jnp.roll(field, 1, axis=0)
    residual = wet_float * (segment_state - previous)
    first = projections(basis, residual)
    middle = residual - combine(first, basis)
    second = projections(basis, middle)
    ortho = middle - combine(second, basis)
    count = NSEG * TRACERS * LEV * COLUMNS
    spread = jnp.sqrt(jnp.sum(ortho * ortho) / count + epsilon)
    new_vector = ortho / spread
    coefficients = jnp.concatenate([first + second, spread[None]])
    return (residual, new_vector, coefficients)
```

```python
import functools

import jax
import jax.numpy as jnp
from jax import lax
from jax.experimental import pallas as pl
from jax.experimental.pallas import tpu as pltpu
from jax.sharding import PartitionSpec as P

uptake_rate = 0.6
half_saturation = 0.3
remin_rate = 0.2
dissolved_share = 0.7
epsilon = 1e-06

SEGS = 2
TRACERS = 2
LEV = 32
NBR = 6
BASIS = 4
WIDTH = 2048
HALO = 512
LANE = 128
TILE = 256
BLOCKS = WIDTH // TILE
GROUPS = WIDTH // HALO
CHUNKS = HALO // LANE
ROWS = SEGS * TRACERS * LEV
GROUP_ROWS = TRACERS * CHUNKS * SEGS * LEV
VMEM = pl.BlockSpec(memory_space=pltpu.VMEM)
PARAMS = pltpu.CompilerParams(vmem_limit_bytes=56 * 1024 * 1024)
f32 = jnp.float32
bf16 = jnp.bfloat16


def shape(*dims):
    return jax.ShapeDtypeStruct(dims, f32)


def group_row(tracer, chunk, seg):
    return ((tracer * CHUNKS + chunk) * SEGS + seg) * LEV


def natural_reader(ref):
    def read(seg, tracer, start):
        return ref[seg, tracer, :, pl.ds(start, TILE)]

    return read


def group_reader(refs):
    def read(seg, tracer, start):
        ref, place = refs[start // HALO]
        chunk = start % HALO // LANE
        parts = [ref[place, pl.ds(group_row(tracer, chunk + h, seg), LEV), :] for h in range(TILE // LANE)]
        return jnp.concatenate(parts, axis=1)

    return read


def split_tile(read, start, xs_ref, place):
    for seg in range(SEGS):
        for tracer in range(TRACERS):
            value = read(seg, tracer, start)
            high = value.astype(bf16)
            low = (value - high.astype(f32)).astype(bf16)
            row = (seg * TRACERS + tracer) * LEV
            xs_ref[place, pl.ds(row, LEV), :] = high
            xs_ref[place, pl.ds(ROWS + row, LEV), :] = low


def picked(xs_ref, places, offsets, index):
    total = None
    depth = lax.broadcasted_iota(jnp.int32, (TILE, TILE), 0)
    for place, offset in zip(places, offsets):
        chosen = jnp.where(depth == index - offset, f32(1), f32(0)).astype(bf16)
        part = jnp.dot(xs_ref[place], chosen, preferred_element_type=f32)
        total = part if total is None else total + part
    return total[:ROWS] + total[ROWS:]


def moved_part(xs_ref, places, offsets, index_of, mixing_of):
    total = [None] * (SEGS * TRACERS)
    for k in range(1, NBR):
        value = picked(xs_ref, places, offsets, index_of(k))
        for seg in range(SEGS):
            mix = mixing_of(seg, k)
            for tracer in range(TRACERS):
                at = seg * TRACERS + tracer
                term = mix * value[at * LEV : (at + 1) * LEV]
                total[at] = term if total[at] is None else total[at] + term
    return total


def factorize(kappa_ref, wet_ref, by_rows_ref, inverse_ref, carry_ref, ratio_ref):
    for group in range(GROUPS):
        for chunk in range(CHUNKS):
            for seg in range(SEGS):
                lanes = pl.ds(group * HALO + chunk * LANE, LANE)
                row = (group * CHUNKS * SEGS + chunk * SEGS + seg) * LEV
                by_rows_ref[pl.ds(row, LEV), :] = kappa_ref[seg, :, lanes]
    wet = []
    for group in range(GROUPS):
        rows = []
        for chunk in range(CHUNKS):
            one = wet_ref[pl.ds(group * CHUNKS + chunk, 1), :]
            rows += [one] * SEGS
        wet.append(jnp.concatenate(rows, axis=0))
    zero = jnp.zeros((CHUNKS * SEGS, LANE), f32)

    def upper_at(group, level):
        if level == 0 or level == LEV:
            return zero
        rows = pl.ds(group * CHUNKS * SEGS * LEV + level, CHUNKS * SEGS, stride=LEV)
        return jnp.where(wet[group] > level, by_rows_ref[rows, :], 0.0)

    upper = [upper_at(group, 0) for group in range(GROUPS)]
    ratio = [zero] * GROUPS
    for level in range(LEV):
        for group in range(GROUPS):
            lower = upper_at(group, level + 1)
            pivot = (1.0 + upper[group] + lower) + upper[group] * ratio[group]
            inverse = 1.0 / pivot
            ratio[group] = -lower * inverse
            inverse_ref[group, level] = jnp.where(wet[group] > level, inverse, 0.0)
            carry_ref[group, level] = upper[group] * inverse
            ratio_ref[group, level] = ratio[group]
            upper[group] = lower


def solve(source_ref, place, inverse_ref, carry_ref, ratio_ref, group, out):
    step = CHUNKS * SEGS

    def source(tracer, level):
        return source_ref[place, pl.ds(group_row(tracer, 0, 0) + level, step, stride=LEV), :]

    value = [[None] * LEV for _ in range(TRACERS)]
    for level in range(LEV):
        inverse = inverse_ref[group, level]
        carry = carry_ref[group, level]
        for tracer in range(TRACERS):
            here = source(tracer, level) * inverse
            if level:
                here = here + carry * value[tracer][level - 1]
            value[tracer][level] = here
    for level in range(LEV - 1, -1, -1):
        ratio = ratio_ref[group, level]
        for tracer in range(TRACERS):
            if level < LEV - 1:
                value[tracer][level] = value[tracer][level] - ratio * value[tracer][level + 1]
            out(tracer, level, value[tracer][level])


def into_group(ref, place):
    def write(tracer, level, value):
        ref[place, pl.ds(group_row(tracer, 0, 0) + level, CHUNKS * SEGS, stride=LEV), :] = value

    return write


def own_part(read, read_moving, table_ref, mixing_ref, light_ref, xs_ref, acc_ref):
    for tile in range(BLOCKS):
        split_tile(read, tile * TILE, xs_ref, tile)

    def finish(block, start, total):
        for seg in range(SEGS):
            columns = pl.ds(start, TILE)
            phosphate = read_moving(seg, 0, block, start)
            organic = read_moving(seg, 1, block, start)
            squared = phosphate * phosphate
            uptake = uptake_rate * light_ref[seg, :, columns] * squared / (squared + half_saturation)
            gains = (remin_rate * organic - uptake, dissolved_share * uptake - remin_rate * organic)
            own = mixing_ref[seg, 0, :, columns]
            for tracer, value in enumerate((phosphate, organic)):
                result = own * value + total[seg * TRACERS + tracer] + gains[tracer]
                for h in range(TILE // LANE):
                    row = group_row(tracer, block % 2 * 2 + h, seg)
                    acc_ref[block // 2, pl.ds(row, LEV), :] = result[:, h * LANE : (h + 1) * LANE]

    for block in range(BLOCKS):
        start = block * TILE
        tiles = list(range(max(0, block - 2), min(BLOCKS, block + 3)))
        total = moved_part(
            xs_ref,
            tiles,
            [tile * TILE for tile in tiles],
            lambda k: table_ref[pl.ds(k, 1), pl.ds(start, TILE)],
            lambda seg, k: mixing_ref[seg, k, :, pl.ds(start, TILE)],
        )
        finish(block, start, total)


def first_own_kernel(
    state_ref, table_ref, mixing_ref, light_ref, kappa_ref, wet_ref,
    edge_ref, middle_ref, inverse_ref, carry_ref, ratio_ref,
    xs_ref, acc_ref, by_rows_ref,
):
    read = natural_reader(state_ref)
    factorize(kappa_ref, wet_ref, by_rows_ref, inverse_ref, carry_ref, ratio_ref)
    own_part(read, lambda seg, tracer, block, start: read(seg, tracer, start), table_ref, mixing_ref, light_ref, xs_ref, acc_ref)
    finish_own(edge_ref, middle_ref, inverse_ref, carry_ref, ratio_ref, acc_ref)


def finish_own(edge_ref, middle_ref, inverse_ref, carry_ref, ratio_ref, acc_ref):
    for place, group in enumerate((0, GROUPS - 1)):
        edge_ref[place] = acc_ref[group]
    for group in range(1, GROUPS - 1):
        solve(acc_ref, group, inverse_ref, carry_ref, ratio_ref, group, into_group(middle_ref, group - 1))


def second_own_kernel(
    head_ref, middle_in_ref, tail_ref, table_ref, mixing_ref, light_ref, inverse_ref, carry_ref, ratio_ref,
    edge_ref, middle_ref,
    xs_ref, acc_ref,
):
    refs = [(head_ref, 0)] + [(middle_in_ref, i) for i in range(GROUPS - 2)] + [(tail_ref, 0)]
    read = group_reader(refs)
    own_part(read, lambda seg, tracer, block, start: read(seg, tracer, start), table_ref, mixing_ref, light_ref, xs_ref, acc_ref)
    finish_own(edge_ref, middle_ref, inverse_ref, carry_ref, ratio_ref, acc_ref)


def edge_kernel(
    natural, left_ref, right_ref, table_ref, mixing_ref, edge_in_ref, inverse_ref, carry_ref, ratio_ref,
    head_ref, tail_ref,
    xs_ref, acc_ref,
):
    for side, ref in enumerate((left_ref, right_ref)):
        read = natural_reader(ref) if natural else group_reader([(ref, 0)])
        for tile in range(HALO // TILE):
            split_tile(read, tile * TILE, xs_ref, side * 2 + tile)
    acc_ref[...] = edge_in_ref[...]
    uses = ((0, 0, (0, 1)), (1, 0, (1,)), (BLOCKS - 2, 1, (2,)), (BLOCKS - 1, 1, (2, 3)))
    offsets = (-HALO, -TILE, WIDTH, WIDTH + TILE)
    for block, side, places in uses:
        start = block * TILE
        total = moved_part(
            xs_ref,
            places,
            [offsets[place] for place in places],
            lambda k: table_ref[pl.ds(k, 1), pl.ds(start, TILE)],
            lambda seg, k: mixing_ref[seg, k, :, pl.ds(start, TILE)],
        )
        for seg in range(SEGS):
            for tracer in range(TRACERS):
                value = total[seg * TRACERS + tracer]
                for h in range(TILE // LANE):
                    row = pl.ds(group_row(tracer, block % 2 * 2 + h, seg), LEV)
                    acc_ref[side, row, :] += value[:, h * LANE : (h + 1) * LANE]
    for side, (group, ref) in enumerate(((0, head_ref), (GROUPS - 1, tail_ref))):
        solve(acc_ref, side, inverse_ref, carry_ref, ratio_ref, group, into_group(ref, 0))


def first_own(state, table, mixing, light, kappa, wet):
    factors = shape(GROUPS, LEV, CHUNKS * SEGS, LANE)
    return pl.pallas_call(
        first_own_kernel,
        out_shape=(shape(2, GROUP_ROWS, LANE), shape(GROUPS - 2, GROUP_ROWS, LANE), factors, factors, factors),
        in_specs=[VMEM] * 6,
        out_specs=(VMEM,) * 5,
        scratch_shapes=[
            pltpu.VMEM((BLOCKS, 2 * ROWS, TILE), bf16),
            pltpu.VMEM((GROUPS, GROUP_ROWS, LANE), f32),
            pltpu.VMEM((GROUPS * CHUNKS * SEGS * LEV, LANE), f32),
        ],
        compiler_params=PARAMS,
        cost_estimate=pl.CostEstimate(flops=6_000_000_000, bytes_accessed=10_000_000, transcendentals=0),
        name="first_step_own",
    )(state, table, mixing, light, kappa, wet)


def second_own(head, middle, tail, table, mixing, light, factors):
    return pl.pallas_call(
        second_own_kernel,
        out_shape=(shape(2, GROUP_ROWS, LANE), shape(GROUPS - 2, GROUP_ROWS, LANE)),
        in_specs=[VMEM] * 9,
        out_specs=(VMEM,) * 2,
        scratch_shapes=[
            pltpu.VMEM((BLOCKS, 2 * ROWS, TILE), bf16),
            pltpu.VMEM((GROUPS, GROUP_ROWS, LANE), f32),
        ],
        compiler_params=PARAMS,
        cost_estimate=pl.CostEstimate(flops=6_000_000_000, bytes_accessed=10_000_000, transcendentals=0),
        name="second_step_own",
    )(head, middle, tail, table, mixing, light, *factors)


def edges(natural, left, right, table, mixing, edge, factors):
    return pl.pallas_call(
        functools.partial(edge_kernel, natural),
        out_shape=(shape(1, GROUP_ROWS, LANE), shape(1, GROUP_ROWS, LANE)),
        in_specs=[VMEM] * 8,
        out_specs=(VMEM,) * 2,
        scratch_shapes=[
            pltpu.VMEM((4, 2 * ROWS, TILE), bf16),
            pltpu.VMEM((2, GROUP_ROWS, LANE), f32),
        ],
        compiler_params=PARAMS,
        cost_estimate=pl.CostEstimate(flops=1_000_000_000, bytes_accessed=8_000_000, transcendentals=0),
        name="first_step_edges" if natural else "second_step_edges",
    )(left, right, table, mixing, edge, *factors)


def residual_kernel(state_ref, wet_ref, basis_ref, head_ref, middle_ref, tail_ref, came_ref, residual_ref, sums_ref):
    pairs = [(i, j) for i in range(BASIS) for j in range(i, BASIS)]
    sums = [jnp.zeros((8, LANE), f32) for _ in range(BASIS + 1 + len(pairs))]
    refs = [(head_ref, 0)] + [(middle_ref, i) for i in range(GROUPS - 2)] + [(tail_ref, 0)]
    level = lax.broadcasted_iota(jnp.int32, (8, LANE), 0)
    for group in range(GROUPS):
        ref, place = refs[group]
        for chunk in range(CHUNKS):
            lanes = pl.ds(group * HALO + chunk * LANE, LANE)
            wet = jnp.broadcast_to(wet_ref[pl.ds(group * CHUNKS + chunk, 1), :], (8, LANE))
            for seg in range(SEGS):
                for tracer in range(TRACERS):
                    for part in range(LEV // 8):
                        rows = pl.ds(part * 8, 8)
                        if seg:
                            before = ref[place, pl.ds(group_row(tracer, chunk, seg - 1) + part * 8, 8), :]
                        else:
                            before = came_ref[group, pl.ds((tracer * CHUNKS + chunk) * LEV + part * 8, 8), :]
                        own = state_ref[seg, tracer, rows, lanes]
                        here = jnp.where(wet > level + part * 8, own - before, 0.0)
                        residual_ref[seg, tracer, rows, lanes] = here
                        vectors = [basis_ref[i, seg, tracer, rows, lanes] for i in range(BASIS)]
                        for i in range(BASIS):
                            sums[i] = sums[i] + vectors[i] * here
                        sums[BASIS] = sums[BASIS] + here * here
                        for at, (i, j) in enumerate(pairs):
                            sums[BASIS + 1 + at] = sums[BASIS + 1 + at] + vectors[i] * vectors[j]
    rows = [jnp.sum(one, axis=0, keepdims=True) for one in sums]
    rows.append(jnp.zeros((16 - len(rows), LANE), f32))
    sums_ref[...] = jnp.concatenate(rows, axis=0)


def residuals(state, wet, basis, head, middle, tail, came):
    return pl.pallas_call(
        residual_kernel,
        out_shape=(shape(SEGS, TRACERS, LEV, WIDTH), shape(16, LANE)),
        in_specs=[VMEM] * 7,
        out_specs=(VMEM,) * 2,
        compiler_params=PARAMS,
        name="residual_and_products",
    )(state, wet, basis, head, middle, tail, came)


def scaled_kernel(count, residual_ref, basis_ref, sums_ref, new_ref, coefficients_ref):
    sums = jnp.sum(sums_ref[...], axis=1, keepdims=True)
    one = [sums[i : i + 1] for i in range(16)]
    first, square, products = one[:BASIS], one[BASIS], iter(one[BASIS + 1 :])
    gram = [[None] * BASIS for _ in range(BASIS)]
    for i in range(BASIS):
        for j in range(i, BASIS):
            gram[i][j] = gram[j][i] = next(products)
    second = [first[i] - sum(gram[i][j] * first[j] for j in range(BASIS)) for i in range(BASIS)]
    both = [first[i] + second[i] for i in range(BASIS)]
    for i in range(BASIS):
        square = square - both[i] * (2.0 * first[i] - sum(gram[i][j] * both[j] for j in range(BASIS)))
    spread = jnp.sqrt(square / count + epsilon)
    lane = lax.broadcasted_iota(jnp.int32, (8, LANE), 1)
    result = jnp.zeros((8, LANE), f32)
    for i, value in enumerate(both + [spread]):
        result = jnp.where(lane == i, value, result)
    coefficients_ref[...] = result
    scale = 1.0 / spread
    weights = [jnp.broadcast_to(-value * scale, (LEV, LANE)) for value in both]
    scale = jnp.broadcast_to(scale, (LEV, LANE))
    for seg in range(SEGS):
        for tracer in range(TRACERS):
            for chunk in range(CHUNKS):
                lanes = pl.ds(chunk * LANE, LANE)
                total = residual_ref[seg, tracer, :, lanes] * scale
                for i in range(BASIS):
                    total = total + weights[i] * basis_ref[i, seg, tracer, :, lanes]
                new_ref[seg, tracer, :, lanes] = total


def scaled(count, residual, basis, sums):
    block = pl.BlockSpec((SEGS, TRACERS, LEV, HALO), lambda g: (0, 0, 0, g))
    return pl.pallas_call(
        functools.partial(scaled_kernel, count),
        grid=(GROUPS,),
        out_shape=(shape(SEGS, TRACERS, LEV, WIDTH), shape(8, LANE)),
        in_specs=[
            block,
            pl.BlockSpec((BASIS, SEGS, TRACERS, LEV, HALO), lambda g: (0, 0, 0, 0, g)),
            pl.BlockSpec((16, LANE), lambda g: (0, 0)),
        ],
        out_specs=(block, pl.BlockSpec((8, LANE), lambda g: (0, 0))),
        compiler_params=PARAMS,
        name="orthogonal_and_scaled",
    )(residual, basis, sums)


def shifted(block, axis, distance):
    count = lax.axis_size(axis)
    return lax.ppermute(block, axis, [(i, (i + distance) % count) for i in range(count)])


def summed_everywhere(value):
    for axis in ("seg", "col"):
        count = lax.axis_size(axis)
        done = 1
        while done < count:
            flip = done if done in (1, 2, 4, 8) else done
            value = value + lax.ppermute(value, axis, [(i, i ^ FLIPS[axis][flip]) for i in range(count)])
            done *= 2
    return value


FLIPS = {"seg": {1: 1, 2: 2, 4: 6}, "col": {1: 1, 2: 3, 4: 4, 8: 12}}


def sent_segment(groups):
    count = groups.shape[0]
    parts = groups.reshape(count, TRACERS * CHUNKS, SEGS, LEV, LANE)[:, :, SEGS - 1]
    return parts.reshape(count, TRACERS * CHUNKS * LEV, LANE)


def per_device(segment_state, light, mixing, kappa, neighbour_columns, wet_levels, basis):
    start = lax.axis_index("col") * WIDTH
    every_column = lax.axis_size("col") * WIDTH
    left = shifted(segment_state[..., WIDTH - HALO :], "col", 1)
    right = shifted(segment_state[..., :HALO], "col", -1)
    table = (neighbour_columns.T - start + HALO + every_column) % every_column - HALO
    table = jnp.concatenate([table, jnp.zeros((8 - NBR, WIDTH), jnp.int32)], axis=0)
    wet = wet_levels.reshape(WIDTH // LANE, LANE)
    edge, middle, *factors = first_own(segment_state, table, mixing, light, kappa, wet)
    head, tail = edges(True, left, right, table, mixing, edge, factors)
    left = shifted(tail, "col", 1)
    right = shifted(head, "col", -1)
    edge, middle = second_own(head, middle, tail, table, mixing, light, factors)
    head, tail = edges(False, left, right, table, mixing, edge, factors)
    came = shifted(jnp.concatenate([sent_segment(head), sent_segment(middle), sent_segment(tail)]), "seg", 1)
    residual, sums = residuals(segment_state, wet, basis, head, middle, tail, came)
    count = lax.axis_size("seg") * SEGS * TRACERS * LEV * every_column
    new_vector, coefficients = scaled(count, residual, basis, summed_everywhere(sums))
    return (residual, new_vector, coefficients[0, : BASIS + 1])


def solution(mesh):
    return jax.shard_map(
        per_device,
        mesh=mesh,
        in_specs=(
            P("seg", None, None, "col"),
            P("seg", None, "col"),
            P("seg", None, None, "col"),
            P("seg", None, "col"),
            P("col", None),
            P("col"),
            P(None, "seg", None, None, "col"),
        ),
        out_specs=(P("seg", None, None, "col"), P("seg", None, None, "col"), P()),
        check_vma=False,
    )
```

```python
import functools

import jax
import jax.numpy as jnp
from jax import lax
from jax.experimental import pallas as pl
from jax.experimental.pallas import tpu as pltpu
from jax.sharding import PartitionSpec as P

uptake_rate = 0.6
half_saturation = 0.3
remin_rate = 0.2
dissolved_share = 0.7
epsilon = 1e-06

SEGS = 2
TRACERS = 2
LEV = 32
NBR = 6
BASIS = 4
WIDTH = 2048
HALO = 512
LANE = 128
TILE = 256
BLOCKS = WIDTH // TILE
GROUPS = WIDTH // HALO
CHUNKS = HALO // LANE
ROWS = SEGS * TRACERS * LEV
GROUP_ROWS = TRACERS * CHUNKS * SEGS * LEV
VMEM = pl.BlockSpec(memory_space=pltpu.VMEM)
PARAMS = pltpu.CompilerParams(vmem_limit_bytes=16 * 1024 * 1024)
ANY = pl.BlockSpec(memory_space=pl.ANY)
HBM = pl.BlockSpec(memory_space=pltpu.HBM)
f32 = jnp.float32
bf16 = jnp.bfloat16


def shape(*dims):
    return jax.ShapeDtypeStruct(dims, f32)


def group_row(tracer, chunk, seg):
    return ((tracer * CHUNKS + chunk) * SEGS + seg) * LEV


def natural_reader(ref):
    def read(seg, tracer, start):
        return ref[seg, tracer, :, pl.ds(start, TILE)]

    return read


def group_reader(refs):
    def read(seg, tracer, start):
        ref, place = refs[start // HALO]
        chunk = start % HALO // LANE
        parts = [ref[place, pl.ds(group_row(tracer, chunk + h, seg), LEV), :] for h in range(TILE // LANE)]
        return jnp.concatenate(parts, axis=1)

    return read


def split_tile(read, start, xs_ref, place):
    for seg in range(SEGS):
        for tracer in range(TRACERS):
            value = read(seg, tracer, start)
            high = value.astype(bf16)
            low = (value - high.astype(f32)).astype(bf16)
            row = (seg * TRACERS + tracer) * LEV
            xs_ref[place, pl.ds(row, LEV), :] = high
            xs_ref[place, pl.ds(ROWS + row, LEV), :] = low


def table_row(every_column, table_ref, k, start):
    columns = pl.ds(start, TILE)
    away = table_ref[pl.ds(k, 1), columns] - table_ref[pl.ds(0, 1), columns]
    away = jnp.where(away > HALO, away - every_column, away)
    away = jnp.where(away < -HALO, away + every_column, away)
    return away + lax.broadcasted_iota(jnp.int32, (1, TILE), 1) + start


def picked(xs_ref, places, offsets, index):
    total = None
    depth = lax.broadcasted_iota(jnp.int32, (TILE, TILE), 0)
    for place, offset in zip(places, offsets):
        chosen = jnp.where(depth == index - offset, f32(1), f32(0)).astype(bf16)
        part = jnp.dot(xs_ref[place], chosen, preferred_element_type=f32)
        total = part if total is None else total + part
    return total[:ROWS] + total[ROWS:]


def moved_part(xs_ref, places, offsets, index_of, mixing_of):
    total = [None] * (SEGS * TRACERS)
    for k in range(1, NBR):
        value = picked(xs_ref, places, offsets, index_of(k))
        for seg in range(SEGS):
            mix = mixing_of(seg, k)
            for tracer in range(TRACERS):
                at = seg * TRACERS + tracer
                term = mix * value[at * LEV : (at + 1) * LEV]
                total[at] = term if total[at] is None else total[at] + term
    return total


def factorize(kappa_ref, wet_ref, by_rows_ref, inverse_ref, carry_ref, ratio_ref):
    for group in range(GROUPS):
        for chunk in range(CHUNKS):
            for seg in range(SEGS):
                lanes = pl.ds(group * HALO + chunk * LANE, LANE)
                row = (group * CHUNKS * SEGS + chunk * SEGS + seg) * LEV
                by_rows_ref[pl.ds(row, LEV), :] = kappa_ref[seg, :, lanes]
    wet = []
    for group in range(GROUPS):
        rows = []
        for chunk in range(CHUNKS):
            one = wet_ref[pl.ds(group * CHUNKS + chunk, 1), :]
            rows += [one] * SEGS
        wet.append(jnp.concatenate(rows, axis=0))
    zero = jnp.zeros((CHUNKS * SEGS, LANE), f32)

    def upper_at(group, level):
        if level == 0 or level == LEV:
            return zero
        rows = pl.ds(group * CHUNKS * SEGS * LEV + level, CHUNKS * SEGS, stride=LEV)
        return jnp.where(wet[group] > level, by_rows_ref[rows, :], 0.0)

    upper = [upper_at(group, 0) for group in range(GROUPS)]
    ratio = [zero] * GROUPS
    for level in range(LEV):
        for group in range(GROUPS):
            lower = upper_at(group, level + 1)
            pivot = (1.0 + upper[group] + lower) + upper[group] * ratio[group]
            inverse = 1.0 / pivot
            ratio[group] = -lower * inverse
            inverse_ref[group, level] = jnp.where(wet[group] > level, inverse, 0.0)
            carry_ref[group, level] = upper[group] * inverse
            ratio_ref[group, level] = ratio[group]
            upper[group] = lower


def solve(source_ref, place, inverse_ref, carry_ref, ratio_ref, group, out):
    step = CHUNKS * SEGS

    def source(tracer, level):
        return source_ref[place, pl.ds(group_row(tracer, 0, 0) + level, step, stride=LEV), :]

    value = [[None] * LEV for _ in range(TRACERS)]
    for level in range(LEV):
        inverse = inverse_ref[group, level]
        carry = carry_ref[group, level]
        for tracer in range(TRACERS):
            here = source(tracer, level) * inverse
            if level:
                here = here + carry * value[tracer][level - 1]
            value[tracer][level] = here
    for level in range(LEV - 1, -1, -1):
        ratio = ratio_ref[group, level]
        for tracer in range(TRACERS):
            if level < LEV - 1:
                value[tracer][level] = value[tracer][level] - ratio * value[tracer][level + 1]
            out(tracer, level, value[tracer][level])


def into_group(ref, place):
    def write(tracer, level, value):
        ref[place, pl.ds(group_row(tracer, 0, 0) + level, CHUNKS * SEGS, stride=LEV), :] = value

    return write


def own_blocks(every_column, blocks, read, table_ref, mixing_ref, light_ref, xs_ref, acc_ref, places, ready=None):
    for block in blocks:
        if ready is not None:
            ready(block)
        start = block * TILE
        tiles = list(range(max(0, block - 2), min(BLOCKS, block + 3)))
        total = moved_part(
            xs_ref,
            tiles,
            [tile * TILE for tile in tiles],
            lambda k: table_row(every_column, table_ref, k, start),
            lambda seg, k: mixing_ref[seg, k, :, pl.ds(start, TILE)],
        )
        for seg in range(SEGS):
            columns = pl.ds(start, TILE)
            phosphate = read(seg, 0, start)
            organic = read(seg, 1, start)
            squared = phosphate * phosphate
            uptake = uptake_rate * light_ref[seg, :, columns] * squared / (squared + half_saturation)
            gains = (remin_rate * organic - uptake, dissolved_share * uptake - remin_rate * organic)
            own = mixing_ref[seg, 0, :, columns]
            for tracer, value in enumerate((phosphate, organic)):
                result = own * value + total[seg * TRACERS + tracer] + gains[tracer]
                for h in range(TILE // LANE):
                    row = group_row(tracer, block % 2 * 2 + h, seg)
                    acc_ref[places[block // 2], pl.ds(row, LEV), :] = result[:, h * LANE : (h + 1) * LANE]


EDGE_BLOCKS = (0, 1, BLOCKS - 2, BLOCKS - 1)
MIDDLE_BLOCKS = tuple(range(2, BLOCKS - 2))
EDGE_PLACES = {0: 0, GROUPS - 1: 1}
MIDDLE_PLACES = {group: group - 1 for group in range(1, GROUPS - 1)}


def sent_rows(from_ref, place, to_ref, to_place):
    for tracer in range(TRACERS):
        for chunk in range(CHUNKS):
            to_ref[to_place, pl.ds((tracer * CHUNKS + chunk) * LEV, LEV), :] = from_ref[
                place, pl.ds(group_row(tracer, chunk, SEGS - 1), LEV), :
            ]


def halves_kernel(state_ref, head_ref, tail_ref):
    head_ref[...] = state_ref[:, :, :, :HALO]
    tail_ref[...] = state_ref[:, :, :, WIDTH - HALO :]


def halves(state):
    half = shape(SEGS, TRACERS, LEV, HALO)
    return call(halves_kernel, "edge_columns", 0, (half, half), [], state)


def first_own_kernel(
    every_column, state_ref, table_in, mixing_in, light_in, kappa_in, wet_in,
    edge_ref, middle_ref, inverse_ref, carry_ref, ratio_ref, table_ref, mixing_ref, light_ref, wet_ref,
    xs_ref, acc_ref, by_rows_ref, kappa_ref, sems,
):
    order = (0, GROUPS - 1) + tuple(range(1, GROUPS - 1))
    parts = [(slice(None),) * 3 + (pl.ds(group * HALO, HALO),) for group in order]
    of_mixing = [(mixing_in.at[part], mixing_ref.at[part]) for part in parts]
    pairs = [(table_in, table_ref), (light_in, light_ref), (kappa_in, kappa_ref), (wet_in, wet_ref)]
    pairs = pairs[:2] + of_mixing[:1] + pairs[2:] + of_mixing[1:]
    copies = [pltpu.make_async_copy(*pair, sems.at[i]) for i, pair in enumerate(pairs)]
    for copy in copies:
        copy.start()
    read = natural_reader(state_ref)
    for tile in range(BLOCKS):
        split_tile(read, tile * TILE, xs_ref, tile)

    def ready(block):
        if block == 0:
            for copy in copies[:3]:
                copy.wait()
        elif block == BLOCKS - 2:
            copies[3].wait()
            copies[4].wait()
            factorize(kappa_ref, wet_ref, by_rows_ref, inverse_ref, carry_ref, ratio_ref)
            for copy in copies[5:]:
                copy.wait()

    own_blocks(every_column, EDGE_BLOCKS, read, table_ref, mixing_ref, light_ref, xs_ref, edge_ref, EDGE_PLACES, ready)
    own_blocks(every_column, MIDDLE_BLOCKS, read, table_ref, mixing_ref, light_ref, xs_ref, acc_ref, MIDDLE_PLACES, ready)
    for group, place in MIDDLE_PLACES.items():
        solve(acc_ref, place, inverse_ref, carry_ref, ratio_ref, group, into_group(middle_ref, place))


def second_reader(head_ref, middle_ref, tail_ref):
    return group_reader([(head_ref, 0)] + [(middle_ref, i) for i in range(GROUPS - 2)] + [(tail_ref, 0)])


def second_middle_kernel(
    every_column, head_ref, middle_in_ref, tail_ref, table_ref, mixing_ref, light_ref, inverse_ref, carry_ref, ratio_ref,
    middle_ref, sent_ref, xs_ref,
    acc_ref,
):
    read = second_reader(head_ref, middle_in_ref, tail_ref)
    for tile in range(BLOCKS):
        split_tile(read, tile * TILE, xs_ref, tile)
    own_blocks(every_column, MIDDLE_BLOCKS, read, table_ref, mixing_ref, light_ref, xs_ref, acc_ref, MIDDLE_PLACES)
    for group, place in MIDDLE_PLACES.items():
        solve(acc_ref, place, inverse_ref, carry_ref, ratio_ref, group, into_group(middle_ref, place))
        sent_rows(middle_ref, place, sent_ref, place)


def second_edge_kernel(every_column, head_ref, middle_ref, tail_ref, table_ref, mixing_ref, light_ref, xs_ref, edge_ref):
    read = second_reader(head_ref, middle_ref, tail_ref)
    own_blocks(every_column, EDGE_BLOCKS, read, table_ref, mixing_ref, light_ref, xs_ref, edge_ref, EDGE_PLACES)


def edge_kernel(
    first, every_column, left_ref, right_ref, table_ref, mixing_ref, edge_in_ref, inverse_ref, carry_ref, ratio_ref,
    *outs_and_scratch,
):
    head_ref, tail_ref, *sent, xs_ref, acc_ref = outs_and_scratch
    for side, ref in enumerate((left_ref, right_ref)):
        read = natural_reader(ref) if first else group_reader([(ref, 0)])
        for tile in range(HALO // TILE):
            split_tile(read, tile * TILE, xs_ref, side * 2 + tile)
    uses = ((0, 0, (0, 1)), (1, 0, (1,)), (BLOCKS - 2, 1, (2,)), (BLOCKS - 1, 1, (2, 3)))
    offsets = (-HALO, -TILE, WIDTH, WIDTH + TILE)
    for block, side, places in uses:
        start = block * TILE
        total = moved_part(
            xs_ref,
            places,
            [offsets[place] for place in places],
            lambda k: table_row(every_column, table_ref, k, start),
            lambda seg, k: mixing_ref[seg, k, :, pl.ds(start, TILE)],
        )
        for seg in range(SEGS):
            for tracer in range(TRACERS):
                value = total[seg * TRACERS + tracer]
                for h in range(TILE // LANE):
                    row = pl.ds(group_row(tracer, block % 2 * 2 + h, seg), LEV)
                    acc_ref[side, row, :] = edge_in_ref[side, row, :] + value[:, h * LANE : (h + 1) * LANE]
    for side, (group, ref) in enumerate(((0, head_ref), (GROUPS - 1, tail_ref))):
        solve(acc_ref, side, inverse_ref, carry_ref, ratio_ref, group, into_group(ref, 0))
        if sent:
            sent_rows(ref, 0, sent[0], side)


EDGE = shape(2, GROUP_ROWS, LANE)
MIDDLE = shape(GROUPS - 2, GROUP_ROWS, LANE)
SENT = shape(2, GROUP_ROWS // SEGS, LANE)
ONE = shape(1, GROUP_ROWS, LANE)


def call(kernel, name, flops, outs, scratch, *operands):
    return pl.pallas_call(
        kernel,
        out_shape=outs,
        in_specs=[VMEM] * len(operands),
        out_specs=jax.tree.map(lambda _: VMEM, outs),
        scratch_shapes=scratch,
        compiler_params=PARAMS,
        cost_estimate=pl.CostEstimate(flops=flops, bytes_accessed=4_000_000, transcendentals=0),
        name=name,
    )(*operands)


def first_own(every_column, state, table, mixing, light, kappa, wet):
    factors = shape(GROUPS, LEV, CHUNKS * SEGS, LANE)
    like = [jax.ShapeDtypeStruct(one.shape, one.dtype) for one in (table, mixing, light, wet)]
    return pl.pallas_call(
        functools.partial(first_own_kernel, every_column),
        out_shape=(EDGE, MIDDLE, factors, factors, factors, *like),
        in_specs=[VMEM] + [HBM] * 5,
        out_specs=(VMEM,) * 9,
        scratch_shapes=[
            pltpu.VMEM((BLOCKS, 2 * ROWS, TILE), bf16),
            pltpu.VMEM((GROUPS - 2, GROUP_ROWS, LANE), f32),
            pltpu.VMEM((GROUPS * CHUNKS * SEGS * LEV, LANE), f32),
            pltpu.VMEM((SEGS, LEV, WIDTH), f32),
            pltpu.SemaphoreType.DMA((4 + GROUPS,)),
        ],
        compiler_params=PARAMS,
        cost_estimate=pl.CostEstimate(flops=6_000_000_000, bytes_accessed=4_000_000, transcendentals=0),
        name="first_step_own",
    )(state, *[pltpu.with_memory_space_constraint(one, pltpu.HBM) for one in (table, mixing, light, kappa, wet)])


def second_middle(every_column, head, middle, tail, table, mixing, light, factors):
    return call(
        functools.partial(second_middle_kernel, every_column), "second_step_middle", 3_500_000_000,
        (MIDDLE, SENT, jax.ShapeDtypeStruct((BLOCKS, 2 * ROWS, TILE), bf16)),
        [pltpu.VMEM((GROUPS - 2, GROUP_ROWS, LANE), f32)],
        head, middle, tail, table, mixing, light, *factors,
    )


def second_edge(every_column, head, middle, tail, table, mixing, light, xs):
    return call(
        functools.partial(second_edge_kernel, every_column), "second_step_edges_own", 2_500_000_000, EDGE, [],
        head, middle, tail, table, mixing, light, xs,
    )


def edges(first, every_column, left, right, table, mixing, edge, factors):
    return call(
        functools.partial(edge_kernel, first, every_column),
        "first_step_edges" if first else "second_step_edges", 1_000_000_000,
        (ONE, ONE) if first else (ONE, ONE, SENT),
        [pltpu.VMEM((4, 2 * ROWS, TILE), bf16), pltpu.VMEM((2, GROUP_ROWS, LANE), f32)],
        left, right, table, mixing, edge, *factors,
    )


PAIRS = [(i, j) for i in range(BASIS) for j in range(i, BASIS)]


def residual_of(groups, segs, state_ref, wet_ref, basis_ref, before_of, write, sums, products):
    level = lax.broadcasted_iota(jnp.int32, (8, LANE), 0)
    for group in groups:
        for chunk in range(CHUNKS):
            lanes = pl.ds(group * HALO + chunk * LANE, LANE)
            wet = jnp.broadcast_to(wet_ref[pl.ds(group * CHUNKS + chunk, 1), :], (8, LANE))
            for seg in segs:
                for tracer in range(TRACERS):
                    for part in range(LEV // 8):
                        rows = pl.ds(part * 8, 8)
                        before = before_of(group, chunk, seg, tracer, part * 8)
                        own = state_ref[seg, tracer, rows, lanes]
                        here = jnp.where(wet > level + part * 8, own - before, 0.0)
                        write(group, chunk, seg, tracer, rows, here)
                        vectors = [basis_ref[i, seg, tracer, rows, lanes] for i in range(BASIS)]
                        for i in range(BASIS):
                            sums[i] = sums[i] + vectors[i] * here
                        sums[BASIS] = sums[BASIS] + here * here
                        if products:
                            for at, (i, j) in enumerate(PAIRS):
                                sums[BASIS + 1 + at] = sums[BASIS + 1 + at] + vectors[i] * vectors[j]


def early_kernel(
    state_ref, wet_ref, basis_ref, head_ref, middle_ref, tail_ref, came_ref, out_ref, residual_ref, sums_ref, sems
):
    refs = [(head_ref, 0)] + [(middle_ref, i) for i in range(GROUPS - 2)] + [(tail_ref, 0)]
    sums = [jnp.zeros((8, LANE), f32) for _ in range(BASIS + 1 + len(PAIRS))]

    def before_of(group, chunk, seg, tracer, level):
        if seg:
            ref, place = refs[group]
            return ref[place, pl.ds(group_row(tracer, chunk, seg - 1) + level, 8), :]
        return came_ref[group - 1, pl.ds((tracer * CHUNKS + chunk) * LEV + level, 8), :]

    def write(group, chunk, seg, tracer, rows, value):
        residual_ref[seg, tracer, rows, pl.ds(group * HALO + chunk * LANE, LANE)] = value

    residual_of(range(GROUPS), range(1, SEGS), state_ref, wet_ref, basis_ref, before_of, write, sums, True)
    parts = [(slice(1, SEGS),), (slice(0, 1), slice(None), slice(None), pl.ds(HALO, WIDTH - 2 * HALO))]
    copies = [pltpu.make_async_copy(residual_ref.at[part], out_ref.at[part], sems.at[i]) for i, part in enumerate(parts)]
    copies[0].start()
    residual_of(range(1, GROUPS - 1), (0,), state_ref, wet_ref, basis_ref, before_of, write, sums, True)
    copies[1].start()
    for group in (0, GROUPS - 1):
        for chunk in range(CHUNKS):
            lanes = pl.ds(group * HALO + chunk * LANE, LANE)
            for tracer in range(TRACERS):
                for part in range(LEV // 8):
                    vectors = [basis_ref[i, 0, tracer, pl.ds(part * 8, 8), lanes] for i in range(BASIS)]
                    for at, (i, j) in enumerate(PAIRS):
                        sums[BASIS + 1 + at] = sums[BASIS + 1 + at] + vectors[i] * vectors[j]
    for i, one in enumerate(sums):
        sums_ref[i] = one
    for copy in copies:
        copy.wait()


def late_kernel(
    state_ref, wet_ref, basis_ref, came_ref, early_ref, unused_ref, residual_ref, sums_ref, pieces_ref, sems
):
    sums = [early_ref[i] for i in range(BASIS + 1 + len(PAIRS))]

    def before_of(group, chunk, seg, tracer, level):
        return came_ref[EDGE_PLACES[group], pl.ds((tracer * CHUNKS + chunk) * LEV + level, 8), :]

    def write(group, chunk, seg, tracer, rows, value):
        pieces_ref[EDGE_PLACES[group], tracer, rows, pl.ds(chunk * LANE, LANE)] = value

    copies = []
    for group, place in EDGE_PLACES.items():
        residual_of((group,), (0,), state_ref, wet_ref, basis_ref, before_of, write, sums, False)
        copy = pltpu.make_async_copy(
            pieces_ref.at[place], residual_ref.at[0, :, :, pl.ds(group * HALO, HALO)], sems.at[place]
        )
        copy.start()
        copies.append(copy)
    rows = [jnp.sum(one, axis=0, keepdims=True) for one in sums]
    rows.append(jnp.zeros((16 - len(rows), LANE), f32))
    sums_ref[...] = jnp.concatenate(rows, axis=0)
    for copy in copies:
        copy.wait()


def early(state, wet, basis, head, middle, tail, came):
    whole = shape(SEGS, TRACERS, LEV, WIDTH)
    return pl.pallas_call(
        early_kernel,
        out_shape=(whole, whole, shape(BASIS + 1 + len(PAIRS), 8, LANE)),
        in_specs=[VMEM] * 7,
        out_specs=(HBM, VMEM, VMEM),
        scratch_shapes=[pltpu.SemaphoreType.DMA((2,))],
        compiler_params=PARAMS,
        cost_estimate=pl.CostEstimate(flops=10_000_000, bytes_accessed=4_000_000, transcendentals=0),
        name="residual_known",
    )(state, wet, basis, head, middle, tail, came)


def late(state, wet, basis, came, sums, residual):
    return pl.pallas_call(
        late_kernel,
        out_shape=(shape(SEGS, TRACERS, LEV, WIDTH), shape(16, LANE), shape(2, TRACERS, LEV, HALO)),
        in_specs=[VMEM] * 5 + [HBM],
        out_specs=(HBM, VMEM, VMEM),
        scratch_shapes=[pltpu.SemaphoreType.DMA((2,))],
        input_output_aliases={5: 0},
        compiler_params=PARAMS,
        cost_estimate=pl.CostEstimate(flops=3_000_000, bytes_accessed=4_000_000, transcendentals=0),
        name="residual_last",
    )(state, wet, basis, came, sums, residual)


def scaled_kernel(count, residual_ref, pieces_ref, basis_ref, sums_ref, new_ref, coefficients_ref):
    sums = jnp.sum(sums_ref[...], axis=1, keepdims=True)
    one = [sums[i : i + 1] for i in range(16)]
    first, square, products = one[:BASIS], one[BASIS], iter(one[BASIS + 1 :])
    gram = [[None] * BASIS for _ in range(BASIS)]
    for i in range(BASIS):
        for j in range(i, BASIS):
            gram[i][j] = gram[j][i] = next(products)
    second = [first[i] - sum(gram[i][j] * first[j] for j in range(BASIS)) for i in range(BASIS)]
    both = [first[i] + second[i] for i in range(BASIS)]
    for i in range(BASIS):
        square = square - both[i] * (2.0 * first[i] - sum(gram[i][j] * both[j] for j in range(BASIS)))
    spread = jnp.sqrt(square / count + epsilon)
    lane = lax.broadcasted_iota(jnp.int32, (8, LANE), 1)
    result = jnp.zeros((8, LANE), f32)
    for i, value in enumerate(both + [spread]):
        result = jnp.where(lane == i, value, result)
    coefficients_ref[...] = result
    scale = 1.0 / spread
    weights = [jnp.broadcast_to(-value * scale, (LEV, LANE)) for value in both]
    scale = jnp.broadcast_to(scale, (LEV, LANE))
    for seg in range(SEGS):
        for tracer in range(TRACERS):
            for chunk in range(WIDTH // LANE):
                lanes = pl.ds(chunk * LANE, LANE)
                group = chunk // CHUNKS
                if seg == 0 and group in EDGE_PLACES:
                    here = pieces_ref[EDGE_PLACES[group], tracer, :, pl.ds(chunk % CHUNKS * LANE, LANE)]
                else:
                    here = residual_ref[seg, tracer, :, lanes]
                total = here * scale
                for i in range(BASIS):
                    total = total + weights[i] * basis_ref[i, seg, tracer, :, lanes]
                new_ref[seg, tracer, :, lanes] = total


def scaled(count, residual, pieces, basis, sums):
    return call(
        functools.partial(scaled_kernel, count), "orthogonal_and_scaled", 4_000_000,
        (shape(SEGS, TRACERS, LEV, WIDTH), shape(8, LANE)), [], residual, pieces, basis, sums,
    )


def shifted(block, axis, distance):
    count = lax.axis_size(axis)
    return lax.ppermute(block, axis, [(i, (i + distance) % count) for i in range(count)])


def summed_everywhere(value):
    for axis in ("seg", "col"):
        count = lax.axis_size(axis)
        done = 1
        while done < count:
            flip = done if done in (1, 2, 4, 8) else done
            value = value + lax.ppermute(value, axis, [(i, i ^ FLIPS[axis][flip]) for i in range(count)])
            done *= 2
    return value


FLIPS = {"seg": {1: 1, 2: 2, 4: 6}, "col": {1: 1, 2: 3, 4: 4, 8: 12}}


def per_device(segment_state, light, mixing, kappa, neighbour_columns, wet_levels, basis):
    every_column = lax.axis_size("col") * WIDTH
    state = pltpu.with_memory_space_constraint(segment_state, pltpu.VMEM)
    head, tail = halves(state)
    left = shifted(tail, "col", 1)
    right = shifted(head, "col", -1)
    table = neighbour_columns.T
    wet = wet_levels.reshape(WIDTH // LANE, LANE)
    edge, middle, *kept = first_own(every_column, state, table, mixing, light, kappa, wet)
    *factors, table, mixing, light, wet = kept
    head, tail = edges(True, every_column, left, right, table, mixing, edge, factors)
    left = shifted(tail, "col", 1)
    right = shifted(head, "col", -1)
    end_middle, sent, xs = second_middle(every_column, head, middle, tail, table, mixing, light, factors)
    came_middle = shifted(sent, "seg", 1)
    edge = second_edge(every_column, head, middle, tail, table, mixing, light, xs)
    head, tail, sent = edges(False, every_column, left, right, table, mixing, edge, factors)
    came_edge = shifted(sent, "seg", 1)
    residual, held, sums = early(state, wet, basis, head, end_middle, tail, came_middle)
    residual, sums, pieces = late(state, wet, basis, came_edge, sums, residual)
    count = lax.axis_size("seg") * SEGS * TRACERS * LEV * every_column
    new_vector, coefficients = scaled(count, held, pieces, basis, summed_everywhere(sums))
    return (residual, new_vector, coefficients[0, : BASIS + 1])


def solution(mesh):
    return jax.shard_map(
        per_device,
        mesh=mesh,
        in_specs=(
            P("seg", None, None, "col"),
            P("seg", None, "col"),
            P("seg", None, None, "col"),
            P("seg", None, "col"),
            P("col", None),
            P("col"),
            P(None, "seg", None, None, "col"),
        ),
        out_specs=(P("seg", None, None, "col"), P("seg", None, None, "col"), P()),
        check_vma=False,
    )
```

```python
import functools

import jax
import jax.numpy as jnp
from jax import lax
from jax.experimental import pallas as pl
from jax.experimental.pallas import tpu as pltpu
from jax.sharding import PartitionSpec as P

uptake_rate = 0.6
half_saturation = 0.3
remin_rate = 0.2
dissolved_share = 0.7
epsilon = 1e-06

SEGS = 2
TRACERS = 2
LEV = 32
NBR = 6
BASIS = 4
WIDTH = 2048
HALO = 512
LANE = 128
TILE = 256
BLOCKS = WIDTH // TILE
GROUPS = WIDTH // HALO
CHUNKS = HALO // LANE
ROWS = SEGS * TRACERS * LEV
GROUP_ROWS = TRACERS * CHUNKS * SEGS * LEV
VMEM = pl.BlockSpec(memory_space=pltpu.VMEM)
PARAMS = pltpu.CompilerParams(vmem_limit_bytes=16 * 1024 * 1024)
ANY = pl.BlockSpec(memory_space=pl.ANY)
HBM = pl.BlockSpec(memory_space=pltpu.HBM)
f32 = jnp.float32
bf16 = jnp.bfloat16


def shape(*dims):
    return jax.ShapeDtypeStruct(dims, f32)


def group_row(tracer, chunk, seg):
    return ((tracer * CHUNKS + chunk) * SEGS + seg) * LEV


def natural_reader(ref):
    def read(seg, tracer, start):
        return ref[seg, tracer, :, pl.ds(start, TILE)]

    return read


def group_reader(refs):
    def read(seg, tracer, start):
        ref, place = refs[start // HALO]
        chunk = start % HALO // LANE
        parts = [ref[place, pl.ds(group_row(tracer, chunk + h, seg), LEV), :] for h in range(TILE // LANE)]
        return jnp.concatenate(parts, axis=1)

    return read


def split_tile(read, start, xs_ref, place):
    for seg in range(SEGS):
        for tracer in range(TRACERS):
            value = read(seg, tracer, start)
            high = value.astype(bf16)
            low = (value - high.astype(f32)).astype(bf16)
            row = (seg * TRACERS + tracer) * LEV
            xs_ref[place, pl.ds(row, LEV), :] = high
            xs_ref[place, pl.ds(ROWS + row, LEV), :] = low


def table_row(every_column, table_ref, k, start):
    columns = pl.ds(start, TILE)
    away = table_ref[pl.ds(k, 1), columns] - table_ref[pl.ds(0, 1), columns]
    away = jnp.where(away > HALO, away - every_column, away)
    away = jnp.where(away < -HALO, away + every_column, away)
    return away + lax.broadcasted_iota(jnp.int32, (1, TILE), 1) + start


def picked(xs_ref, places, offsets, index):
    total = None
    depth = lax.broadcasted_iota(jnp.int32, (TILE, TILE), 0)
    for place, offset in zip(places, offsets):
        chosen = jnp.where(depth == index - offset, f32(1), f32(0)).astype(bf16)
        part = jnp.dot(xs_ref[place], chosen, preferred_element_type=f32)
        total = part if total is None else total + part
    return total[:ROWS] + total[ROWS:]


def moved_part(xs_ref, places, offsets, index_of, mixing_of):
    total = [None] * (SEGS * TRACERS)
    for k in range(1, NBR):
        value = picked(xs_ref, places, offsets, index_of(k))
        for seg in range(SEGS):
            mix = mixing_of(seg, k)
            for tracer in range(TRACERS):
                at = seg * TRACERS + tracer
                term = mix * value[at * LEV : (at + 1) * LEV]
                total[at] = term if total[at] is None else total[at] + term
    return total


def factorize(kappa_ref, wet_ref, by_rows_ref, inverse_ref, carry_ref, ratio_ref):
    for group in range(GROUPS):
        for chunk in range(CHUNKS):
            for seg in range(SEGS):
                lanes = pl.ds(group * HALO + chunk * LANE, LANE)
                row = (group * CHUNKS * SEGS + chunk * SEGS + seg) * LEV
                by_rows_ref[pl.ds(row, LEV), :] = kappa_ref[seg, :, lanes]
    wet = []
    for group in range(GROUPS):
        rows = []
        for chunk in range(CHUNKS):
            one = wet_ref[pl.ds(group * CHUNKS + chunk, 1), :]
            rows += [one] * SEGS
        wet.append(jnp.concatenate(rows, axis=0))
    zero = jnp.zeros((CHUNKS * SEGS, LANE), f32)

    def upper_at(group, level):
        if level == 0 or level == LEV:
            return zero
        rows = pl.ds(group * CHUNKS * SEGS * LEV + level, CHUNKS * SEGS, stride=LEV)
        return jnp.where(wet[group] > level, by_rows_ref[rows, :], 0.0)

    upper = [upper_at(group, 0) for group in range(GROUPS)]
    ratio = [zero] * GROUPS
    for level in range(LEV):
        for group in range(GROUPS):
            lower = upper_at(group, level + 1)
            pivot = (1.0 + upper[group] + lower) + upper[group] * ratio[group]
            inverse = 1.0 / pivot
            ratio[group] = -lower * inverse
            inverse_ref[group, level] = jnp.where(wet[group] > level, inverse, 0.0)
            carry_ref[group, level] = upper[group] * inverse
            ratio_ref[group, level] = ratio[group]
            upper[group] = lower


def solve(source_ref, place, inverse_ref, carry_ref, ratio_ref, group, out):
    step = CHUNKS * SEGS

    def source(tracer, level):
        return source_ref[place, pl.ds(group_row(tracer, 0, 0) + level, step, stride=LEV), :]

    value = [[None] * LEV for _ in range(TRACERS)]
    for level in range(LEV):
        inverse = inverse_ref[group, level]
        carry = carry_ref[group, level]
        for tracer in range(TRACERS):
            here = source(tracer, level) * inverse
            if level:
                here = here + carry * value[tracer][level - 1]
            value[tracer][level] = here
    for level in range(LEV - 1, -1, -1):
        ratio = ratio_ref[group, level]
        for tracer in range(TRACERS):
            if level < LEV - 1:
                value[tracer][level] = value[tracer][level] - ratio * value[tracer][level + 1]
            out(tracer, level, value[tracer][level])


def into_group(ref, place):
    def write(tracer, level, value):
        ref[place, pl.ds(group_row(tracer, 0, 0) + level, CHUNKS * SEGS, stride=LEV), :] = value

    return write


def own_blocks(every_column, blocks, read, table_ref, mixing_ref, light_ref, xs_ref, acc_ref, places, ready=None):
    for block in blocks:
        if ready is not None:
            ready(block)
        start = block * TILE
        tiles = list(range(max(0, block - 2), min(BLOCKS, block + 3)))
        total = moved_part(
            xs_ref,
            tiles,
            [tile * TILE for tile in tiles],
            lambda k: table_row(every_column, table_ref, k, start),
            lambda seg, k: mixing_ref[seg, k, :, pl.ds(start, TILE)],
        )
        for seg in range(SEGS):
            columns = pl.ds(start, TILE)
            phosphate = read(seg, 0, start)
            organic = read(seg, 1, start)
            squared = phosphate * phosphate
            uptake = uptake_rate * light_ref[seg, :, columns] * squared / (squared + half_saturation)
            gains = (remin_rate * organic - uptake, dissolved_share * uptake - remin_rate * organic)
            own = mixing_ref[seg, 0, :, columns]
            for tracer, value in enumerate((phosphate, organic)):
                result = own * value + total[seg * TRACERS + tracer] + gains[tracer]
                for h in range(TILE // LANE):
                    row = group_row(tracer, block % 2 * 2 + h, seg)
                    acc_ref[places[block // 2], pl.ds(row, LEV), :] = result[:, h * LANE : (h + 1) * LANE]


EDGE_BLOCKS = (0, 1, BLOCKS - 2, BLOCKS - 1)
MIDDLE_BLOCKS = tuple(range(2, BLOCKS - 2))
EDGE_PLACES = {0: 0, GROUPS - 1: 1}
MIDDLE_PLACES = {group: group - 1 for group in range(1, GROUPS - 1)}


def sent_rows(from_ref, place, to_ref, to_place):
    for tracer in range(TRACERS):
        for chunk in range(CHUNKS):
            to_ref[to_place, pl.ds((tracer * CHUNKS + chunk) * LEV, LEV), :] = from_ref[
                place, pl.ds(group_row(tracer, chunk, SEGS - 1), LEV), :
            ]


def halves_kernel(state_ref, head_ref, tail_ref):
    head_ref[...] = state_ref[:, :, :, :HALO]
    tail_ref[...] = state_ref[:, :, :, WIDTH - HALO :]


def halves(state):
    half = shape(SEGS, TRACERS, LEV, HALO)
    return call(halves_kernel, "edge_columns", 0, (half, half), [], state)


def first_own_kernel(
    every_column, state_ref, table_in, mixing_in, light_in, kappa_in, wet_in,
    edge_ref, middle_ref, inverse_ref, carry_ref, ratio_ref, table_ref, mixing_ref, light_ref, wet_ref,
    xs_ref, acc_ref, by_rows_ref, kappa_ref, sems,
):
    order = (0, GROUPS - 1) + tuple(range(1, GROUPS - 1))
    parts = [(slice(None),) * 3 + (pl.ds(group * HALO, HALO),) for group in order]
    of_mixing = [(mixing_in.at[part], mixing_ref.at[part]) for part in parts]
    pairs = [(table_in, table_ref), (light_in, light_ref), (kappa_in, kappa_ref), (wet_in, wet_ref)]
    pairs = pairs[:2] + of_mixing[:1] + pairs[2:] + of_mixing[1:]
    copies = [pltpu.make_async_copy(*pair, sems.at[i]) for i, pair in enumerate(pairs)]
    for copy in copies:
        copy.start()
    read = natural_reader(state_ref)
    for tile in range(BLOCKS):
        split_tile(read, tile * TILE, xs_ref, tile)

    def ready(block):
        if block == 0:
            for copy in copies[:3]:
                copy.wait()
        elif block == BLOCKS - 2:
            copies[3].wait()
            copies[4].wait()
            factorize(kappa_ref, wet_ref, by_rows_ref, inverse_ref, carry_ref, ratio_ref)
            for copy in copies[5:]:
                copy.wait()

    own_blocks(every_column, EDGE_BLOCKS, read, table_ref, mixing_ref, light_ref, xs_ref, edge_ref, EDGE_PLACES, ready)
    own_blocks(every_column, MIDDLE_BLOCKS, read, table_ref, mixing_ref, light_ref, xs_ref, acc_ref, MIDDLE_PLACES, ready)
    for group, place in MIDDLE_PLACES.items():
        solve(acc_ref, place, inverse_ref, carry_ref, ratio_ref, group, into_group(middle_ref, place))


def second_reader(head_ref, middle_ref, tail_ref):
    return group_reader([(head_ref, 0)] + [(middle_ref, i) for i in range(GROUPS - 2)] + [(tail_ref, 0)])


def second_middle_kernel(
    every_column, head_ref, middle_in_ref, tail_ref, table_ref, mixing_ref, light_ref, inverse_ref, carry_ref, ratio_ref,
    middle_ref, sent_ref, xs_ref,
    acc_ref,
):
    read = second_reader(head_ref, middle_in_ref, tail_ref)
    for tile in range(BLOCKS):
        split_tile(read, tile * TILE, xs_ref, tile)
    own_blocks(every_column, MIDDLE_BLOCKS, read, table_ref, mixing_ref, light_ref, xs_ref, acc_ref, MIDDLE_PLACES)
    for group, place in MIDDLE_PLACES.items():
        solve(acc_ref, place, inverse_ref, carry_ref, ratio_ref, group, into_group(middle_ref, place))
        sent_rows(middle_ref, place, sent_ref, place)


def second_edge_kernel(every_column, head_ref, middle_ref, tail_ref, table_ref, mixing_ref, light_ref, xs_ref, edge_ref):
    read = second_reader(head_ref, middle_ref, tail_ref)
    own_blocks(every_column, EDGE_BLOCKS, read, table_ref, mixing_ref, light_ref, xs_ref, edge_ref, EDGE_PLACES)


def edge_kernel(
    first, every_column, left_ref, right_ref, table_ref, mixing_ref, edge_in_ref, inverse_ref, carry_ref, ratio_ref,
    *outs_and_scratch,
):
    head_ref, tail_ref, *sent, xs_ref, acc_ref = outs_and_scratch
    for side, ref in enumerate((left_ref, right_ref)):
        read = natural_reader(ref) if first else group_reader([(ref, 0)])
        for tile in range(HALO // TILE):
            split_tile(read, tile * TILE, xs_ref, side * 2 + tile)
    uses = ((0, 0, (0, 1)), (1, 0, (1,)), (BLOCKS - 2, 1, (2,)), (BLOCKS - 1, 1, (2, 3)))
    offsets = (-HALO, -TILE, WIDTH, WIDTH + TILE)
    for block, side, places in uses:
        start = block * TILE
        total = moved_part(
            xs_ref,
            places,
            [offsets[place] for place in places],
            lambda k: table_row(every_column, table_ref, k, start),
            lambda seg, k: mixing_ref[seg, k, :, pl.ds(start, TILE)],
        )
        for seg in range(SEGS):
            for tracer in range(TRACERS):
                value = total[seg * TRACERS + tracer]
                for h in range(TILE // LANE):
                    row = pl.ds(group_row(tracer, block % 2 * 2 + h, seg), LEV)
                    acc_ref[side, row, :] = edge_in_ref[side, row, :] + value[:, h * LANE : (h + 1) * LANE]
    for side, (group, ref) in enumerate(((0, head_ref), (GROUPS - 1, tail_ref))):
        solve(acc_ref, side, inverse_ref, carry_ref, ratio_ref, group, into_group(ref, 0))
        if sent:
            sent_rows(ref, 0, sent[0], side)


EDGE = shape(2, GROUP_ROWS, LANE)
MIDDLE = shape(GROUPS - 2, GROUP_ROWS, LANE)
SENT = shape(2, GROUP_ROWS // SEGS, LANE)
ONE = shape(1, GROUP_ROWS, LANE)


def call(kernel, name, flops, outs, scratch, *operands):
    return pl.pallas_call(
        kernel,
        out_shape=outs,
        in_specs=[VMEM] * len(operands),
        out_specs=jax.tree.map(lambda _: VMEM, outs),
        scratch_shapes=scratch,
        compiler_params=PARAMS,
        cost_estimate=pl.CostEstimate(flops=flops, bytes_accessed=4_000_000, transcendentals=0),
        name=name,
    )(*operands)


def first_own(every_column, state, table, mixing, light, kappa, wet):
    factors = shape(GROUPS, LEV, CHUNKS * SEGS, LANE)
    like = [jax.ShapeDtypeStruct(one.shape, one.dtype) for one in (table, mixing, light, wet)]
    return pl.pallas_call(
        functools.partial(first_own_kernel, every_column),
        out_shape=(EDGE, MIDDLE, factors, factors, factors, *like),
        in_specs=[VMEM] + [HBM] * 5,
        out_specs=(VMEM,) * 9,
        scratch_shapes=[
            pltpu.VMEM((BLOCKS, 2 * ROWS, TILE), bf16),
            pltpu.VMEM((GROUPS - 2, GROUP_ROWS, LANE), f32),
            pltpu.VMEM((GROUPS * CHUNKS * SEGS * LEV, LANE), f32),
            pltpu.VMEM((SEGS, LEV, WIDTH), f32),
            pltpu.SemaphoreType.DMA((4 + GROUPS,)),
        ],
        compiler_params=PARAMS,
        cost_estimate=pl.CostEstimate(flops=6_000_000_000, bytes_accessed=4_000_000, transcendentals=0),
        name="first_step_own",
    )(state, *[pltpu.with_memory_space_constraint(one, pltpu.HBM) for one in (table, mixing, light, kappa, wet)])


def second_middle(every_column, head, middle, tail, table, mixing, light, factors):
    return call(
        functools.partial(second_middle_kernel, every_column), "second_step_middle", 3_500_000_000,
        (MIDDLE, SENT, jax.ShapeDtypeStruct((BLOCKS, 2 * ROWS, TILE), bf16)),
        [pltpu.VMEM((GROUPS - 2, GROUP_ROWS, LANE), f32)],
        head, middle, tail, table, mixing, light, *factors,
    )


def second_edge(every_column, head, middle, tail, table, mixing, light, xs):
    return call(
        functools.partial(second_edge_kernel, every_column), "second_step_edges_own", 2_500_000_000, EDGE, [],
        head, middle, tail, table, mixing, light, xs,
    )


def edges(first, every_column, left, right, table, mixing, edge, factors):
    return call(
        functools.partial(edge_kernel, first, every_column),
        "first_step_edges" if first else "second_step_edges", 1_000_000_000,
        (ONE, ONE) if first else (ONE, ONE, SENT),
        [pltpu.VMEM((4, 2 * ROWS, TILE), bf16), pltpu.VMEM((2, GROUP_ROWS, LANE), f32)],
        left, right, table, mixing, edge, *factors,
    )


PAIRS = [(i, j) for i in range(BASIS) for j in range(i, BASIS)]


def residual_of(groups, segs, state_ref, wet_ref, basis_ref, before_of, write, sums, products):
    level = lax.broadcasted_iota(jnp.int32, (8, LANE), 0)
    for group in groups:
        for chunk in range(CHUNKS):
            lanes = pl.ds(group * HALO + chunk * LANE, LANE)
            wet = jnp.broadcast_to(wet_ref[pl.ds(group * CHUNKS + chunk, 1), :], (8, LANE))
            for seg in segs:
                for tracer in range(TRACERS):
                    for part in range(LEV // 8):
                        rows = pl.ds(part * 8, 8)
                        before = before_of(group, chunk, seg, tracer, part * 8)
                        own = state_ref[seg, tracer, rows, lanes]
                        here = jnp.where(wet > level + part * 8, own - before, 0.0)
                        write(group, chunk, seg, tracer, rows, here)
                        vectors = [basis_ref[i, seg, tracer, rows, lanes] for i in range(BASIS)]
                        for i in range(BASIS):
                            sums[i] = sums[i] + vectors[i] * here
                        sums[BASIS] = sums[BASIS] + here * here
                        if products:
                            for at, (i, j) in enumerate(PAIRS):
                                sums[BASIS + 1 + at] = sums[BASIS + 1 + at] + vectors[i] * vectors[j]


def early_kernel(
    state_ref, wet_ref, basis_ref, head_ref, middle_ref, tail_ref, came_ref, out_ref, residual_ref, sums_ref, sems
):
    refs = [(head_ref, 0)] + [(middle_ref, i) for i in range(GROUPS - 2)] + [(tail_ref, 0)]
    sums = [jnp.zeros((8, LANE), f32) for _ in range(BASIS + 1 + len(PAIRS))]

    def before_of(group, chunk, seg, tracer, level):
        if seg:
            ref, place = refs[group]
            return ref[place, pl.ds(group_row(tracer, chunk, seg - 1) + level, 8), :]
        return came_ref[group - 1, pl.ds((tracer * CHUNKS + chunk) * LEV + level, 8), :]

    def write(group, chunk, seg, tracer, rows, value):
        residual_ref[seg, tracer, rows, pl.ds(group * HALO + chunk * LANE, LANE)] = value

    residual_of(range(GROUPS), range(1, SEGS), state_ref, wet_ref, basis_ref, before_of, write, sums, True)
    parts = [(slice(1, SEGS),), (slice(0, 1), slice(None), slice(None), pl.ds(HALO, WIDTH - 2 * HALO))]
    copies = [pltpu.make_async_copy(residual_ref.at[part], out_ref.at[part], sems.at[i]) for i, part in enumerate(parts)]
    copies[0].start()
    residual_of(range(1, GROUPS - 1), (0,), state_ref, wet_ref, basis_ref, before_of, write, sums, True)
    copies[1].start()
    for group in (0, GROUPS - 1):
        for chunk in range(CHUNKS):
            lanes = pl.ds(group * HALO + chunk * LANE, LANE)
            for tracer in range(TRACERS):
                for part in range(LEV // 8):
                    vectors = [basis_ref[i, 0, tracer, pl.ds(part * 8, 8), lanes] for i in range(BASIS)]
                    for at, (i, j) in enumerate(PAIRS):
                        sums[BASIS + 1 + at] = sums[BASIS + 1 + at] + vectors[i] * vectors[j]
    for i, one in enumerate(sums):
        sums_ref[i] = one
    for copy in copies:
        copy.wait()


def late_kernel(
    state_ref, wet_ref, basis_ref, came_ref, early_ref, unused_ref, residual_ref, sums_ref, pieces_ref, sems
):
    sums = [early_ref[i] for i in range(BASIS + 1 + len(PAIRS))]

    def before_of(group, chunk, seg, tracer, level):
        return came_ref[EDGE_PLACES[group], pl.ds((tracer * CHUNKS + chunk) * LEV + level, 8), :]

    def write(group, chunk, seg, tracer, rows, value):
        pieces_ref[EDGE_PLACES[group], tracer, rows, pl.ds(chunk * LANE, LANE)] = value

    copies = []
    for group, place in EDGE_PLACES.items():
        residual_of((group,), (0,), state_ref, wet_ref, basis_ref, before_of, write, sums, False)
        copy = pltpu.make_async_copy(
            pieces_ref.at[place], residual_ref.at[0, :, :, pl.ds(group * HALO, HALO)], sems.at[place]
        )
        copy.start()
        copies.append(copy)
    lane = lax.broadcasted_iota(jnp.int32, (8, LANE), 1)
    row = jnp.zeros((8, LANE), f32)
    for i, one in enumerate(sums):
        row = jnp.where(lane == i, jnp.sum(jnp.sum(one, axis=0, keepdims=True), axis=1, keepdims=True), row)
    for i in range(sums_ref.shape[0] // 8):
        sums_ref[pl.ds(8 * i, 8), :] = row
    for copy in copies:
        copy.wait()


def early(state, wet, basis, head, middle, tail, came):
    whole = shape(SEGS, TRACERS, LEV, WIDTH)
    return pl.pallas_call(
        early_kernel,
        out_shape=(whole, whole, shape(BASIS + 1 + len(PAIRS), 8, LANE)),
        in_specs=[VMEM] * 7,
        out_specs=(HBM, VMEM, VMEM),
        scratch_shapes=[pltpu.SemaphoreType.DMA((2,))],
        compiler_params=PARAMS,
        cost_estimate=pl.CostEstimate(flops=10_000_000, bytes_accessed=4_000_000, transcendentals=0),
        name="residual_known",
    )(state, wet, basis, head, middle, tail, came)


def late(devices, state, wet, basis, came, sums, residual):
    return pl.pallas_call(
        late_kernel,
        out_shape=(shape(SEGS, TRACERS, LEV, WIDTH), shape(devices, LANE), shape(2, TRACERS, LEV, HALO)),
        in_specs=[VMEM] * 5 + [HBM],
        out_specs=(HBM, VMEM, VMEM),
        scratch_shapes=[pltpu.SemaphoreType.DMA((2,))],
        input_output_aliases={5: 0},
        compiler_params=PARAMS,
        cost_estimate=pl.CostEstimate(flops=3_000_000, bytes_accessed=4_000_000, transcendentals=0),
        name="residual_last",
    )(state, wet, basis, came, sums, residual)


def scaled_kernel(count, residual_ref, pieces_ref, basis_ref, sums_ref, new_ref, coefficients_ref):
    sums = jnp.sum(sums_ref[...], axis=0, keepdims=True)
    one = [sums[:, i : i + 1] for i in range(BASIS + 1 + len(PAIRS))]
    first, square, products = one[:BASIS], one[BASIS], iter(one[BASIS + 1 :])
    gram = [[None] * BASIS for _ in range(BASIS)]
    for i in range(BASIS):
        for j in range(i, BASIS):
            gram[i][j] = gram[j][i] = next(products)
    second = [first[i] - sum(gram[i][j] * first[j] for j in range(BASIS)) for i in range(BASIS)]
    both = [first[i] + second[i] for i in range(BASIS)]
    for i in range(BASIS):
        square = square - both[i] * (2.0 * first[i] - sum(gram[i][j] * both[j] for j in range(BASIS)))
    spread = jnp.sqrt(square / count + epsilon)
    lane = lax.broadcasted_iota(jnp.int32, (8, LANE), 1)
    result = jnp.zeros((8, LANE), f32)
    for i, value in enumerate(both + [spread]):
        result = jnp.where(lane == i, value, result)
    coefficients_ref[...] = result
    scale = 1.0 / spread
    weights = [jnp.broadcast_to(-value * scale, (LEV, LANE)) for value in both]
    scale = jnp.broadcast_to(scale, (LEV, LANE))
    for seg in range(SEGS):
        for tracer in range(TRACERS):
            for chunk in range(WIDTH // LANE):
                lanes = pl.ds(chunk * LANE, LANE)
                group = chunk // CHUNKS
                if seg == 0 and group in EDGE_PLACES:
                    here = pieces_ref[EDGE_PLACES[group], tracer, :, pl.ds(chunk % CHUNKS * LANE, LANE)]
                else:
                    here = residual_ref[seg, tracer, :, lanes]
                total = here * scale
                for i in range(BASIS):
                    total = total + weights[i] * basis_ref[i, seg, tracer, :, lanes]
                new_ref[seg, tracer, :, lanes] = total


def scaled(count, residual, pieces, basis, sums):
    return call(
        functools.partial(scaled_kernel, count), "orthogonal_and_scaled", 4_000_000,
        (shape(SEGS, TRACERS, LEV, WIDTH), shape(8, LANE)), [], residual, pieces, basis, sums,
    )


def shifted(block, axis, distance):
    count = lax.axis_size(axis)
    return lax.ppermute(block, axis, [(i, (i + distance) % count) for i in range(count)])


def per_device(segment_state, light, mixing, kappa, neighbour_columns, wet_levels, basis):
    every_column = lax.axis_size("col") * WIDTH
    state = pltpu.with_memory_space_constraint(segment_state, pltpu.VMEM)
    head, tail = halves(state)
    left = shifted(tail, "col", 1)
    right = shifted(head, "col", -1)
    table = neighbour_columns.T
    wet = wet_levels.reshape(WIDTH // LANE, LANE)
    edge, middle, *kept = first_own(every_column, state, table, mixing, light, kappa, wet)
    *factors, table, mixing, light, wet = kept
    head, tail = edges(True, every_column, left, right, table, mixing, edge, factors)
    left = shifted(tail, "col", 1)
    right = shifted(head, "col", -1)
    end_middle, sent, xs = second_middle(every_column, head, middle, tail, table, mixing, light, factors)
    came_middle = shifted(sent, "seg", 1)
    edge = second_edge(every_column, head, middle, tail, table, mixing, light, xs)
    head, tail, sent = edges(False, every_column, left, right, table, mixing, edge, factors)
    came_edge = shifted(sent, "seg", 1)
    residual, held, sums = early(state, wet, basis, head, end_middle, tail, came_middle)
    devices = lax.axis_size("seg") * lax.axis_size("col")
    residual, sums, pieces = late(devices, state, wet, basis, came_edge, sums, residual)
    sums = lax.all_to_all(sums, ("seg", "col"), 0, 0, tiled=True)
    count = lax.axis_size("seg") * SEGS * TRACERS * LEV * every_column
    new_vector, coefficients = scaled(count, held, pieces, basis, sums)
    return (residual, new_vector, coefficients[0, : BASIS + 1])


def solution(mesh):
    return jax.shard_map(
        per_device,
        mesh=mesh,
        in_specs=(
            P("seg", None, None, "col"),
            P("seg", None, "col"),
            P("seg", None, None, "col"),
            P("seg", None, "col"),
            P("col", None),
            P("col"),
            P(None, "seg", None, None, "col"),
        ),
        out_specs=(P("seg", None, None, "col"), P("seg", None, None, "col"), P()),
        check_vma=False,
    )
```

```python
import functools

import jax
import jax.numpy as jnp
from jax import lax
from jax.experimental import pallas as pl
from jax.experimental.pallas import tpu as pltpu
from jax.sharding import PartitionSpec as P

uptake_rate = 0.6
half_saturation = 0.3
remin_rate = 0.2
dissolved_share = 0.7
epsilon = 1e-06

SEGS = 2
TRACERS = 2
LEV = 32
NBR = 6
BASIS = 4
WIDTH = 2048
HALO = 512
LANE = 128
TILE = 256
BLOCKS = WIDTH // TILE
GROUPS = WIDTH // HALO
CHUNKS = HALO // LANE
ROWS = SEGS * TRACERS * LEV
GROUP_ROWS = TRACERS * CHUNKS * SEGS * LEV
VMEM = pl.BlockSpec(memory_space=pltpu.VMEM)
PARAMS = pltpu.CompilerParams(vmem_limit_bytes=16 * 1024 * 1024)
ANY = pl.BlockSpec(memory_space=pl.ANY)
HBM = pl.BlockSpec(memory_space=pltpu.HBM)
f32 = jnp.float32
bf16 = jnp.bfloat16


def shape(*dims):
    return jax.ShapeDtypeStruct(dims, f32)


def group_row(tracer, chunk, seg):
    return ((tracer * CHUNKS + chunk) * SEGS + seg) * LEV


def natural_reader(ref):
    def read(seg, tracer, start):
        return ref[seg, tracer, :, pl.ds(start, TILE)]

    def one(seg, tracer, level, start):
        return ref[seg, tracer, pl.ds(level, 8), pl.ds(start, LANE)]

    return read, one


def group_reader(refs):
    def read(seg, tracer, start):
        ref, place = refs[start // HALO]
        chunk = start % HALO // LANE
        parts = [ref[place, pl.ds(group_row(tracer, chunk + h, seg), LEV), :] for h in range(TILE // LANE)]
        return jnp.concatenate(parts, axis=1)

    def one(seg, tracer, level, start):
        ref, place = refs[start // HALO]
        return ref[place, pl.ds(group_row(tracer, start % HALO // LANE, seg) + level, 8), :]

    return read, one


def split_tile(read, start, xs_ref, place):
    for seg in range(SEGS):
        for tracer in range(TRACERS):
            value = read(seg, tracer, start)
            high = value.astype(bf16)
            low = (value - high.astype(f32)).astype(bf16)
            row = (seg * TRACERS + tracer) * LEV
            xs_ref[place, pl.ds(row, LEV), :] = high
            xs_ref[place, pl.ds(ROWS + row, LEV), :] = low


def table_row(every_column, table_ref, k, start):
    columns = pl.ds(start, TILE)
    away = table_ref[pl.ds(k, 1), columns] - table_ref[pl.ds(0, 1), columns]
    away = jnp.where(away > HALO, away - every_column, away)
    away = jnp.where(away < -HALO, away + every_column, away)
    return away + lax.broadcasted_iota(jnp.int32, (1, TILE), 1)


def picked(xs_ref, places, offsets, index):
    total = None
    depth = lax.broadcasted_iota(jnp.int32, (TILE, TILE), 0)
    for place, offset in zip(places, offsets):
        chosen = jnp.where(depth == index - offset, f32(1), f32(0)).astype(bf16)
        part = jnp.dot(xs_ref[place], chosen, preferred_element_type=f32)
        total = part if total is None else total + part
    return total[:ROWS] + total[ROWS:]


def gathered(one, chunks, index):
    halves = []
    for h in range(TILE // LANE):
        at = jnp.broadcast_to(index[:, h * LANE : (h + 1) * LANE], (8, LANE))
        lane = at & (LANE - 1)
        usable = [(start, first) for start, first in chunks if abs(first - h * LANE) <= HALO]
        chosen = [at - lane == first for _, first in usable]
        rows = []
        for seg in range(SEGS):
            for tracer in range(TRACERS):
                for level in range(0, LEV, 8):
                    total = jnp.zeros((8, LANE), f32)
                    for (start, _), here in zip(usable, chosen):
                        value = jnp.take_along_axis(one(seg, tracer, level, start), lane, axis=1, mode="promise_in_bounds")
                        total = jnp.where(here, value, total)
                    rows.append(total)
        halves.append(jnp.concatenate(rows, axis=0))
    return jnp.concatenate(halves, axis=1)


def moved_part(xs_ref, places, offsets, index_of, mixing_of, one, chunks, by_lane):
    total = [None] * (SEGS * TRACERS)
    for k in range(1, NBR):
        index = index_of(k)
        value = gathered(one, chunks, index) if k in by_lane else picked(xs_ref, places, offsets, index)
        for seg in range(SEGS):
            mix = mixing_of(seg, k)
            for tracer in range(TRACERS):
                at = seg * TRACERS + tracer
                term = mix * value[at * LEV : (at + 1) * LEV]
                total[at] = term if total[at] is None else total[at] + term
    return total


def factorize(kappa_ref, wet_ref, by_rows_ref, inverse_ref, carry_ref, ratio_ref):
    for group in range(GROUPS):
        for chunk in range(CHUNKS):
            for seg in range(SEGS):
                lanes = pl.ds(group * HALO + chunk * LANE, LANE)
                row = (group * CHUNKS * SEGS + chunk * SEGS + seg) * LEV
                by_rows_ref[pl.ds(row, LEV), :] = kappa_ref[seg, :, lanes]
    wet = []
    for group in range(GROUPS):
        rows = []
        for chunk in range(CHUNKS):
            one = wet_ref[pl.ds(group * CHUNKS + chunk, 1), :]
            rows += [one] * SEGS
        wet.append(jnp.concatenate(rows, axis=0))
    zero = jnp.zeros((CHUNKS * SEGS, LANE), f32)

    def upper_at(group, level):
        if level == 0 or level == LEV:
            return zero
        rows = pl.ds(group * CHUNKS * SEGS * LEV + level, CHUNKS * SEGS, stride=LEV)
        return jnp.where(wet[group] > level, by_rows_ref[rows, :], 0.0)

    upper = [upper_at(group, 0) for group in range(GROUPS)]
    ratio = [zero] * GROUPS
    for level in range(LEV):
        for group in range(GROUPS):
            lower = upper_at(group, level + 1)
            pivot = (1.0 + upper[group] + lower) + upper[group] * ratio[group]
            inverse = 1.0 / pivot
            ratio[group] = -lower * inverse
            inverse_ref[group, level] = jnp.where(wet[group] > level, inverse, 0.0)
            carry_ref[group, level] = upper[group] * inverse
            ratio_ref[group, level] = ratio[group]
            upper[group] = lower


def solve(source_ref, place, inverse_ref, carry_ref, ratio_ref, group, out):
    step = CHUNKS * SEGS

    def source(tracer, level):
        return source_ref[place, pl.ds(group_row(tracer, 0, 0) + level, step, stride=LEV), :]

    value = [[None] * LEV for _ in range(TRACERS)]
    for level in range(LEV):
        inverse = inverse_ref[group, level]
        carry = carry_ref[group, level]
        for tracer in range(TRACERS):
            here = source(tracer, level) * inverse
            if level:
                here = here + carry * value[tracer][level - 1]
            value[tracer][level] = here
    for level in range(LEV - 1, -1, -1):
        ratio = ratio_ref[group, level]
        for tracer in range(TRACERS):
            if level < LEV - 1:
                value[tracer][level] = value[tracer][level] - ratio * value[tracer][level + 1]
            out(tracer, level, value[tracer][level])


def into_group(ref, place):
    def write(tracer, level, value):
        ref[place, pl.ds(group_row(tracer, 0, 0) + level, CHUNKS * SEGS, stride=LEV), :] = value

    return write


def own_blocks(every_column, blocks, readers, table_ref, mixing_ref, light_ref, xs_ref, acc_ref, places, ready=None):
    read, one = readers
    for block in blocks:
        if ready is not None:
            ready(block)
        start = block * TILE
        tiles = list(range(max(0, block - 2), min(BLOCKS, block + 3)))
        total = moved_part(
            xs_ref,
            tiles,
            [tile * TILE - start for tile in tiles],
            lambda k: table_row(every_column, table_ref, k, start),
            lambda seg, k: mixing_ref[seg, k, :, pl.ds(start, TILE)],
            one,
            [(tile * TILE + h, tile * TILE + h - start) for tile in tiles for h in range(0, TILE, LANE)],
            by_lane(block),
        )
        for seg in range(SEGS):
            columns = pl.ds(start, TILE)
            phosphate = read(seg, 0, start)
            organic = read(seg, 1, start)
            squared = phosphate * phosphate
            uptake = uptake_rate * light_ref[seg, :, columns] * squared / (squared + half_saturation)
            gains = (remin_rate * organic - uptake, dissolved_share * uptake - remin_rate * organic)
            own = mixing_ref[seg, 0, :, columns]
            for tracer, value in enumerate((phosphate, organic)):
                result = own * value + total[seg * TRACERS + tracer] + gains[tracer]
                for h in range(TILE // LANE):
                    row = group_row(tracer, block % 2 * 2 + h, seg)
                    acc_ref[places[block // 2], pl.ds(row, LEV), :] = result[:, h * LANE : (h + 1) * LANE]


def by_lane(block):
    return (4, 5) if block % 2 else (5,)


EDGE_BLOCKS = (0, 1, BLOCKS - 2, BLOCKS - 1)
MIDDLE_BLOCKS = tuple(range(2, BLOCKS - 2))
EDGE_PLACES = {0: 0, GROUPS - 1: 1}
MIDDLE_PLACES = {group: group - 1 for group in range(1, GROUPS - 1)}


def sent_rows(from_ref, place, to_ref, to_place):
    for tracer in range(TRACERS):
        for chunk in range(CHUNKS):
            to_ref[to_place, pl.ds((tracer * CHUNKS + chunk) * LEV, LEV), :] = from_ref[
                place, pl.ds(group_row(tracer, chunk, SEGS - 1), LEV), :
            ]


def halves_kernel(state_ref, head_ref, tail_ref):
    head_ref[...] = state_ref[:, :, :, :HALO]
    tail_ref[...] = state_ref[:, :, :, WIDTH - HALO :]


def halves(state):
    half = shape(SEGS, TRACERS, LEV, HALO)
    return call(halves_kernel, "edge_columns", 0, (half, half), [], state)


def first_own_kernel(
    every_column, state_ref, table_in, mixing_in, light_in, kappa_in, wet_in,
    edge_ref, middle_ref, inverse_ref, carry_ref, ratio_ref, table_ref, mixing_ref, light_ref, wet_ref,
    xs_ref, acc_ref, by_rows_ref, kappa_ref, sems,
):
    order = (0, GROUPS - 1) + tuple(range(1, GROUPS - 1))
    parts = [(slice(None),) * 3 + (pl.ds(group * HALO, HALO),) for group in order]
    of_mixing = [(mixing_in.at[part], mixing_ref.at[part]) for part in parts]
    pairs = [(table_in, table_ref), (light_in, light_ref), (kappa_in, kappa_ref), (wet_in, wet_ref)]
    pairs = pairs[:2] + of_mixing[:1] + pairs[2:] + of_mixing[1:]
    copies = [pltpu.make_async_copy(*pair, sems.at[i]) for i, pair in enumerate(pairs)]
    for copy in copies:
        copy.start()
    read = natural_reader(state_ref)
    for tile in range(BLOCKS):
        split_tile(read[0], tile * TILE, xs_ref, tile)

    def ready(block):
        if block == 0:
            for copy in copies[:3]:
                copy.wait()
        elif block == BLOCKS - 2:
            copies[3].wait()
            copies[4].wait()
            factorize(kappa_ref, wet_ref, by_rows_ref, inverse_ref, carry_ref, ratio_ref)
            for copy in copies[5:]:
                copy.wait()

    own_blocks(every_column, EDGE_BLOCKS, read, table_ref, mixing_ref, light_ref, xs_ref, edge_ref, EDGE_PLACES, ready)
    own_blocks(every_column, MIDDLE_BLOCKS, read, table_ref, mixing_ref, light_ref, xs_ref, acc_ref, MIDDLE_PLACES, ready)
    for group, place in MIDDLE_PLACES.items():
        solve(acc_ref, place, inverse_ref, carry_ref, ratio_ref, group, into_group(middle_ref, place))


def second_reader(head_ref, middle_ref, tail_ref):
    return group_reader([(head_ref, 0)] + [(middle_ref, i) for i in range(GROUPS - 2)] + [(tail_ref, 0)])


def second_middle_kernel(
    every_column, head_ref, middle_in_ref, tail_ref, table_ref, mixing_ref, light_ref, inverse_ref, carry_ref, ratio_ref,
    middle_ref, sent_ref, xs_ref,
    acc_ref,
):
    read = second_reader(head_ref, middle_in_ref, tail_ref)
    for tile in range(BLOCKS):
        split_tile(read[0], tile * TILE, xs_ref, tile)
    own_blocks(every_column, MIDDLE_BLOCKS, read, table_ref, mixing_ref, light_ref, xs_ref, acc_ref, MIDDLE_PLACES)
    for group, place in MIDDLE_PLACES.items():
        solve(acc_ref, place, inverse_ref, carry_ref, ratio_ref, group, into_group(middle_ref, place))
        sent_rows(middle_ref, place, sent_ref, place)


def second_edge_kernel(every_column, head_ref, middle_ref, tail_ref, table_ref, mixing_ref, light_ref, xs_ref, edge_ref):
    read = second_reader(head_ref, middle_ref, tail_ref)
    own_blocks(every_column, EDGE_BLOCKS, read, table_ref, mixing_ref, light_ref, xs_ref, edge_ref, EDGE_PLACES)


def edge_kernel(
    first, every_column, left_ref, right_ref, table_ref, mixing_ref, edge_in_ref, inverse_ref, carry_ref, ratio_ref,
    *outs_and_scratch,
):
    head_ref, tail_ref, *sent, xs_ref, acc_ref = outs_and_scratch
    readers = []
    for side, ref in enumerate((left_ref, right_ref)):
        readers.append(natural_reader(ref) if first else group_reader([(ref, 0)]))
        for tile in range(HALO // TILE):
            split_tile(readers[side][0], tile * TILE, xs_ref, side * 2 + tile)
    uses = ((0, 0, (0, 1)), (1, 0, (1,)), (BLOCKS - 2, 1, (2,)), (BLOCKS - 1, 1, (2, 3)))
    offsets = (-HALO, -TILE, WIDTH, WIDTH + TILE)
    for block, side, places in uses:
        start = block * TILE
        total = moved_part(
            xs_ref,
            places,
            [offsets[place] - start for place in places],
            lambda k: table_row(every_column, table_ref, k, start),
            lambda seg, k: mixing_ref[seg, k, :, pl.ds(start, TILE)],
            readers[side][1],
            [(place % 2 * TILE + h, offsets[place] + h - start) for place in places for h in range(0, TILE, LANE)],
            by_lane(block),
        )
        for seg in range(SEGS):
            for tracer in range(TRACERS):
                value = total[seg * TRACERS + tracer]
                for h in range(TILE // LANE):
                    row = pl.ds(group_row(tracer, block % 2 * 2 + h, seg), LEV)
                    acc_ref[side, row, :] = edge_in_ref[side, row, :] + value[:, h * LANE : (h + 1) * LANE]
    for side, (group, ref) in enumerate(((0, head_ref), (GROUPS - 1, tail_ref))):
        solve(acc_ref, side, inverse_ref, carry_ref, ratio_ref, group, into_group(ref, 0))
        if sent:
            sent_rows(ref, 0, sent[0], side)


EDGE = shape(2, GROUP_ROWS, LANE)
MIDDLE = shape(GROUPS - 2, GROUP_ROWS, LANE)
SENT = shape(2, GROUP_ROWS // SEGS, LANE)
ONE = shape(1, GROUP_ROWS, LANE)


def call(kernel, name, flops, outs, scratch, *operands):
    return pl.pallas_call(
        kernel,
        out_shape=outs,
        in_specs=[VMEM] * len(operands),
        out_specs=jax.tree.map(lambda _: VMEM, outs),
        scratch_shapes=scratch,
        compiler_params=PARAMS,
        cost_estimate=pl.CostEstimate(flops=flops, bytes_accessed=4_000_000, transcendentals=0),
        name=name,
    )(*operands)


def first_own(every_column, state, table, mixing, light, kappa, wet):
    factors = shape(GROUPS, LEV, CHUNKS * SEGS, LANE)
    like = [jax.ShapeDtypeStruct(one.shape, one.dtype) for one in (table, mixing, light, wet)]
    return pl.pallas_call(
        functools.partial(first_own_kernel, every_column),
        out_shape=(EDGE, MIDDLE, factors, factors, factors, *like),
        in_specs=[VMEM] + [HBM] * 5,
        out_specs=(VMEM,) * 9,
        scratch_shapes=[
            pltpu.VMEM((BLOCKS, 2 * ROWS, TILE), bf16),
            pltpu.VMEM((GROUPS - 2, GROUP_ROWS, LANE), f32),
            pltpu.VMEM((GROUPS * CHUNKS * SEGS * LEV, LANE), f32),
            pltpu.VMEM((SEGS, LEV, WIDTH), f32),
            pltpu.SemaphoreType.DMA((4 + GROUPS,)),
        ],
        compiler_params=PARAMS,
        cost_estimate=pl.CostEstimate(flops=6_000_000_000, bytes_accessed=4_000_000, transcendentals=0),
        name="first_step_own",
    )(state, *[pltpu.with_memory_space_constraint(one, pltpu.HBM) for one in (table, mixing, light, kappa, wet)])


def second_middle(every_column, head, middle, tail, table, mixing, light, factors):
    return call(
        functools.partial(second_middle_kernel, every_column), "second_step_middle", 3_500_000_000,
        (MIDDLE, SENT, jax.ShapeDtypeStruct((BLOCKS, 2 * ROWS, TILE), bf16)),
        [pltpu.VMEM((GROUPS - 2, GROUP_ROWS, LANE), f32)],
        head, middle, tail, table, mixing, light, *factors,
    )


def second_edge(every_column, head, middle, tail, table, mixing, light, xs):
    return call(
        functools.partial(second_edge_kernel, every_column), "second_step_edges_own", 2_500_000_000, EDGE, [],
        head, middle, tail, table, mixing, light, xs,
    )


def edges(first, every_column, left, right, table, mixing, edge, factors):
    return call(
        functools.partial(edge_kernel, first, every_column),
        "first_step_edges" if first else "second_step_edges", 1_000_000_000,
        (ONE, ONE) if first else (ONE, ONE, SENT),
        [pltpu.VMEM((4, 2 * ROWS, TILE), bf16), pltpu.VMEM((2, GROUP_ROWS, LANE), f32)],
        left, right, table, mixing, edge, *factors,
    )


PAIRS = [(i, j) for i in range(BASIS) for j in range(i, BASIS)]


def residual_of(groups, segs, state_ref, wet_ref, basis_ref, before_of, write, sums, products):
    level = lax.broadcasted_iota(jnp.int32, (8, LANE), 0)
    for group in groups:
        for chunk in range(CHUNKS):
            lanes = pl.ds(group * HALO + chunk * LANE, LANE)
            wet = jnp.broadcast_to(wet_ref[pl.ds(group * CHUNKS + chunk, 1), :], (8, LANE))
            for seg in segs:
                for tracer in range(TRACERS):
                    for part in range(LEV // 8):
                        rows = pl.ds(part * 8, 8)
                        before = before_of(group, chunk, seg, tracer, part * 8)
                        own = state_ref[seg, tracer, rows, lanes]
                        here = jnp.where(wet > level + part * 8, own - before, 0.0)
                        write(group, chunk, seg, tracer, rows, here)
                        vectors = [basis_ref[i, seg, tracer, rows, lanes] for i in range(BASIS)]
                        for i in range(BASIS):
                            sums[i] = sums[i] + vectors[i] * here
                        sums[BASIS] = sums[BASIS] + here * here
                        if products:
                            for at, (i, j) in enumerate(PAIRS):
                                sums[BASIS + 1 + at] = sums[BASIS + 1 + at] + vectors[i] * vectors[j]


def early_kernel(
    state_ref, wet_ref, basis_ref, head_ref, middle_ref, tail_ref, came_ref, out_ref, residual_ref, sums_ref, sems
):
    refs = [(head_ref, 0)] + [(middle_ref, i) for i in range(GROUPS - 2)] + [(tail_ref, 0)]
    sums = [jnp.zeros((8, LANE), f32) for _ in range(BASIS + 1 + len(PAIRS))]

    def before_of(group, chunk, seg, tracer, level):
        if seg:
            ref, place = refs[group]
            return ref[place, pl.ds(group_row(tracer, chunk, seg - 1) + level, 8), :]
        return came_ref[group - 1, pl.ds((tracer * CHUNKS + chunk) * LEV + level, 8), :]

    def write(group, chunk, seg, tracer, rows, value):
        residual_ref[seg, tracer, rows, pl.ds(group * HALO + chunk * LANE, LANE)] = value

    residual_of(range(GROUPS), range(1, SEGS), state_ref, wet_ref, basis_ref, before_of, write, sums, True)
    parts = [(slice(1, SEGS),), (slice(0, 1), slice(None), slice(None), pl.ds(HALO, WIDTH - 2 * HALO))]
    copies = [pltpu.make_async_copy(residual_ref.at[part], out_ref.at[part], sems.at[i]) for i, part in enumerate(parts)]
    copies[0].start()
    residual_of(range(1, GROUPS - 1), (0,), state_ref, wet_ref, basis_ref, before_of, write, sums, True)
    copies[1].start()
    for group in (0, GROUPS - 1):
        for chunk in range(CHUNKS):
            lanes = pl.ds(group * HALO + chunk * LANE, LANE)
            for tracer in range(TRACERS):
                for part in range(LEV // 8):
                    vectors = [basis_ref[i, 0, tracer, pl.ds(part * 8, 8), lanes] for i in range(BASIS)]
                    for at, (i, j) in enumerate(PAIRS):
                        sums[BASIS + 1 + at] = sums[BASIS + 1 + at] + vectors[i] * vectors[j]
    for i, one in enumerate(sums):
        sums_ref[i] = one
    for copy in copies:
        copy.wait()


def late_kernel(
    state_ref, wet_ref, basis_ref, came_ref, early_ref, unused_ref, residual_ref, sums_ref, pieces_ref, sems
):
    sums = [early_ref[i] for i in range(BASIS + 1 + len(PAIRS))]

    def before_of(group, chunk, seg, tracer, level):
        return came_ref[EDGE_PLACES[group], pl.ds((tracer * CHUNKS + chunk) * LEV + level, 8), :]

    def write(group, chunk, seg, tracer, rows, value):
        pieces_ref[EDGE_PLACES[group], tracer, rows, pl.ds(chunk * LANE, LANE)] = value

    copies = []
    for group, place in EDGE_PLACES.items():
        residual_of((group,), (0,), state_ref, wet_ref, basis_ref, before_of, write, sums, False)
        copy = pltpu.make_async_copy(
            pieces_ref.at[place], residual_ref.at[0, :, :, pl.ds(group * HALO, HALO)], sems.at[place]
        )
        copy.start()
        copies.append(copy)
    lane = lax.broadcasted_iota(jnp.int32, (8, LANE), 1)
    row = jnp.zeros((8, LANE), f32)
    for i, one in enumerate(sums):
        row = jnp.where(lane == i, jnp.sum(jnp.sum(one, axis=0, keepdims=True), axis=1, keepdims=True), row)
    for i in range(sums_ref.shape[0] // 8):
        sums_ref[pl.ds(8 * i, 8), :] = row
    for copy in copies:
        copy.wait()


def early(state, wet, basis, head, middle, tail, came):
    whole = shape(SEGS, TRACERS, LEV, WIDTH)
    return pl.pallas_call(
        early_kernel,
        out_shape=(whole, whole, shape(BASIS + 1 + len(PAIRS), 8, LANE)),
        in_specs=[VMEM] * 7,
        out_specs=(HBM, VMEM, VMEM),
        scratch_shapes=[pltpu.SemaphoreType.DMA((2,))],
        compiler_params=PARAMS,
        cost_estimate=pl.CostEstimate(flops=10_000_000, bytes_accessed=4_000_000, transcendentals=0),
        name="residual_known",
    )(state, wet, basis, head, middle, tail, came)


def late(devices, state, wet, basis, came, sums, residual):
    return pl.pallas_call(
        late_kernel,
        out_shape=(shape(SEGS, TRACERS, LEV, WIDTH), shape(devices, LANE), shape(2, TRACERS, LEV, HALO)),
        in_specs=[VMEM] * 5 + [HBM],
        out_specs=(HBM, VMEM, VMEM),
        scratch_shapes=[pltpu.SemaphoreType.DMA((2,))],
        input_output_aliases={5: 0},
        compiler_params=PARAMS,
        cost_estimate=pl.CostEstimate(flops=3_000_000, bytes_accessed=4_000_000, transcendentals=0),
        name="residual_last",
    )(state, wet, basis, came, sums, residual)


def scaled_kernel(count, residual_ref, pieces_ref, basis_ref, sums_ref, new_out_ref, coefficients_ref, new_ref, sems):
    sums = jnp.sum(sums_ref[...], axis=0, keepdims=True)
    one = [sums[:, i : i + 1] for i in range(BASIS + 1 + len(PAIRS))]
    first, square, products = one[:BASIS], one[BASIS], iter(one[BASIS + 1 :])
    gram = [[None] * BASIS for _ in range(BASIS)]
    for i in range(BASIS):
        for j in range(i, BASIS):
            gram[i][j] = gram[j][i] = next(products)
    second = [first[i] - sum(gram[i][j] * first[j] for j in range(BASIS)) for i in range(BASIS)]
    both = [first[i] + second[i] for i in range(BASIS)]
    for i in range(BASIS):
        square = square - both[i] * (2.0 * first[i] - sum(gram[i][j] * both[j] for j in range(BASIS)))
    spread = jnp.sqrt(jnp.maximum(square, 0.0) / count + epsilon)
    lane = lax.broadcasted_iota(jnp.int32, (8, LANE), 1)
    result = jnp.zeros((8, LANE), f32)
    for i, value in enumerate(both + [spread]):
        result = jnp.where(lane == i, value, result)
    coefficients_ref[...] = result[0, : BASIS + 1]
    scale = 1.0 / spread
    weights = [jnp.broadcast_to(-value * scale, (LEV, LANE)) for value in both]
    scale = jnp.broadcast_to(scale, (LEV, LANE))
    copies = []
    for seg in range(SEGS):
        for tracer in range(TRACERS):
            for chunk in range(WIDTH // LANE):
                lanes = pl.ds(chunk * LANE, LANE)
                group = chunk // CHUNKS
                if seg == 0 and group in EDGE_PLACES:
                    here = pieces_ref[EDGE_PLACES[group], tracer, :, pl.ds(chunk % CHUNKS * LANE, LANE)]
                else:
                    here = residual_ref[seg, tracer, :, lanes]
                total = here * scale
                for i in range(BASIS):
                    total = total + weights[i] * basis_ref[i, seg, tracer, :, lanes]
                new_ref[seg, tracer, :, lanes] = total
            at = seg * TRACERS + tracer
            copy = pltpu.make_async_copy(new_ref.at[seg, tracer], new_out_ref.at[seg, tracer], sems.at[at])
            copy.start()
            copies.append(copy)
    for copy in copies:
        copy.wait()


def scaled(count, residual, pieces, basis, sums):
    whole = (SEGS, TRACERS, LEV, WIDTH)
    return pl.pallas_call(
        functools.partial(scaled_kernel, count),
        out_shape=(shape(*whole), shape(BASIS + 1)),
        in_specs=[VMEM] * 4,
        out_specs=(HBM, VMEM),
        scratch_shapes=[pltpu.VMEM(whole, f32), pltpu.SemaphoreType.DMA((SEGS * TRACERS,))],
        compiler_params=PARAMS,
        cost_estimate=pl.CostEstimate(flops=4_000_000, bytes_accessed=4_000_000, transcendentals=0),
        name="orthogonal_and_scaled",
    )(residual, pieces, basis, sums)


def shifted(block, axis, distance):
    count = lax.axis_size(axis)
    return lax.ppermute(block, axis, [(i, (i + distance) % count) for i in range(count)])


def per_device(segment_state, light, mixing, kappa, neighbour_columns, wet_levels, basis):
    every_column = lax.axis_size("col") * WIDTH
    state = pltpu.with_memory_space_constraint(segment_state, pltpu.VMEM)
    head, tail = halves(state)
    left = shifted(tail, "col", 1)
    right = shifted(head, "col", -1)
    table = neighbour_columns.T
    wet = wet_levels.reshape(WIDTH // LANE, LANE)
    edge, middle, *kept = first_own(every_column, state, table, mixing, light, kappa, wet)
    *factors, table, mixing, light, wet = kept
    head, tail = edges(True, every_column, left, right, table, mixing, edge, factors)
    left = shifted(tail, "col", 1)
    right = shifted(head, "col", -1)
    end_middle, sent, xs = second_middle(every_column, head, middle, tail, table, mixing, light, factors)
    came_middle = shifted(sent, "seg", 1)
    edge = second_edge(every_column, head, middle, tail, table, mixing, light, xs)
    head, tail, sent = edges(False, every_column, left, right, table, mixing, edge, factors)
    came_edge = shifted(sent, "seg", 1)
    residual, held, sums = early(state, wet, basis, head, end_middle, tail, came_middle)
    devices = lax.axis_size("seg") * lax.axis_size("col")
    residual, sums, pieces = late(devices, state, wet, basis, came_edge, sums, residual)
    sums = lax.all_to_all(sums, ("seg", "col"), 0, 0, tiled=True)
    count = lax.axis_size("seg") * SEGS * TRACERS * LEV * every_column
    new_vector, coefficients = scaled(count, held, pieces, basis, sums)
    return (residual, new_vector, coefficients)


def solution(mesh):
    return jax.shard_map(
        per_device,
        mesh=mesh,
        in_specs=(
            P("seg", None, None, "col"),
            P("seg", None, "col"),
            P("seg", None, None, "col"),
            P("seg", None, "col"),
            P("col", None),
            P("col"),
            P(None, "seg", None, None, "col"),
        ),
        out_specs=(P("seg", None, None, "col"), P("seg", None, None, "col"), P()),
        check_vma=False,
    )
```

```python
import functools

import jax
import jax.numpy as jnp
from jax import lax
from jax.experimental import pallas as pl
from jax.experimental.pallas import tpu as pltpu
from jax.sharding import PartitionSpec as P

uptake_rate = 0.6
half_saturation = 0.3
remin_rate = 0.2
dissolved_share = 0.7
epsilon = 1e-06

SEGS = 2
TRACERS = 2
LEV = 32
NBR = 6
BASIS = 4
WIDTH = 2048
HALO = 512
LANE = 128
TILE = 256
BLOCKS = WIDTH // TILE
GROUPS = WIDTH // HALO
CHUNKS = HALO // LANE
ROWS = SEGS * TRACERS * LEV
GROUP_ROWS = TRACERS * CHUNKS * SEGS * LEV
VMEM = pl.BlockSpec(memory_space=pltpu.VMEM)
PARAMS = pltpu.CompilerParams(vmem_limit_bytes=16 * 1024 * 1024)
ANY = pl.BlockSpec(memory_space=pl.ANY)
HBM = pl.BlockSpec(memory_space=pltpu.HBM)
f32 = jnp.float32
bf16 = jnp.bfloat16


def shape(*dims):
    return jax.ShapeDtypeStruct(dims, f32)


def group_row(tracer, chunk, seg):
    return ((tracer * CHUNKS + chunk) * SEGS + seg) * LEV


def natural_reader(ref):
    def read(seg, tracer, start):
        return ref[seg, tracer, :, pl.ds(start, TILE)]

    def one(seg, tracer, level, start):
        return ref[seg, tracer, pl.ds(level, 8), pl.ds(start, LANE)]

    return read, one


def group_reader(refs):
    def read(seg, tracer, start):
        ref, place = refs[start // HALO]
        chunk = start % HALO // LANE
        parts = [ref[place, pl.ds(group_row(tracer, chunk + h, seg), LEV), :] for h in range(TILE // LANE)]
        return jnp.concatenate(parts, axis=1)

    def one(seg, tracer, level, start):
        ref, place = refs[start // HALO]
        return ref[place, pl.ds(group_row(tracer, start % HALO // LANE, seg) + level, 8), :]

    return read, one


def split_tile(read, start, xs_ref, place):
    for seg in range(SEGS):
        for tracer in range(TRACERS):
            value = read(seg, tracer, start)
            high = value.astype(bf16)
            low = (value - high.astype(f32)).astype(bf16)
            row = (seg * TRACERS + tracer) * LEV
            xs_ref[place, pl.ds(row, LEV), :] = high
            xs_ref[place, pl.ds(ROWS + row, LEV), :] = low


def table_row(every_column, table_ref, k, start):
    columns = pl.ds(start, TILE)
    away = table_ref[pl.ds(k, 1), columns] - table_ref[pl.ds(0, 1), columns]
    away = jnp.where(away > HALO, away - every_column, away)
    away = jnp.where(away < -HALO, away + every_column, away)
    return away + lax.broadcasted_iota(jnp.int32, (1, TILE), 1)


def picked(xs_ref, places, offsets, index):
    total = None
    depth = lax.broadcasted_iota(jnp.int32, (TILE, TILE), 0)
    for place, offset in zip(places, offsets):
        chosen = jnp.where(depth == index - offset, f32(1), f32(0)).astype(bf16)
        part = jnp.dot(xs_ref[place], chosen, preferred_element_type=f32)
        total = part if total is None else total + part
    return total[:ROWS] + total[ROWS:]


def gathered(one, chunks, index):
    halves = []
    for h in range(TILE // LANE):
        at = jnp.broadcast_to(index[:, h * LANE : (h + 1) * LANE], (8, LANE))
        lane = at & (LANE - 1)
        usable = [(start, first) for start, first in chunks if abs(first - h * LANE) <= HALO]
        chosen = [at - lane == first for _, first in usable]
        rows = []
        for seg in range(SEGS):
            for tracer in range(TRACERS):
                for level in range(0, LEV, 8):
                    total = jnp.zeros((8, LANE), f32)
                    for (start, _), here in zip(usable, chosen):
                        value = jnp.take_along_axis(one(seg, tracer, level, start), lane, axis=1, mode="promise_in_bounds")
                        total = jnp.where(here, value, total)
                    rows.append(total)
        halves.append(jnp.concatenate(rows, axis=0))
    return jnp.concatenate(halves, axis=1)


def moved_part(xs_ref, places, offsets, index_of, mixing_of, one, chunks, by_lane):
    total = [None] * (SEGS * TRACERS)
    for k in range(1, NBR):
        index = index_of(k)
        value = gathered(one, chunks, index) if k in by_lane else picked(xs_ref, places, offsets, index)
        for seg in range(SEGS):
            mix = mixing_of(seg, k)
            for tracer in range(TRACERS):
                at = seg * TRACERS + tracer
                term = mix * value[at * LEV : (at + 1) * LEV]
                total[at] = term if total[at] is None else total[at] + term
    return total


def factorize(kappa_ref, wet_ref, by_rows_ref, inverse_ref, carry_ref, ratio_ref):
    for group in range(GROUPS):
        for chunk in range(CHUNKS):
            for seg in range(SEGS):
                lanes = pl.ds(group * HALO + chunk * LANE, LANE)
                row = (group * CHUNKS * SEGS + chunk * SEGS + seg) * LEV
                by_rows_ref[pl.ds(row, LEV), :] = kappa_ref[seg, :, lanes]
    wet = []
    for group in range(GROUPS):
        rows = []
        for chunk in range(CHUNKS):
            one = wet_ref[pl.ds(group * CHUNKS + chunk, 1), :]
            rows += [one] * SEGS
        wet.append(jnp.concatenate(rows, axis=0))
    zero = jnp.zeros((CHUNKS * SEGS, LANE), f32)

    def upper_at(group, level):
        if level == 0 or level == LEV:
            return zero
        rows = pl.ds(group * CHUNKS * SEGS * LEV + level, CHUNKS * SEGS, stride=LEV)
        return jnp.where(wet[group] > level, by_rows_ref[rows, :], 0.0)

    upper = [upper_at(group, 0) for group in range(GROUPS)]
    ratio = [zero] * GROUPS
    for level in range(LEV):
        for group in range(GROUPS):
            lower = upper_at(group, level + 1)
            pivot = (1.0 + upper[group] + lower) + upper[group] * ratio[group]
            inverse = 1.0 / pivot
            ratio[group] = -lower * inverse
            inverse_ref[group, level] = jnp.where(wet[group] > level, inverse, 0.0)
            carry_ref[group, level] = upper[group] * inverse
            ratio_ref[group, level] = ratio[group]
            upper[group] = lower


def solve(source_ref, place, inverse_ref, carry_ref, ratio_ref, group, out):
    step = CHUNKS * SEGS

    def source(tracer, level):
        return source_ref[place, pl.ds(group_row(tracer, 0, 0) + level, step, stride=LEV), :]

    value = [[None] * LEV for _ in range(TRACERS)]
    for level in range(LEV):
        inverse = inverse_ref[group, level]
        carry = carry_ref[group, level]
        for tracer in range(TRACERS):
            here = source(tracer, level) * inverse
            if level:
                here = here + carry * value[tracer][level - 1]
            value[tracer][level] = here
    for level in range(LEV - 1, -1, -1):
        ratio = ratio_ref[group, level]
        for tracer in range(TRACERS):
            if level < LEV - 1:
                value[tracer][level] = value[tracer][level] - ratio * value[tracer][level + 1]
            out(tracer, level, value[tracer][level])


def into_group(ref, place):
    def write(tracer, level, value):
        ref[place, pl.ds(group_row(tracer, 0, 0) + level, CHUNKS * SEGS, stride=LEV), :] = value

    return write


def own_blocks(every_column, blocks, readers, table_ref, mixing_ref, light_ref, xs_ref, acc_ref, places):
    read, one = readers
    for block in blocks:
        start = block * TILE
        tiles = list(range(max(0, block - 2), min(BLOCKS, block + 3)))
        total = moved_part(
            xs_ref,
            tiles,
            [tile * TILE - start for tile in tiles],
            lambda k: table_row(every_column, table_ref, k, start),
            lambda seg, k: mixing_ref[seg, k, :, pl.ds(start, TILE)],
            one,
            [(tile * TILE + h, tile * TILE + h - start) for tile in tiles for h in range(0, TILE, LANE)],
            by_lane(block),
        )
        for seg in range(SEGS):
            columns = pl.ds(start, TILE)
            phosphate = read(seg, 0, start)
            organic = read(seg, 1, start)
            squared = phosphate * phosphate
            uptake = uptake_rate * light_ref[seg, :, columns] * squared / (squared + half_saturation)
            gains = (remin_rate * organic - uptake, dissolved_share * uptake - remin_rate * organic)
            own = mixing_ref[seg, 0, :, columns]
            for tracer, value in enumerate((phosphate, organic)):
                result = own * value + total[seg * TRACERS + tracer] + gains[tracer]
                for h in range(TILE // LANE):
                    row = group_row(tracer, block % 2 * 2 + h, seg)
                    acc_ref[places[block // 2], pl.ds(row, LEV), :] = result[:, h * LANE : (h + 1) * LANE]


def by_lane(block):
    return (4, 5) if block % 2 else (5,)


EDGE_BLOCKS = (0, 1, BLOCKS - 2, BLOCKS - 1)
MIDDLE_BLOCKS = tuple(range(2, BLOCKS - 2))
EDGE_PLACES = {0: 0, GROUPS - 1: 1}
MIDDLE_PLACES = {group: group - 1 for group in range(1, GROUPS - 1)}


def sent_rows(from_ref, place, to_ref, to_place):
    for tracer in range(TRACERS):
        for chunk in range(CHUNKS):
            to_ref[to_place, pl.ds((tracer * CHUNKS + chunk) * LEV, LEV), :] = from_ref[
                place, pl.ds(group_row(tracer, chunk, SEGS - 1), LEV), :
            ]


QUARTER = (slice(None), slice(None), slice(None), pl.ds(0, HALO))


def halves_kernel(
    state_in, table_in, light_in, mixing_in,
    head_ref, tail_ref, state_ref, table_ref, light_ref, mixing_ref,
    sems,
):
    pairs = [(state_in, state_ref), (table_in, table_ref), (light_in, light_ref), (mixing_in.at[QUARTER], mixing_ref)]
    copies = [pltpu.make_async_copy(*pair, sems.at[i]) for i, pair in enumerate(pairs)]
    for copy in copies:
        copy.start()
    copies[0].wait()
    head_ref[...] = state_ref[:, :, :, :HALO]
    tail_ref[...] = state_ref[:, :, :, WIDTH - HALO :]
    for copy in copies[1:]:
        copy.wait()


def in_hbm(*arrays):
    return [pltpu.with_memory_space_constraint(one, pltpu.HBM) for one in arrays]


def halves(state, table, light, mixing):
    half = shape(SEGS, TRACERS, LEV, HALO)
    like = [jax.ShapeDtypeStruct(one.shape, one.dtype) for one in (state, table, light)]
    return pl.pallas_call(
        halves_kernel,
        out_shape=(half, half, *like, shape(SEGS, NBR, LEV, HALO)),
        in_specs=[HBM] * 4,
        out_specs=(VMEM,) * 6,
        scratch_shapes=[pltpu.SemaphoreType.DMA((4,))],
        compiler_params=PARAMS,
        cost_estimate=pl.CostEstimate(flops=0, bytes_accessed=4_000_000, transcendentals=0),
        name="edge_columns",
    )(*in_hbm(state, table, light, mixing))


def first_own_kernel(
    every_column, state_ref, table_ref, light_ref, quarter_ref, mixing_in, kappa_in, wet_in,
    edge_ref, middle_ref, inverse_ref, carry_ref, ratio_ref, mixing_ref, wet_ref,
    xs_ref, acc_ref, by_rows_ref, kappa_ref, sems,
):
    order = (GROUPS - 1,) + tuple(range(1, GROUPS - 1)) + (0,)
    parts = [(slice(None),) * 3 + (pl.ds(group * HALO, HALO),) for group in order]
    pairs = [(kappa_in, kappa_ref), (wet_in, wet_ref)] + [(mixing_in.at[part], mixing_ref.at[part]) for part in parts]
    copies = [pltpu.make_async_copy(*pair, sems.at[i]) for i, pair in enumerate(pairs)]
    for copy in copies:
        copy.start()
    read = natural_reader(state_ref)
    for tile in range(BLOCKS):
        split_tile(read[0], tile * TILE, xs_ref, tile)
    own_blocks(every_column, EDGE_BLOCKS[:2], read, table_ref, quarter_ref, light_ref, xs_ref, edge_ref, EDGE_PLACES)
    for copy in copies:
        copy.wait()
    factorize(kappa_ref, wet_ref, by_rows_ref, inverse_ref, carry_ref, ratio_ref)
    own_blocks(every_column, EDGE_BLOCKS[2:], read, table_ref, mixing_ref, light_ref, xs_ref, edge_ref, EDGE_PLACES)
    own_blocks(every_column, MIDDLE_BLOCKS, read, table_ref, mixing_ref, light_ref, xs_ref, acc_ref, MIDDLE_PLACES)
    for group, place in MIDDLE_PLACES.items():
        solve(acc_ref, place, inverse_ref, carry_ref, ratio_ref, group, into_group(middle_ref, place))


def second_reader(head_ref, middle_ref, tail_ref):
    return group_reader([(head_ref, 0)] + [(middle_ref, i) for i in range(GROUPS - 2)] + [(tail_ref, 0)])


def second_middle_kernel(
    every_column, head_ref, middle_in_ref, tail_ref, table_ref, mixing_ref, light_ref, inverse_ref, carry_ref, ratio_ref,
    middle_ref, sent_ref, xs_ref,
    acc_ref,
):
    read = second_reader(head_ref, middle_in_ref, tail_ref)
    for tile in range(BLOCKS):
        split_tile(read[0], tile * TILE, xs_ref, tile)
    own_blocks(every_column, MIDDLE_BLOCKS, read, table_ref, mixing_ref, light_ref, xs_ref, acc_ref, MIDDLE_PLACES)
    for group, place in MIDDLE_PLACES.items():
        solve(acc_ref, place, inverse_ref, carry_ref, ratio_ref, group, into_group(middle_ref, place))
        sent_rows(middle_ref, place, sent_ref, place)


def second_edge_kernel(every_column, head_ref, middle_ref, tail_ref, table_ref, mixing_ref, light_ref, xs_ref, edge_ref):
    read = second_reader(head_ref, middle_ref, tail_ref)
    own_blocks(every_column, EDGE_BLOCKS, read, table_ref, mixing_ref, light_ref, xs_ref, edge_ref, EDGE_PLACES)


def edge_kernel(
    first, every_column, left_ref, right_ref, table_ref, mixing_ref, edge_in_ref, inverse_ref, carry_ref, ratio_ref,
    *outs_and_scratch,
):
    head_ref, tail_ref, *sent, xs_ref, acc_ref = outs_and_scratch
    readers = []
    for side, ref in enumerate((left_ref, right_ref)):
        readers.append(natural_reader(ref) if first else group_reader([(ref, 0)]))
        for tile in range(HALO // TILE):
            split_tile(readers[side][0], tile * TILE, xs_ref, side * 2 + tile)
    uses = ((0, 0, (0, 1)), (1, 0, (1,)), (BLOCKS - 2, 1, (2,)), (BLOCKS - 1, 1, (2, 3)))
    offsets = (-HALO, -TILE, WIDTH, WIDTH + TILE)
    for block, side, places in uses:
        start = block * TILE
        total = moved_part(
            xs_ref,
            places,
            [offsets[place] - start for place in places],
            lambda k: table_row(every_column, table_ref, k, start),
            lambda seg, k: mixing_ref[seg, k, :, pl.ds(start, TILE)],
            readers[side][1],
            [(place % 2 * TILE + h, offsets[place] + h - start) for place in places for h in range(0, TILE, LANE)],
            by_lane(block),
        )
        for seg in range(SEGS):
            for tracer in range(TRACERS):
                value = total[seg * TRACERS + tracer]
                for h in range(TILE // LANE):
                    row = pl.ds(group_row(tracer, block % 2 * 2 + h, seg), LEV)
                    acc_ref[side, row, :] = edge_in_ref[side, row, :] + value[:, h * LANE : (h + 1) * LANE]
    for side, (group, ref) in enumerate(((0, head_ref), (GROUPS - 1, tail_ref))):
        solve(acc_ref, side, inverse_ref, carry_ref, ratio_ref, group, into_group(ref, 0))
        if sent:
            sent_rows(ref, 0, sent[0], side)


EDGE = shape(2, GROUP_ROWS, LANE)
MIDDLE = shape(GROUPS - 2, GROUP_ROWS, LANE)
SENT = shape(2, GROUP_ROWS // SEGS, LANE)
ONE = shape(1, GROUP_ROWS, LANE)


def call(kernel, name, flops, outs, scratch, *operands):
    return pl.pallas_call(
        kernel,
        out_shape=outs,
        in_specs=[VMEM] * len(operands),
        out_specs=jax.tree.map(lambda _: VMEM, outs),
        scratch_shapes=scratch,
        compiler_params=PARAMS,
        cost_estimate=pl.CostEstimate(flops=flops, bytes_accessed=4_000_000, transcendentals=0),
        name=name,
    )(*operands)


def first_own(every_column, state, table, light, quarter, mixing, kappa, wet):
    factors = shape(GROUPS, LEV, CHUNKS * SEGS, LANE)
    like = [jax.ShapeDtypeStruct(one.shape, one.dtype) for one in (mixing, wet)]
    return pl.pallas_call(
        functools.partial(first_own_kernel, every_column),
        out_shape=(EDGE, MIDDLE, factors, factors, factors, *like),
        in_specs=[VMEM] * 4 + [HBM] * 3,
        out_specs=(VMEM,) * 7,
        scratch_shapes=[
            pltpu.VMEM((BLOCKS, 2 * ROWS, TILE), bf16),
            pltpu.VMEM((GROUPS - 2, GROUP_ROWS, LANE), f32),
            pltpu.VMEM((GROUPS * CHUNKS * SEGS * LEV, LANE), f32),
            pltpu.VMEM((SEGS, LEV, WIDTH), f32),
            pltpu.SemaphoreType.DMA((2 + GROUPS,)),
        ],
        compiler_params=PARAMS,
        cost_estimate=pl.CostEstimate(flops=6_000_000_000, bytes_accessed=4_000_000, transcendentals=0),
        name="first_step_own",
    )(state, table, light, quarter, *in_hbm(mixing, kappa, wet))


def second_middle(every_column, head, middle, tail, table, mixing, light, factors):
    return call(
        functools.partial(second_middle_kernel, every_column), "second_step_middle", 3_500_000_000,
        (MIDDLE, SENT, jax.ShapeDtypeStruct((BLOCKS, 2 * ROWS, TILE), bf16)),
        [pltpu.VMEM((GROUPS - 2, GROUP_ROWS, LANE), f32)],
        head, middle, tail, table, mixing, light, *factors,
    )


def second_edge(every_column, head, middle, tail, table, mixing, light, xs):
    return call(
        functools.partial(second_edge_kernel, every_column), "second_step_edges_own", 2_500_000_000, EDGE, [],
        head, middle, tail, table, mixing, light, xs,
    )


def edges(first, every_column, left, right, table, mixing, edge, factors):
    return call(
        functools.partial(edge_kernel, first, every_column),
        "first_step_edges" if first else "second_step_edges", 1_000_000_000,
        (ONE, ONE) if first else (ONE, ONE, SENT),
        [pltpu.VMEM((4, 2 * ROWS, TILE), bf16), pltpu.VMEM((2, GROUP_ROWS, LANE), f32)],
        left, right, table, mixing, edge, *factors,
    )


PAIRS = [(i, j) for i in range(BASIS) for j in range(i, BASIS)]
SUMS = BASIS + 1 + len(PAIRS)
KNOWN = ((range(GROUPS), range(1, SEGS)), (range(1, GROUPS - 1), (0,)))
UNKNOWN = (((0, GROUPS - 1), (0,)),)


def pieces_of(areas):
    for groups, segs in areas:
        for group in groups:
            for chunk in range(CHUNKS):
                lanes = pl.ds(group * HALO + chunk * LANE, LANE)
                for seg in segs:
                    for tracer in range(TRACERS):
                        for level in range(0, LEV, 8):
                            yield group, chunk, seg, tracer, level, pl.ds(level, 8), lanes


def residual_at(place, state_ref, wet_ref, before):
    group, chunk, seg, tracer, level, rows, lanes = place
    wet = jnp.broadcast_to(wet_ref[pl.ds(group * CHUNKS + chunk, 1), :], (8, LANE))
    here = wet > lax.broadcasted_iota(jnp.int32, (8, LANE), 0) + level
    return jnp.where(here, state_ref[seg, tracer, rows, lanes] - before, 0.0)


def basis_at(place, basis_ref):
    _, _, seg, tracer, _, rows, lanes = place
    return [basis_ref[i, seg, tracer, rows, lanes] for i in range(BASIS)]


def add_products(sums, vectors):
    for at, (i, j) in enumerate(PAIRS):
        sums[at] = sums[at] + vectors[i] * vectors[j]


def add_rest(sums, vectors, value, guess):
    for i in range(BASIS):
        value = value - guess[i] * vectors[i]
    for i in range(BASIS):
        sums[i] = sums[i] + vectors[i] * value
    sums[BASIS] = sums[BASIS] + value * value


def symmetric(values):
    matrix = [[None] * BASIS for _ in range(BASIS)]
    for (i, j), value in zip(PAIRS, values):
        matrix[i][j] = matrix[j][i] = value
    return matrix


def whole_sum(value):
    return jnp.sum(jnp.sum(value, axis=0, keepdims=True), axis=1, keepdims=True)


def least_squares(products, right):
    gram = symmetric(products)
    factor = [[None] * BASIS for _ in range(BASIS)]
    pivots, inverses, weights = [], [], []
    for i in range(BASIS):
        for j in range(i):
            value = gram[i][j]
            for k in range(j):
                value = value - factor[i][k] * pivots[k] * factor[j][k]
            factor[i][j] = value * inverses[j]
        pivot = gram[i][i]
        for k in range(i):
            pivot = pivot - factor[i][k] * factor[i][k] * pivots[k]
        usable = (pivot > 1e-3 * gram[i][i]) & (pivot > 1e-30)
        pivots.append(pivot)
        inverses.append(jnp.where(usable, 1.0 / jnp.where(usable, pivot, 1.0), 0.0))
        value = right[i]
        for k in range(i):
            value = value - factor[i][k] * weights[k]
        weights.append(value)
    for i in range(BASIS - 1, -1, -1):
        value = weights[i] * inverses[i]
        for k in range(i + 1, BASIS):
            value = value - factor[k][i] * weights[k]
        weights[i] = value
    return weights


def early_kernel(
    state_ref, wet_ref, basis_ref, head_ref, middle_ref, tail_ref, came_ref,
    out_ref, residual_ref, sums_ref, guess_ref, sems,
):
    refs = [(head_ref, 0)] + [(middle_ref, i) for i in range(GROUPS - 2)] + [(tail_ref, 0)]
    zero = jnp.zeros((8, LANE), f32)
    first = [zero] * BASIS
    products = [zero] * len(PAIRS)
    for place in pieces_of(KNOWN):
        group, chunk, seg, tracer, level, rows, lanes = place
        if seg:
            ref, at = refs[group]
            before = ref[at, pl.ds(group_row(tracer, chunk, seg - 1) + level, 8), :]
        else:
            before = came_ref[group - 1, pl.ds((tracer * CHUNKS + chunk) * LEV + level, 8), :]
        value = residual_at(place, state_ref, wet_ref, before)
        residual_ref[seg, tracer, rows, lanes] = value
        vectors = basis_at(place, basis_ref)
        for i in range(BASIS):
            first[i] = first[i] + vectors[i] * value
        add_products(products, vectors)
    parts = [(slice(1, SEGS),), (slice(0, 1), slice(None), slice(None), pl.ds(HALO, WIDTH - 2 * HALO))]
    copies = [pltpu.make_async_copy(residual_ref.at[part], out_ref.at[part], sems.at[i]) for i, part in enumerate(parts)]
    for copy in copies:
        copy.start()
    weights = least_squares([whole_sum(one) for one in products], [whole_sum(one) for one in first])
    guess = [jnp.broadcast_to(weight, (8, LANE)) for weight in weights]
    sums = [zero] * (BASIS + 1)
    for place in pieces_of(KNOWN):
        _, _, seg, tracer, _, rows, lanes = place
        add_rest(sums, basis_at(place, basis_ref), residual_ref[seg, tracer, rows, lanes], guess)
    for place in pieces_of(UNKNOWN):
        add_products(products, basis_at(place, basis_ref))
    for i, one in enumerate(sums + products):
        sums_ref[i] = one
    for i, one in enumerate(guess):
        guess_ref[i] = one
    for copy in copies:
        copy.wait()


def late_kernel(state_ref, wet_ref, basis_ref, came_ref, early_ref, guess_ref, pieces_ref, sums_ref):
    guess = [guess_ref[i] for i in range(BASIS)]
    sums = [early_ref[i] for i in range(SUMS)]
    for place in pieces_of(UNKNOWN):
        group, chunk, seg, tracer, level, rows, lanes = place
        before = came_ref[EDGE_PLACES[group], pl.ds((tracer * CHUNKS + chunk) * LEV + level, 8), :]
        value = residual_at(place, state_ref, wet_ref, before)
        pieces_ref[EDGE_PLACES[group], tracer, rows, pl.ds(chunk * LANE, LANE)] = value
        add_rest(sums, basis_at(place, basis_ref), value, guess)
    lane = lax.broadcasted_iota(jnp.int32, (8, LANE), 1)
    row = jnp.zeros((8, LANE), f32)
    for i, one in enumerate([whole_sum(one) for one in sums] + guess):
        row = jnp.where(lane == i, one, row)
    for i in range(sums_ref.shape[0] // 8):
        sums_ref[pl.ds(8 * i, 8), :] = row


def early(state, wet, basis, head, middle, tail, came):
    whole = shape(SEGS, TRACERS, LEV, WIDTH)
    return pl.pallas_call(
        early_kernel,
        out_shape=(whole, whole, shape(SUMS, 8, LANE), shape(BASIS, 8, LANE)),
        in_specs=[VMEM] * 7,
        out_specs=(HBM, VMEM, VMEM, VMEM),
        scratch_shapes=[pltpu.SemaphoreType.DMA((2,))],
        compiler_params=PARAMS,
        cost_estimate=pl.CostEstimate(flops=10_000_000, bytes_accessed=4_000_000, transcendentals=0),
        name="residual_known",
    )(state, wet, basis, head, middle, tail, came)


def late(devices, state, wet, basis, came, sums, guess):
    return call(
        late_kernel, "residual_last", 3_000_000, (shape(2, TRACERS, LEV, HALO), shape(devices, LANE)), [],
        state, wet, basis, came, sums, guess,
    )


def scaled_kernel(
    count, residual_ref, pieces_ref, basis_ref, sums_ref, unused_ref,
    out_ref, new_out_ref, coefficients_ref, new_ref, sems,
):
    copies = []

    def send(from_ref, to_ref):
        copies.append(pltpu.make_async_copy(from_ref, to_ref, sems.at[len(copies)]))
        copies[-1].start()

    for group, place in EDGE_PLACES.items():
        send(pieces_ref.at[place], out_ref.at[0, :, :, pl.ds(group * HALO, HALO)])
    sums = sums_ref[...]
    if sums.shape[0] < LANE:
        sums = jnp.concatenate([sums, jnp.zeros((LANE - sums.shape[0], LANE), f32)], axis=0)
    sums = sums.T
    row = [sums[i : i + 1] for i in range(SUMS + BASIS)]
    of_rest, squares, products, guess = row[:BASIS], row[BASIS], row[BASIS + 1 : SUMS], row[SUMS:]
    gram = symmetric(products)
    first = [of_rest[i] + sum(gram[i][j] * guess[j] for j in range(BASIS)) for i in range(BASIS)]
    totals = jnp.concatenate(first + products + [jnp.zeros((2, LANE), f32)], axis=0)
    totals = jnp.sum(totals, axis=1, keepdims=True)
    one = [totals[i : i + 1] for i in range(SUMS)]
    first, products = one[:BASIS], one[BASIS : SUMS - 1]
    whole_gram = symmetric(products)
    second = [first[i] - sum(whole_gram[i][j] * first[j] for j in range(BASIS)) for i in range(BASIS)]
    both = [first[i] + second[i] for i in range(BASIS)]
    away = [both[i] - guess[i] for i in range(BASIS)]
    for i in range(BASIS):
        squares = squares + away[i] * (sum(gram[i][j] * away[j] for j in range(BASIS)) - 2.0 * of_rest[i])
    square = jnp.maximum(jnp.sum(squares, axis=1, keepdims=True), 0.0)
    spread = jnp.sqrt(square / count + epsilon)
    lane = lax.broadcasted_iota(jnp.int32, (8, LANE), 1)
    result = jnp.zeros((8, LANE), f32)
    for i, value in enumerate(both + [spread]):
        result = jnp.where(lane == i, value, result)
    coefficients_ref[...] = result[0, : BASIS + 1]
    scale = 1.0 / spread
    weights = [jnp.broadcast_to(-value * scale, (LEV, LANE)) for value in both]
    scale = jnp.broadcast_to(scale, (LEV, LANE))
    for seg in range(SEGS):
        for tracer in range(TRACERS):
            for chunk in range(WIDTH // LANE):
                lanes = pl.ds(chunk * LANE, LANE)
                group = chunk // CHUNKS
                if seg == 0 and group in EDGE_PLACES:
                    here = pieces_ref[EDGE_PLACES[group], tracer, :, pl.ds(chunk % CHUNKS * LANE, LANE)]
                else:
                    here = residual_ref[seg, tracer, :, lanes]
                total = here * scale
                for i in range(BASIS):
                    total = total + weights[i] * basis_ref[i, seg, tracer, :, lanes]
                new_ref[seg, tracer, :, lanes] = total
            send(new_ref.at[seg, tracer], new_out_ref.at[seg, tracer])
    for copy in copies:
        copy.wait()


def scaled(count, residual, pieces, basis, sums, out):
    whole = (SEGS, TRACERS, LEV, WIDTH)
    return pl.pallas_call(
        functools.partial(scaled_kernel, count),
        out_shape=(shape(*whole), shape(*whole), shape(BASIS + 1)),
        in_specs=[VMEM] * 4 + [HBM],
        out_specs=(HBM, HBM, VMEM),
        scratch_shapes=[pltpu.VMEM(whole, f32), pltpu.SemaphoreType.DMA((2 + SEGS * TRACERS,))],
        input_output_aliases={4: 0},
        compiler_params=PARAMS,
        cost_estimate=pl.CostEstimate(flops=4_000_000, bytes_accessed=4_000_000, transcendentals=0),
        name="orthogonal_and_scaled",
    )(residual, pieces, basis, sums, out)


def shifted(block, axis, distance):
    count = lax.axis_size(axis)
    return lax.ppermute(block, axis, [(i, (i + distance) % count) for i in range(count)])


def per_device(segment_state, light, mixing, kappa, neighbour_columns, wet_levels, basis):
    every_column = lax.axis_size("col") * WIDTH
    table = neighbour_columns.T
    wet = wet_levels.reshape(WIDTH // LANE, LANE)
    head, tail, state, table, light, quarter = halves(segment_state, table, light, mixing)
    left = shifted(tail, "col", 1)
    right = shifted(head, "col", -1)
    edge, middle, *factors, mixing, wet = first_own(every_column, state, table, light, quarter, mixing, kappa, wet)
    head, tail = edges(True, every_column, left, right, table, mixing, edge, factors)
    left = shifted(tail, "col", 1)
    right = shifted(head, "col", -1)
    end_middle, sent, xs = second_middle(every_column, head, middle, tail, table, mixing, light, factors)
    came_middle = shifted(sent, "seg", 1)
    edge = second_edge(every_column, head, middle, tail, table, mixing, light, xs)
    head, tail, sent = edges(False, every_column, left, right, table, mixing, edge, factors)
    came_edge = shifted(sent, "seg", 1)
    residual, held, sums, guess = early(state, wet, basis, head, end_middle, tail, came_middle)
    devices = lax.axis_size("seg") * lax.axis_size("col")
    pieces, sums = late(devices, state, wet, basis, came_edge, sums, guess)
    sums = lax.all_to_all(sums, ("seg", "col"), 0, 0, tiled=True)
    count = lax.axis_size("seg") * SEGS * TRACERS * LEV * every_column
    return scaled(count, held, pieces, basis, sums, residual)


def solution(mesh):
    return jax.shard_map(
        per_device,
        mesh=mesh,
        in_specs=(
            P("seg", None, None, "col"),
            P("seg", None, "col"),
            P("seg", None, None, "col"),
            P("seg", None, "col"),
            P("col", None),
            P("col"),
            P(None, "seg", None, None, "col"),
        ),
        out_specs=(P("seg", None, None, "col"), P("seg", None, None, "col"), P()),
        check_vma=False,
    )
```

```python
import functools

import jax
import jax.numpy as jnp
from jax import lax
from jax.experimental import pallas as pl
from jax.experimental.pallas import tpu as pltpu
from jax.sharding import PartitionSpec as P

uptake_rate = 0.6
half_saturation = 0.3
remin_rate = 0.2
dissolved_share = 0.7
epsilon = 1e-06

SEGS = 2
TRACERS = 2
LEV = 32
NBR = 6
BASIS = 4
WIDTH = 2048
HALO = 512
LANE = 128
TILE = 256
BLOCKS = WIDTH // TILE
GROUPS = WIDTH // HALO
CHUNKS = HALO // LANE
ROWS = SEGS * TRACERS * LEV
GROUP_ROWS = TRACERS * CHUNKS * SEGS * LEV
VMEM = pl.BlockSpec(memory_space=pltpu.VMEM)
PARAMS = pltpu.CompilerParams(vmem_limit_bytes=16 * 1024 * 1024)
ANY = pl.BlockSpec(memory_space=pl.ANY)
HBM = pl.BlockSpec(memory_space=pltpu.HBM)
f32 = jnp.float32
bf16 = jnp.bfloat16


def shape(*dims):
    return jax.ShapeDtypeStruct(dims, f32)


def group_row(tracer, chunk, seg):
    return ((tracer * CHUNKS + chunk) * SEGS + seg) * LEV


def natural_reader(ref):
    def read(seg, tracer, start):
        return ref[seg, tracer, :, pl.ds(start, TILE)]

    def one(seg, tracer, level, start):
        return ref[seg, tracer, pl.ds(level, 8), pl.ds(start, LANE)]

    return read, one


def group_reader(refs):
    def read(seg, tracer, start):
        ref, place = refs[start // HALO]
        chunk = start % HALO // LANE
        parts = [ref[place, pl.ds(group_row(tracer, chunk + h, seg), LEV), :] for h in range(TILE // LANE)]
        return jnp.concatenate(parts, axis=1)

    def one(seg, tracer, level, start):
        ref, place = refs[start // HALO]
        return ref[place, pl.ds(group_row(tracer, start % HALO // LANE, seg) + level, 8), :]

    return read, one


def split_tile(read, start, xs_ref, place):
    for seg in range(SEGS):
        for tracer in range(TRACERS):
            value = read(seg, tracer, start)
            high = value.astype(bf16)
            low = (value - high.astype(f32)).astype(bf16)
            row = (seg * TRACERS + tracer) * LEV
            xs_ref[place, pl.ds(row, LEV), :] = high
            xs_ref[place, pl.ds(ROWS + row, LEV), :] = low


def table_row(every_column, table_ref, k, start):
    columns = pl.ds(start, TILE)
    away = table_ref[pl.ds(k, 1), columns] - table_ref[pl.ds(0, 1), columns]
    away = jnp.where(away > HALO, away - every_column, away)
    away = jnp.where(away < -HALO, away + every_column, away)
    return away + lax.broadcasted_iota(jnp.int32, (1, TILE), 1)


def picked(xs_ref, places, offsets, index):
    total = None
    depth = lax.broadcasted_iota(jnp.int16, (TILE, TILE), 0)
    for place, offset in zip(places, offsets):
        wanted = jnp.broadcast_to(index - offset, (16, TILE)).astype(jnp.int16)
        wanted = jnp.concatenate([wanted] * (TILE // 16), axis=0)
        chosen = jnp.where(depth == wanted, bf16(1), bf16(0))
        part = jnp.dot(xs_ref[place], chosen, preferred_element_type=f32)
        total = part if total is None else total + part
    return total[:ROWS] + total[ROWS:]


def gathered(one, chunks, index):
    halves = []
    for h in range(TILE // LANE):
        at = jnp.broadcast_to(index[:, h * LANE : (h + 1) * LANE], (8, LANE))
        lane = at & (LANE - 1)
        usable = [(start, first) for start, first in chunks if abs(first - h * LANE) <= HALO]
        chosen = [at - lane == first for _, first in usable]
        rows = []
        for seg in range(SEGS):
            for tracer in range(TRACERS):
                for level in range(0, LEV, 8):
                    total = jnp.zeros((8, LANE), f32)
                    for (start, _), here in zip(usable, chosen):
                        value = jnp.take_along_axis(one(seg, tracer, level, start), lane, axis=1, mode="promise_in_bounds")
                        total = jnp.where(here, value, total)
                    rows.append(total)
        halves.append(jnp.concatenate(rows, axis=0))
    return jnp.concatenate(halves, axis=1)


def moved_part(xs_ref, places, offsets, index_of, mixing_of, one, chunks, by_lane):
    total = [None] * (SEGS * TRACERS)
    for k in range(1, NBR):
        index = index_of(k)
        value = gathered(one, chunks, index) if k in by_lane else picked(xs_ref, places, offsets, index)
        for seg in range(SEGS):
            mix = mixing_of(seg, k)
            for tracer in range(TRACERS):
                at = seg * TRACERS + tracer
                term = mix * value[at * LEV : (at + 1) * LEV]
                total[at] = term if total[at] is None else total[at] + term
    return total


def factorize(kappa_ref, wet_ref, by_rows_ref, inverse_ref, carry_ref, ratio_ref):
    for group in range(GROUPS):
        for chunk in range(CHUNKS):
            for seg in range(SEGS):
                lanes = pl.ds(group * HALO + chunk * LANE, LANE)
                row = (group * CHUNKS * SEGS + chunk * SEGS + seg) * LEV
                by_rows_ref[pl.ds(row, LEV), :] = kappa_ref[seg, :, lanes]
    wet = []
    for group in range(GROUPS):
        rows = []
        for chunk in range(CHUNKS):
            one = wet_ref[pl.ds(group * CHUNKS + chunk, 1), :]
            rows += [one] * SEGS
        wet.append(jnp.concatenate(rows, axis=0))
    zero = jnp.zeros((CHUNKS * SEGS, LANE), f32)

    def upper_at(group, level):
        if level == 0 or level == LEV:
            return zero
        rows = pl.ds(group * CHUNKS * SEGS * LEV + level, CHUNKS * SEGS, stride=LEV)
        return jnp.where(wet[group] > level, by_rows_ref[rows, :], 0.0)

    upper = [upper_at(group, 0) for group in range(GROUPS)]
    ratio = [zero] * GROUPS
    for level in range(LEV):
        for group in range(GROUPS):
            lower = upper_at(group, level + 1)
            pivot = (1.0 + upper[group] + lower) + upper[group] * ratio[group]
            inverse = 1.0 / pivot
            ratio[group] = -lower * inverse
            inverse_ref[group, level] = jnp.where(wet[group] > level, inverse, 0.0)
            carry_ref[group, level] = upper[group] * inverse
            ratio_ref[group, level] = ratio[group]
            upper[group] = lower


def solve(source_ref, place, inverse_ref, carry_ref, ratio_ref, group, out):
    step = CHUNKS * SEGS

    def source(tracer, level):
        return source_ref[place, pl.ds(group_row(tracer, 0, 0) + level, step, stride=LEV), :]

    value = [[None] * LEV for _ in range(TRACERS)]
    for level in range(LEV):
        inverse = inverse_ref[group, level]
        carry = carry_ref[group, level]
        for tracer in range(TRACERS):
            here = source(tracer, level) * inverse
            if level:
                here = here + carry * value[tracer][level - 1]
            value[tracer][level] = here
    for level in range(LEV - 1, -1, -1):
        ratio = ratio_ref[group, level]
        for tracer in range(TRACERS):
            if level < LEV - 1:
                value[tracer][level] = value[tracer][level] - ratio * value[tracer][level + 1]
            out(tracer, level, value[tracer][level])


def into_group(ref, place):
    def write(tracer, level, value):
        ref[place, pl.ds(group_row(tracer, 0, 0) + level, CHUNKS * SEGS, stride=LEV), :] = value

    return write


def own_blocks(every_column, blocks, readers, table_ref, mixing_ref, light_ref, xs_ref, acc_ref, places):
    read, one = readers
    for block in blocks:
        start = block * TILE
        tiles = list(range(max(0, block - 2), min(BLOCKS, block + 3)))
        total = moved_part(
            xs_ref,
            tiles,
            [tile * TILE - start for tile in tiles],
            lambda k: table_row(every_column, table_ref, k, start),
            lambda seg, k: mixing_ref[seg, k, :, pl.ds(start, TILE)],
            one,
            [(tile * TILE + h, tile * TILE + h - start) for tile in tiles for h in range(0, TILE, LANE)],
            by_lane(block),
        )
        for seg in range(SEGS):
            columns = pl.ds(start, TILE)
            phosphate = read(seg, 0, start)
            organic = read(seg, 1, start)
            squared = phosphate * phosphate
            uptake = uptake_rate * light_ref[seg, :, columns] * squared / (squared + half_saturation)
            gains = (remin_rate * organic - uptake, dissolved_share * uptake - remin_rate * organic)
            own = mixing_ref[seg, 0, :, columns]
            for tracer, value in enumerate((phosphate, organic)):
                result = own * value + total[seg * TRACERS + tracer] + gains[tracer]
                for h in range(TILE // LANE):
                    row = group_row(tracer, block % 2 * 2 + h, seg)
                    acc_ref[places[block // 2], pl.ds(row, LEV), :] = result[:, h * LANE : (h + 1) * LANE]


def by_lane(block):
    return (4, 5)


EDGE_BLOCKS = (0, 1, BLOCKS - 2, BLOCKS - 1)
MIDDLE_BLOCKS = tuple(range(2, BLOCKS - 2))
EDGE_PLACES = {0: 0, GROUPS - 1: 1}
MIDDLE_PLACES = {group: group - 1 for group in range(1, GROUPS - 1)}


def sent_rows(from_ref, place, to_ref, to_place):
    for tracer in range(TRACERS):
        for chunk in range(CHUNKS):
            to_ref[to_place, pl.ds((tracer * CHUNKS + chunk) * LEV, LEV), :] = from_ref[
                place, pl.ds(group_row(tracer, chunk, SEGS - 1), LEV), :
            ]


QUARTER = (slice(None), slice(None), slice(None), pl.ds(0, HALO))


def halves_kernel(
    state_in, table_in, light_in, mixing_in,
    head_ref, tail_ref, state_ref, table_ref, light_ref, mixing_ref,
    sems,
):
    pairs = [(state_in, state_ref), (table_in, table_ref), (light_in, light_ref), (mixing_in.at[QUARTER], mixing_ref)]
    copies = [pltpu.make_async_copy(*pair, sems.at[i]) for i, pair in enumerate(pairs)]
    for copy in copies:
        copy.start()
    copies[0].wait()
    head_ref[...] = state_ref[:, :, :, :HALO]
    tail_ref[...] = state_ref[:, :, :, WIDTH - HALO :]
    for copy in copies[1:]:
        copy.wait()


def in_hbm(*arrays):
    return [pltpu.with_memory_space_constraint(one, pltpu.HBM) for one in arrays]


def halves(state, table, light, mixing):
    half = shape(SEGS, TRACERS, LEV, HALO)
    like = [jax.ShapeDtypeStruct(one.shape, one.dtype) for one in (state, table, light)]
    return pl.pallas_call(
        halves_kernel,
        out_shape=(half, half, *like, shape(SEGS, NBR, LEV, HALO)),
        in_specs=[HBM] * 4,
        out_specs=(VMEM,) * 6,
        scratch_shapes=[pltpu.SemaphoreType.DMA((4,))],
        compiler_params=PARAMS,
        cost_estimate=pl.CostEstimate(flops=0, bytes_accessed=4_000_000, transcendentals=0),
        name="edge_columns",
    )(*in_hbm(state, table, light, mixing))


def first_own_kernel(
    every_column, state_ref, table_ref, light_ref, quarter_ref, mixing_in, kappa_in, wet_in,
    edge_ref, middle_ref, inverse_ref, carry_ref, ratio_ref, mixing_ref, wet_ref,
    xs_ref, acc_ref, by_rows_ref, kappa_ref, sems,
):
    order = (GROUPS - 1,) + tuple(range(1, GROUPS - 1)) + (0,)
    parts = [(slice(None),) * 3 + (pl.ds(group * HALO, HALO),) for group in order]
    pairs = [(kappa_in, kappa_ref), (wet_in, wet_ref)] + [(mixing_in.at[part], mixing_ref.at[part]) for part in parts]
    copies = [pltpu.make_async_copy(*pair, sems.at[i]) for i, pair in enumerate(pairs)]
    for copy in copies:
        copy.start()
    read = natural_reader(state_ref)
    for tile in range(BLOCKS):
        split_tile(read[0], tile * TILE, xs_ref, tile)
    own_blocks(every_column, EDGE_BLOCKS[:2], read, table_ref, quarter_ref, light_ref, xs_ref, edge_ref, EDGE_PLACES)
    for copy in copies:
        copy.wait()
    own_blocks(every_column, EDGE_BLOCKS[2:], read, table_ref, mixing_ref, light_ref, xs_ref, edge_ref, EDGE_PLACES)
    factorize(kappa_ref, wet_ref, by_rows_ref, inverse_ref, carry_ref, ratio_ref)
    own_blocks(every_column, MIDDLE_BLOCKS, read, table_ref, mixing_ref, light_ref, xs_ref, acc_ref, MIDDLE_PLACES)
    for group, place in MIDDLE_PLACES.items():
        solve(acc_ref, place, inverse_ref, carry_ref, ratio_ref, group, into_group(middle_ref, place))


def second_reader(head_ref, middle_ref, tail_ref):
    return group_reader([(head_ref, 0)] + [(middle_ref, i) for i in range(GROUPS - 2)] + [(tail_ref, 0)])


def second_middle_kernel(
    every_column, head_ref, middle_in_ref, tail_ref, table_ref, mixing_ref, light_ref, inverse_ref, carry_ref, ratio_ref,
    middle_ref, sent_ref, xs_ref,
    acc_ref,
):
    read = second_reader(head_ref, middle_in_ref, tail_ref)
    for tile in range(BLOCKS):
        split_tile(read[0], tile * TILE, xs_ref, tile)
    own_blocks(every_column, MIDDLE_BLOCKS, read, table_ref, mixing_ref, light_ref, xs_ref, acc_ref, MIDDLE_PLACES)
    for group, place in MIDDLE_PLACES.items():
        solve(acc_ref, place, inverse_ref, carry_ref, ratio_ref, group, into_group(middle_ref, place))
        sent_rows(middle_ref, place, sent_ref, place)


def second_edge_kernel(every_column, head_ref, middle_ref, tail_ref, table_ref, mixing_ref, light_ref, xs_ref, edge_ref):
    read = second_reader(head_ref, middle_ref, tail_ref)
    own_blocks(every_column, EDGE_BLOCKS, read, table_ref, mixing_ref, light_ref, xs_ref, edge_ref, EDGE_PLACES)


def edge_kernel(
    first, every_column, left_ref, right_ref, table_ref, mixing_ref, edge_in_ref, inverse_ref, carry_ref, ratio_ref,
    *outs_and_scratch,
):
    head_ref, tail_ref, *sent, xs_ref, acc_ref = outs_and_scratch
    readers = []
    for side, ref in enumerate((left_ref, right_ref)):
        readers.append(natural_reader(ref) if first else group_reader([(ref, 0)]))
        for tile in range(HALO // TILE):
            split_tile(readers[side][0], tile * TILE, xs_ref, side * 2 + tile)
    uses = ((0, 0, (0, 1)), (1, 0, (1,)), (BLOCKS - 2, 1, (2,)), (BLOCKS - 1, 1, (2, 3)))
    offsets = (-HALO, -TILE, WIDTH, WIDTH + TILE)
    for block, side, places in uses:
        start = block * TILE
        total = moved_part(
            xs_ref,
            places,
            [offsets[place] - start for place in places],
            lambda k: table_row(every_column, table_ref, k, start),
            lambda seg, k: mixing_ref[seg, k, :, pl.ds(start, TILE)],
            readers[side][1],
            [(place % 2 * TILE + h, offsets[place] + h - start) for place in places for h in range(0, TILE, LANE)],
            by_lane(block),
        )
        for seg in range(SEGS):
            for tracer in range(TRACERS):
                value = total[seg * TRACERS + tracer]
                for h in range(TILE // LANE):
                    row = pl.ds(group_row(tracer, block % 2 * 2 + h, seg), LEV)
                    acc_ref[side, row, :] = edge_in_ref[side, row, :] + value[:, h * LANE : (h + 1) * LANE]
    for side, (group, ref) in enumerate(((0, head_ref), (GROUPS - 1, tail_ref))):
        solve(acc_ref, side, inverse_ref, carry_ref, ratio_ref, group, into_group(ref, 0))
        if sent:
            sent_rows(ref, 0, sent[0], side)


EDGE = shape(2, GROUP_ROWS, LANE)
MIDDLE = shape(GROUPS - 2, GROUP_ROWS, LANE)
SENT = shape(2, GROUP_ROWS // SEGS, LANE)
ONE = shape(1, GROUP_ROWS, LANE)


def call(kernel, name, flops, outs, scratch, *operands):
    return pl.pallas_call(
        kernel,
        out_shape=outs,
        in_specs=[VMEM] * len(operands),
        out_specs=jax.tree.map(lambda _: VMEM, outs),
        scratch_shapes=scratch,
        compiler_params=PARAMS,
        cost_estimate=pl.CostEstimate(flops=flops, bytes_accessed=4_000_000, transcendentals=0),
        name=name,
    )(*operands)


def first_own(every_column, state, table, light, quarter, mixing, kappa, wet):
    factors = shape(GROUPS, LEV, CHUNKS * SEGS, LANE)
    like = [jax.ShapeDtypeStruct(one.shape, one.dtype) for one in (mixing, wet)]
    return pl.pallas_call(
        functools.partial(first_own_kernel, every_column),
        out_shape=(EDGE, MIDDLE, factors, factors, factors, *like),
        in_specs=[VMEM] * 4 + [HBM] * 3,
        out_specs=(VMEM,) * 7,
        scratch_shapes=[
            pltpu.VMEM((BLOCKS, 2 * ROWS, TILE), bf16),
            pltpu.VMEM((GROUPS - 2, GROUP_ROWS, LANE), f32),
            pltpu.VMEM((GROUPS * CHUNKS * SEGS * LEV, LANE), f32),
            pltpu.VMEM((SEGS, LEV, WIDTH), f32),
            pltpu.SemaphoreType.DMA((2 + GROUPS,)),
        ],
        compiler_params=PARAMS,
        cost_estimate=pl.CostEstimate(flops=6_000_000_000, bytes_accessed=4_000_000, transcendentals=0),
        name="first_step_own",
    )(state, table, light, quarter, *in_hbm(mixing, kappa, wet))


def second_middle(every_column, head, middle, tail, table, mixing, light, factors):
    return call(
        functools.partial(second_middle_kernel, every_column), "second_step_middle", 3_500_000_000,
        (MIDDLE, SENT, jax.ShapeDtypeStruct((BLOCKS, 2 * ROWS, TILE), bf16)),
        [pltpu.VMEM((GROUPS - 2, GROUP_ROWS, LANE), f32)],
        head, middle, tail, table, mixing, light, *factors,
    )


def second_edge(every_column, head, middle, tail, table, mixing, light, xs):
    return call(
        functools.partial(second_edge_kernel, every_column), "second_step_edges_own", 2_500_000_000, EDGE, [],
        head, middle, tail, table, mixing, light, xs,
    )


def edges(first, every_column, left, right, table, mixing, edge, factors):
    return call(
        functools.partial(edge_kernel, first, every_column),
        "first_step_edges" if first else "second_step_edges", 1_000_000_000,
        (ONE, ONE) if first else (ONE, ONE, SENT),
        [pltpu.VMEM((4, 2 * ROWS, TILE), bf16), pltpu.VMEM((2, GROUP_ROWS, LANE), f32)],
        left, right, table, mixing, edge, *factors,
    )


PAIRS = [(i, j) for i in range(BASIS) for j in range(i, BASIS)]
SUMS = BASIS + 1 + len(PAIRS)
KNOWN = ((range(GROUPS), range(1, SEGS)), (range(1, GROUPS - 1), (0,)))
UNKNOWN = (((0, GROUPS - 1), (0,)),)


def pieces_of(areas):
    for groups, segs in areas:
        for group in groups:
            for chunk in range(CHUNKS):
                lanes = pl.ds(group * HALO + chunk * LANE, LANE)
                for seg in segs:
                    for tracer in range(TRACERS):
                        for level in range(0, LEV, 8):
                            yield group, chunk, seg, tracer, level, pl.ds(level, 8), lanes


def residual_at(place, state_ref, wet_ref, before):
    group, chunk, seg, tracer, level, rows, lanes = place
    wet = jnp.broadcast_to(wet_ref[pl.ds(group * CHUNKS + chunk, 1), :], (8, LANE))
    here = wet > lax.broadcasted_iota(jnp.int32, (8, LANE), 0) + level
    return jnp.where(here, state_ref[seg, tracer, rows, lanes] - before, 0.0)


def basis_at(place, basis_ref):
    _, _, seg, tracer, _, rows, lanes = place
    return [basis_ref[i, seg, tracer, rows, lanes] for i in range(BASIS)]


def add_products(sums, vectors):
    for at, (i, j) in enumerate(PAIRS):
        sums[at] = sums[at] + vectors[i] * vectors[j]


def add_rest(sums, vectors, value, guess):
    for i in range(BASIS):
        value = value - guess[i] * vectors[i]
    for i in range(BASIS):
        sums[i] = sums[i] + vectors[i] * value
    sums[BASIS] = sums[BASIS] + value * value


def symmetric(values):
    matrix = [[None] * BASIS for _ in range(BASIS)]
    for (i, j), value in zip(PAIRS, values):
        matrix[i][j] = matrix[j][i] = value
    return matrix


def whole_sum(value):
    return jnp.sum(jnp.sum(value, axis=0, keepdims=True), axis=1, keepdims=True)


def least_squares(products, right):
    gram = symmetric(products)
    factor = [[None] * BASIS for _ in range(BASIS)]
    pivots, inverses, weights = [], [], []
    for i in range(BASIS):
        for j in range(i):
            value = gram[i][j]
            for k in range(j):
                value = value - factor[i][k] * pivots[k] * factor[j][k]
            factor[i][j] = value * inverses[j]
        pivot = gram[i][i]
        for k in range(i):
            pivot = pivot - factor[i][k] * factor[i][k] * pivots[k]
        usable = (pivot > 1e-3 * gram[i][i]) & (pivot > 1e-30)
        pivots.append(pivot)
        inverses.append(jnp.where(usable, 1.0 / jnp.where(usable, pivot, 1.0), 0.0))
        value = right[i]
        for k in range(i):
            value = value - factor[i][k] * weights[k]
        weights.append(value)
    for i in range(BASIS - 1, -1, -1):
        value = weights[i] * inverses[i]
        for k in range(i + 1, BASIS):
            value = value - factor[k][i] * weights[k]
        weights[i] = value
    return weights


def early_kernel(
    state_ref, wet_ref, basis_ref, head_ref, middle_ref, tail_ref, came_ref,
    out_ref, residual_ref, sums_ref, guess_ref, sems,
):
    refs = [(head_ref, 0)] + [(middle_ref, i) for i in range(GROUPS - 2)] + [(tail_ref, 0)]
    zero = jnp.zeros((8, LANE), f32)
    first = [zero] * BASIS
    products = [zero] * len(PAIRS)
    for place in pieces_of(KNOWN):
        group, chunk, seg, tracer, level, rows, lanes = place
        if seg:
            ref, at = refs[group]
            before = ref[at, pl.ds(group_row(tracer, chunk, seg - 1) + level, 8), :]
        else:
            before = came_ref[group - 1, pl.ds((tracer * CHUNKS + chunk) * LEV + level, 8), :]
        value = residual_at(place, state_ref, wet_ref, before)
        residual_ref[seg, tracer, rows, lanes] = value
        vectors = basis_at(place, basis_ref)
        for i in range(BASIS):
            first[i] = first[i] + vectors[i] * value
        add_products(products, vectors)
    parts = [(slice(1, SEGS),), (slice(0, 1), slice(None), slice(None), pl.ds(HALO, WIDTH - 2 * HALO))]
    copies = [pltpu.make_async_copy(residual_ref.at[part], out_ref.at[part], sems.at[i]) for i, part in enumerate(parts)]
    for copy in copies:
        copy.start()
    weights = least_squares([whole_sum(one) for one in products], [whole_sum(one) for one in first])
    guess = [jnp.broadcast_to(weight, (8, LANE)) for weight in weights]
    sums = [zero] * (BASIS + 1)
    for place in pieces_of(KNOWN):
        _, _, seg, tracer, _, rows, lanes = place
        add_rest(sums, basis_at(place, basis_ref), residual_ref[seg, tracer, rows, lanes], guess)
    for place in pieces_of(UNKNOWN):
        add_products(products, basis_at(place, basis_ref))
    for i, one in enumerate(sums + products):
        sums_ref[i] = one
    for i, one in enumerate(guess):
        guess_ref[i] = one
    for copy in copies:
        copy.wait()


def late_kernel(state_ref, wet_ref, basis_ref, came_ref, early_ref, guess_ref, pieces_ref, sums_ref):
    guess = [guess_ref[i] for i in range(BASIS)]
    sums = [early_ref[i] for i in range(SUMS)]
    for place in pieces_of(UNKNOWN):
        group, chunk, seg, tracer, level, rows, lanes = place
        before = came_ref[EDGE_PLACES[group], pl.ds((tracer * CHUNKS + chunk) * LEV + level, 8), :]
        value = residual_at(place, state_ref, wet_ref, before)
        pieces_ref[EDGE_PLACES[group], tracer, rows, pl.ds(chunk * LANE, LANE)] = value
        add_rest(sums, basis_at(place, basis_ref), value, guess)
    lane = lax.broadcasted_iota(jnp.int32, (8, LANE), 1)
    row = jnp.zeros((8, LANE), f32)
    for i, one in enumerate([whole_sum(one) for one in sums] + guess):
        row = jnp.where(lane == i, one, row)
    for i in range(sums_ref.shape[0] // 8):
        sums_ref[pl.ds(8 * i, 8), :] = row


def early(state, wet, basis, head, middle, tail, came):
    whole = shape(SEGS, TRACERS, LEV, WIDTH)
    return pl.pallas_call(
        early_kernel,
        out_shape=(whole, whole, shape(SUMS, 8, LANE), shape(BASIS, 8, LANE)),
        in_specs=[VMEM] * 7,
        out_specs=(HBM, VMEM, VMEM, VMEM),
        scratch_shapes=[pltpu.SemaphoreType.DMA((2,))],
        compiler_params=PARAMS,
        cost_estimate=pl.CostEstimate(flops=10_000_000, bytes_accessed=4_000_000, transcendentals=0),
        name="residual_known",
    )(state, wet, basis, head, middle, tail, came)


def late(devices, state, wet, basis, came, sums, guess):
    return call(
        late_kernel, "residual_last", 3_000_000, (shape(2, TRACERS, LEV, HALO), shape(devices, LANE)), [],
        state, wet, basis, came, sums, guess,
    )


def scaled_kernel(
    count, residual_ref, pieces_ref, basis_ref, sums_ref, unused_ref,
    out_ref, new_out_ref, coefficients_ref, new_ref, sems,
):
    copies = []

    def send(from_ref, to_ref):
        copies.append(pltpu.make_async_copy(from_ref, to_ref, sems.at[len(copies)]))
        copies[-1].start()

    for group, place in EDGE_PLACES.items():
        send(pieces_ref.at[place], out_ref.at[0, :, :, pl.ds(group * HALO, HALO)])
    sums = sums_ref[...]
    if sums.shape[0] < LANE:
        sums = jnp.concatenate([sums, jnp.zeros((LANE - sums.shape[0], LANE), f32)], axis=0)
    sums = sums.T
    row = [sums[i : i + 1] for i in range(SUMS + BASIS)]
    of_rest, squares, products, guess = row[:BASIS], row[BASIS], row[BASIS + 1 : SUMS], row[SUMS:]
    gram = symmetric(products)
    first = [of_rest[i] + sum(gram[i][j] * guess[j] for j in range(BASIS)) for i in range(BASIS)]
    totals = jnp.concatenate(first + products + [jnp.zeros((2, LANE), f32)], axis=0)
    totals = jnp.sum(totals, axis=1, keepdims=True)
    one = [totals[i : i + 1] for i in range(SUMS)]
    first, products = one[:BASIS], one[BASIS : SUMS - 1]
    whole_gram = symmetric(products)
    second = [first[i] - sum(whole_gram[i][j] * first[j] for j in range(BASIS)) for i in range(BASIS)]
    both = [first[i] + second[i] for i in range(BASIS)]
    away = [both[i] - guess[i] for i in range(BASIS)]
    for i in range(BASIS):
        squares = squares + away[i] * (sum(gram[i][j] * away[j] for j in range(BASIS)) - 2.0 * of_rest[i])
    square = jnp.maximum(jnp.sum(squares, axis=1, keepdims=True), 0.0)
    spread = jnp.sqrt(square / count + epsilon)
    lane = lax.broadcasted_iota(jnp.int32, (8, LANE), 1)
    result = jnp.zeros((8, LANE), f32)
    for i, value in enumerate(both + [spread]):
        result = jnp.where(lane == i, value, result)
    coefficients_ref[...] = result[0, : BASIS + 1]
    scale = 1.0 / spread
    weights = [jnp.broadcast_to(-value * scale, (LEV, LANE)) for value in both]
    scale = jnp.broadcast_to(scale, (LEV, LANE))
    for seg in range(SEGS):
        for tracer in range(TRACERS):
            for chunk in range(WIDTH // LANE):
                lanes = pl.ds(chunk * LANE, LANE)
                group = chunk // CHUNKS
                if seg == 0 and group in EDGE_PLACES:
                    here = pieces_ref[EDGE_PLACES[group], tracer, :, pl.ds(chunk % CHUNKS * LANE, LANE)]
                else:
                    here = residual_ref[seg, tracer, :, lanes]
                total = here * scale
                for i in range(BASIS):
                    total = total + weights[i] * basis_ref[i, seg, tracer, :, lanes]
                new_ref[seg, tracer, :, lanes] = total
            send(new_ref.at[seg, tracer], new_out_ref.at[seg, tracer])
    for copy in copies:
        copy.wait()


def scaled(count, residual, pieces, basis, sums, out):
    whole = (SEGS, TRACERS, LEV, WIDTH)
    return pl.pallas_call(
        functools.partial(scaled_kernel, count),
        out_shape=(shape(*whole), shape(*whole), shape(BASIS + 1)),
        in_specs=[VMEM] * 4 + [HBM],
        out_specs=(HBM, HBM, VMEM),
        scratch_shapes=[pltpu.VMEM(whole, f32), pltpu.SemaphoreType.DMA((2 + SEGS * TRACERS,))],
        input_output_aliases={4: 0},
        compiler_params=PARAMS,
        cost_estimate=pl.CostEstimate(flops=4_000_000, bytes_accessed=4_000_000, transcendentals=0),
        name="orthogonal_and_scaled",
    )(residual, pieces, basis, sums, out)


def shifted(block, axis, distance):
    count = lax.axis_size(axis)
    return lax.ppermute(block, axis, [(i, (i + distance) % count) for i in range(count)])


def per_device(segment_state, light, mixing, kappa, neighbour_columns, wet_levels, basis):
    every_column = lax.axis_size("col") * WIDTH
    table = neighbour_columns.T
    wet = wet_levels.reshape(WIDTH // LANE, LANE)
    head, tail, state, table, light, quarter = halves(segment_state, table, light, mixing)
    left = shifted(tail, "col", 1)
    right = shifted(head, "col", -1)
    edge, middle, *factors, mixing, wet = first_own(every_column, state, table, light, quarter, mixing, kappa, wet)
    head, tail = edges(True, every_column, left, right, table, mixing, edge, factors)
    left = shifted(tail, "col", 1)
    right = shifted(head, "col", -1)
    end_middle, sent, xs = second_middle(every_column, head, middle, tail, table, mixing, light, factors)
    came_middle = shifted(sent, "seg", 1)
    edge = second_edge(every_column, head, middle, tail, table, mixing, light, xs)
    head, tail, sent = edges(False, every_column, left, right, table, mixing, edge, factors)
    came_edge = shifted(sent, "seg", 1)
    residual, held, sums, guess = early(state, wet, basis, head, end_middle, tail, came_middle)
    devices = lax.axis_size("seg") * lax.axis_size("col")
    pieces, sums = late(devices, state, wet, basis, came_edge, sums, guess)
    sums = lax.all_to_all(sums, ("seg", "col"), 0, 0, tiled=True)
    count = lax.axis_size("seg") * SEGS * TRACERS * LEV * every_column
    return scaled(count, held, pieces, basis, sums, residual)


def solution(mesh):
    return jax.shard_map(
        per_device,
        mesh=mesh,
        in_specs=(
            P("seg", None, None, "col"),
            P("seg", None, "col"),
            P("seg", None, None, "col"),
            P("seg", None, "col"),
            P("col", None),
            P("col"),
            P(None, "seg", None, None, "col"),
        ),
        out_specs=(P("seg", None, None, "col"), P("seg", None, None, "col"), P()),
        check_vma=False,
    )
```

```python
import functools

import jax
import jax.numpy as jnp
from jax import lax
from jax.experimental import pallas as pl
from jax.experimental.pallas import tpu as pltpu
from jax.sharding import PartitionSpec as P

uptake_rate = 0.6
half_saturation = 0.3
remin_rate = 0.2
dissolved_share = 0.7
epsilon = 1e-06

SEGS = 2
TRACERS = 2
LEV = 32
NBR = 6
BASIS = 4
WIDTH = 2048
HALO = 512
LANE = 128
TILE = 256
BLOCKS = WIDTH // TILE
GROUPS = WIDTH // HALO
CHUNKS = HALO // LANE
ROWS = SEGS * TRACERS * LEV
GROUP_ROWS = TRACERS * CHUNKS * SEGS * LEV
VMEM = pl.BlockSpec(memory_space=pltpu.VMEM)
PARAMS = pltpu.CompilerParams(vmem_limit_bytes=16 * 1024 * 1024)
ANY = pl.BlockSpec(memory_space=pl.ANY)
HBM = pl.BlockSpec(memory_space=pltpu.HBM)
f32 = jnp.float32
bf16 = jnp.bfloat16


def shape(*dims):
    return jax.ShapeDtypeStruct(dims, f32)


def group_row(tracer, chunk, seg):
    return ((tracer * CHUNKS + chunk) * SEGS + seg) * LEV


def natural_reader(ref):
    def read(seg, tracer, start):
        return ref[seg, tracer, :, pl.ds(start, TILE)]

    def one(seg, tracer, level, start):
        return ref[seg, tracer, pl.ds(level, 8), pl.ds(start, LANE)]

    return read, one


def group_reader(refs):
    def read(seg, tracer, start):
        ref, place = refs[start // HALO]
        chunk = start % HALO // LANE
        parts = [ref[place, pl.ds(group_row(tracer, chunk + h, seg), LEV), :] for h in range(TILE // LANE)]
        return jnp.concatenate(parts, axis=1)

    def one(seg, tracer, level, start):
        ref, place = refs[start // HALO]
        return ref[place, pl.ds(group_row(tracer, start % HALO // LANE, seg) + level, 8), :]

    return read, one


def split_tile(read, start, xs_ref, place):
    for seg in range(SEGS):
        for tracer in range(TRACERS):
            value = read(seg, tracer, start)
            high = value.astype(bf16)
            low = (value - high.astype(f32)).astype(bf16)
            row = (seg * TRACERS + tracer) * LEV
            xs_ref[place, pl.ds(row, LEV), :] = high
            xs_ref[place, pl.ds(ROWS + row, LEV), :] = low


def table_row(every_column, table_ref, k, start):
    columns = pl.ds(start, TILE)
    away = table_ref[pl.ds(k, 1), columns] - table_ref[pl.ds(0, 1), columns]
    away = jnp.where(away > HALO, away - every_column, away)
    away = jnp.where(away < -HALO, away + every_column, away)
    return away + lax.broadcasted_iota(jnp.int32, (1, TILE), 1)


def picked(xs_ref, places, offsets, index):
    total = None
    depth = lax.broadcasted_iota(jnp.int16, (TILE, TILE), 0)
    for place, offset in zip(places, offsets):
        wanted = jnp.broadcast_to(index - offset, (16, TILE)).astype(jnp.int16)
        wanted = jnp.concatenate([wanted] * (TILE // 16), axis=0)
        chosen = jnp.where(depth == wanted, bf16(1), bf16(0))
        part = jnp.dot(xs_ref[place], chosen, preferred_element_type=f32)
        total = part if total is None else total + part
    return total[:ROWS] + total[ROWS:]


def gathered(one, chunks, index):
    halves = []
    for h in range(TILE // LANE):
        at = jnp.broadcast_to(index[:, h * LANE : (h + 1) * LANE], (8, LANE))
        lane = at & (LANE - 1)
        usable = [(start, first) for start, first in chunks if abs(first - h * LANE) <= HALO]
        chosen = [at - lane == first for _, first in usable]
        rows = []
        for seg in range(SEGS):
            for tracer in range(TRACERS):
                for level in range(0, LEV, 8):
                    total = jnp.zeros((8, LANE), f32)
                    for (start, _), here in zip(usable, chosen):
                        value = jnp.take_along_axis(one(seg, tracer, level, start), lane, axis=1, mode="promise_in_bounds")
                        total = jnp.where(here, value, total)
                    rows.append(total)
        halves.append(jnp.concatenate(rows, axis=0))
    return jnp.concatenate(halves, axis=1)


def moved_part(xs_ref, places, offsets, index_of, mixing_of, one, chunks, by_lane):
    total = [None] * (SEGS * TRACERS)
    for k in range(1, NBR):
        index = index_of(k)
        value = gathered(one, chunks, index) if k in by_lane else picked(xs_ref, places, offsets, index)
        for seg in range(SEGS):
            mix = mixing_of(seg, k)
            for tracer in range(TRACERS):
                at = seg * TRACERS + tracer
                term = mix * value[at * LEV : (at + 1) * LEV]
                total[at] = term if total[at] is None else total[at] + term
    return total


def factorize(kappa_ref, wet_ref, by_rows_ref, inverse_ref, carry_ref, ratio_ref):
    for group in range(GROUPS):
        for chunk in range(CHUNKS):
            for seg in range(SEGS):
                lanes = pl.ds(group * HALO + chunk * LANE, LANE)
                row = (group * CHUNKS * SEGS + chunk * SEGS + seg) * LEV
                by_rows_ref[pl.ds(row, LEV), :] = kappa_ref[seg, :, lanes]
    wet = []
    for group in range(GROUPS):
        rows = []
        for chunk in range(CHUNKS):
            one = wet_ref[pl.ds(group * CHUNKS + chunk, 1), :]
            rows += [one] * SEGS
        wet.append(jnp.concatenate(rows, axis=0))
    zero = jnp.zeros((CHUNKS * SEGS, LANE), f32)

    def upper_at(group, level):
        if level == 0 or level == LEV:
            return zero
        rows = pl.ds(group * CHUNKS * SEGS * LEV + level, CHUNKS * SEGS, stride=LEV)
        return jnp.where(wet[group] > level, by_rows_ref[rows, :], 0.0)

    upper = [upper_at(group, 0) for group in range(GROUPS)]
    ratio = [zero] * GROUPS
    for level in range(LEV):
        for group in range(GROUPS):
            lower = upper_at(group, level + 1)
            pivot = (1.0 + upper[group] + lower) + upper[group] * ratio[group]
            inverse = 1.0 / pivot
            ratio[group] = -lower * inverse
            inverse_ref[group, level] = jnp.where(wet[group] > level, inverse, 0.0)
            carry_ref[group, level] = upper[group] * inverse
            ratio_ref[group, level] = ratio[group]
            upper[group] = lower


def solve(source_ref, place, inverse_ref, carry_ref, ratio_ref, group, out):
    step = CHUNKS * SEGS

    def source(tracer, level):
        return source_ref[place, pl.ds(group_row(tracer, 0, 0) + level, step, stride=LEV), :]

    value = [[None] * LEV for _ in range(TRACERS)]
    for level in range(LEV):
        inverse = inverse_ref[group, level]
        carry = carry_ref[group, level]
        for tracer in range(TRACERS):
            here = source(tracer, level) * inverse
            if level:
                here = here + carry * value[tracer][level - 1]
            value[tracer][level] = here
    for level in range(LEV - 1, -1, -1):
        ratio = ratio_ref[group, level]
        for tracer in range(TRACERS):
            if level < LEV - 1:
                value[tracer][level] = value[tracer][level] - ratio * value[tracer][level + 1]
            out(tracer, level, value[tracer][level])


def into_group(ref, place):
    def write(tracer, level, value):
        ref[place, pl.ds(group_row(tracer, 0, 0) + level, CHUNKS * SEGS, stride=LEV), :] = value

    return write


def own_blocks(every_column, blocks, readers, table_ref, mixing_ref, light_ref, xs_ref, acc_ref, places):
    read, one = readers
    for block in blocks:
        start = block * TILE
        tiles = list(range(max(0, block - 2), min(BLOCKS, block + 3)))
        total = moved_part(
            xs_ref,
            tiles,
            [tile * TILE - start for tile in tiles],
            lambda k: table_row(every_column, table_ref, k, start),
            lambda seg, k: mixing_ref[seg, k, :, pl.ds(start, TILE)],
            one,
            [(tile * TILE + h, tile * TILE + h - start) for tile in tiles for h in range(0, TILE, LANE)],
            by_lane(block),
        )
        for seg in range(SEGS):
            columns = pl.ds(start, TILE)
            phosphate = read(seg, 0, start)
            organic = read(seg, 1, start)
            squared = phosphate * phosphate
            uptake = uptake_rate * light_ref[seg, :, columns] * squared / (squared + half_saturation)
            gains = (remin_rate * organic - uptake, dissolved_share * uptake - remin_rate * organic)
            own = mixing_ref[seg, 0, :, columns]
            for tracer, value in enumerate((phosphate, organic)):
                result = own * value + total[seg * TRACERS + tracer] + gains[tracer]
                for h in range(TILE // LANE):
                    row = group_row(tracer, block % 2 * 2 + h, seg)
                    acc_ref[places[block // 2], pl.ds(row, LEV), :] = result[:, h * LANE : (h + 1) * LANE]


def by_lane(block):
    return (4, 5)


EDGE_BLOCKS = (0, 1, BLOCKS - 2, BLOCKS - 1)
MIDDLE_BLOCKS = tuple(range(2, BLOCKS - 2))
EDGE_PLACES = {0: 0, GROUPS - 1: 1}
MIDDLE_PLACES = {group: group - 1 for group in range(1, GROUPS - 1)}


def sent_rows(from_ref, place, to_ref, to_place):
    for tracer in range(TRACERS):
        for chunk in range(CHUNKS):
            to_ref[to_place, pl.ds((tracer * CHUNKS + chunk) * LEV, LEV), :] = from_ref[
                place, pl.ds(group_row(tracer, chunk, SEGS - 1), LEV), :
            ]


def halves_kernel(
    state_in, table_in,
    head_ref, tail_ref, state_ref, table_ref,
    sems,
):
    pairs = [(state_in, state_ref), (table_in, table_ref)]
    copies = [pltpu.make_async_copy(*pair, sems.at[i]) for i, pair in enumerate(pairs)]
    for copy in copies:
        copy.start()
    copies[0].wait()
    head_ref[...] = state_ref[:, :, :, :HALO]
    tail_ref[...] = state_ref[:, :, :, WIDTH - HALO :]
    for copy in copies[1:]:
        copy.wait()


def in_hbm(*arrays):
    return [pltpu.with_memory_space_constraint(one, pltpu.HBM) for one in arrays]


def halves(state, table):
    half = shape(SEGS, TRACERS, LEV, HALO)
    like = [jax.ShapeDtypeStruct(one.shape, one.dtype) for one in (state, table)]
    return pl.pallas_call(
        halves_kernel,
        out_shape=(half, half, *like),
        in_specs=[HBM] * 2,
        out_specs=(VMEM,) * 4,
        scratch_shapes=[pltpu.SemaphoreType.DMA((2,))],
        compiler_params=PARAMS,
        cost_estimate=pl.CostEstimate(flops=0, bytes_accessed=4_000_000, transcendentals=0),
        name="edge_columns",
    )(*in_hbm(state, table))


def first_own_kernel(
    every_column, state_ref, table_ref, light_in, mixing_in, kappa_in, wet_in,
    edge_ref, middle_ref, inverse_ref, carry_ref, ratio_ref, light_ref, mixing_ref, wet_ref,
    xs_ref, acc_ref, by_rows_ref, kappa_ref, sems,
):
    order = (0, GROUPS - 1) + tuple(range(1, GROUPS - 1))
    parts = [(slice(None),) * 3 + (pl.ds(group * HALO, HALO),) for group in order]
    pairs = [(mixing_in.at[part], mixing_ref.at[part]) for part in parts]
    pairs = pairs[:1] + [(light_in, light_ref), (kappa_in, kappa_ref), (wet_in, wet_ref)] + pairs[1:]
    copies = [pltpu.make_async_copy(*pair, sems.at[i]) for i, pair in enumerate(pairs)]
    for copy in copies:
        copy.start()
    read = natural_reader(state_ref)
    for tile in range(BLOCKS):
        split_tile(read[0], tile * TILE, xs_ref, tile)
    for copy in copies[:2]:
        copy.wait()
    own_blocks(every_column, EDGE_BLOCKS[:2], read, table_ref, mixing_ref, light_ref, xs_ref, edge_ref, EDGE_PLACES)
    for copy in copies[2:]:
        copy.wait()
    own_blocks(every_column, EDGE_BLOCKS[2:], read, table_ref, mixing_ref, light_ref, xs_ref, edge_ref, EDGE_PLACES)
    factorize(kappa_ref, wet_ref, by_rows_ref, inverse_ref, carry_ref, ratio_ref)
    own_blocks(every_column, MIDDLE_BLOCKS, read, table_ref, mixing_ref, light_ref, xs_ref, acc_ref, MIDDLE_PLACES)
    for group, place in MIDDLE_PLACES.items():
        solve(acc_ref, place, inverse_ref, carry_ref, ratio_ref, group, into_group(middle_ref, place))


def second_reader(head_ref, middle_ref, tail_ref):
    return group_reader([(head_ref, 0)] + [(middle_ref, i) for i in range(GROUPS - 2)] + [(tail_ref, 0)])


def second_middle_kernel(
    every_column, head_ref, middle_in_ref, tail_ref, table_ref, mixing_ref, light_ref, inverse_ref, carry_ref, ratio_ref,
    middle_ref, sent_ref, xs_ref,
    acc_ref,
):
    read = second_reader(head_ref, middle_in_ref, tail_ref)
    for tile in range(BLOCKS):
        split_tile(read[0], tile * TILE, xs_ref, tile)
    own_blocks(every_column, MIDDLE_BLOCKS, read, table_ref, mixing_ref, light_ref, xs_ref, acc_ref, MIDDLE_PLACES)
    for group, place in MIDDLE_PLACES.items():
        solve(acc_ref, place, inverse_ref, carry_ref, ratio_ref, group, into_group(middle_ref, place))
        sent_rows(middle_ref, place, sent_ref, place)


def second_edge_kernel(every_column, head_ref, middle_ref, tail_ref, table_ref, mixing_ref, light_ref, xs_ref, edge_ref):
    read = second_reader(head_ref, middle_ref, tail_ref)
    own_blocks(every_column, EDGE_BLOCKS, read, table_ref, mixing_ref, light_ref, xs_ref, edge_ref, EDGE_PLACES)


def edge_kernel(
    first, every_column, left_ref, right_ref, table_ref, mixing_ref, edge_in_ref, inverse_ref, carry_ref, ratio_ref,
    *outs_and_scratch,
):
    head_ref, tail_ref, *sent, xs_ref, acc_ref = outs_and_scratch
    readers = []
    for side, ref in enumerate((left_ref, right_ref)):
        readers.append(natural_reader(ref) if first else group_reader([(ref, 0)]))
        for tile in range(HALO // TILE):
            split_tile(readers[side][0], tile * TILE, xs_ref, side * 2 + tile)
    uses = ((0, 0, (0, 1)), (1, 0, (1,)), (BLOCKS - 2, 1, (2,)), (BLOCKS - 1, 1, (2, 3)))
    offsets = (-HALO, -TILE, WIDTH, WIDTH + TILE)
    for block, side, places in uses:
        start = block * TILE
        total = moved_part(
            xs_ref,
            places,
            [offsets[place] - start for place in places],
            lambda k: table_row(every_column, table_ref, k, start),
            lambda seg, k: mixing_ref[seg, k, :, pl.ds(start, TILE)],
            readers[side][1],
            [(place % 2 * TILE + h, offsets[place] + h - start) for place in places for h in range(0, TILE, LANE)],
            by_lane(block),
        )
        for seg in range(SEGS):
            for tracer in range(TRACERS):
                value = total[seg * TRACERS + tracer]
                for h in range(TILE // LANE):
                    row = pl.ds(group_row(tracer, block % 2 * 2 + h, seg), LEV)
                    acc_ref[side, row, :] = edge_in_ref[side, row, :] + value[:, h * LANE : (h + 1) * LANE]
    for side, (group, ref) in enumerate(((0, head_ref), (GROUPS - 1, tail_ref))):
        solve(acc_ref, side, inverse_ref, carry_ref, ratio_ref, group, into_group(ref, 0))
        if sent:
            sent_rows(ref, 0, sent[0], side)


EDGE = shape(2, GROUP_ROWS, LANE)
MIDDLE = shape(GROUPS - 2, GROUP_ROWS, LANE)
SENT = shape(2, GROUP_ROWS // SEGS, LANE)
ONE = shape(1, GROUP_ROWS, LANE)


def call(kernel, name, flops, outs, scratch, *operands):
    return pl.pallas_call(
        kernel,
        out_shape=outs,
        in_specs=[VMEM] * len(operands),
        out_specs=jax.tree.map(lambda _: VMEM, outs),
        scratch_shapes=scratch,
        compiler_params=PARAMS,
        cost_estimate=pl.CostEstimate(flops=flops, bytes_accessed=4_000_000, transcendentals=0),
        name=name,
    )(*operands)


def first_own(every_column, state, table, light, mixing, kappa, wet):
    factors = shape(GROUPS, LEV, CHUNKS * SEGS, LANE)
    like = [jax.ShapeDtypeStruct(one.shape, one.dtype) for one in (light, mixing, wet)]
    return pl.pallas_call(
        functools.partial(first_own_kernel, every_column),
        out_shape=(EDGE, MIDDLE, factors, factors, factors, *like),
        in_specs=[VMEM] * 2 + [HBM] * 4,
        out_specs=(VMEM,) * 8,
        scratch_shapes=[
            pltpu.VMEM((BLOCKS, 2 * ROWS, TILE), bf16),
            pltpu.VMEM((GROUPS - 2, GROUP_ROWS, LANE), f32),
            pltpu.VMEM((GROUPS * CHUNKS * SEGS * LEV, LANE), f32),
            pltpu.VMEM((SEGS, LEV, WIDTH), f32),
            pltpu.SemaphoreType.DMA((3 + GROUPS,)),
        ],
        compiler_params=PARAMS,
        cost_estimate=pl.CostEstimate(flops=6_000_000_000, bytes_accessed=4_000_000, transcendentals=0),
        name="first_step_own",
    )(state, table, *in_hbm(light, mixing, kappa, wet))


def second_middle(every_column, head, middle, tail, table, mixing, light, factors):
    return call(
        functools.partial(second_middle_kernel, every_column), "second_step_middle", 3_500_000_000,
        (MIDDLE, SENT, jax.ShapeDtypeStruct((BLOCKS, 2 * ROWS, TILE), bf16)),
        [pltpu.VMEM((GROUPS - 2, GROUP_ROWS, LANE), f32)],
        head, middle, tail, table, mixing, light, *factors,
    )


def second_edge(every_column, head, middle, tail, table, mixing, light, xs):
    return call(
        functools.partial(second_edge_kernel, every_column), "second_step_edges_own", 2_500_000_000, EDGE, [],
        head, middle, tail, table, mixing, light, xs,
    )


def edges(first, every_column, left, right, table, mixing, edge, factors):
    return call(
        functools.partial(edge_kernel, first, every_column),
        "first_step_edges" if first else "second_step_edges", 1_000_000_000,
        (ONE, ONE) if first else (ONE, ONE, SENT),
        [pltpu.VMEM((4, 2 * ROWS, TILE), bf16), pltpu.VMEM((2, GROUP_ROWS, LANE), f32)],
        left, right, table, mixing, edge, *factors,
    )


PAIRS = [(i, j) for i in range(BASIS) for j in range(i, BASIS)]
SUMS = BASIS + 1 + len(PAIRS)
KNOWN = ((range(GROUPS), range(1, SEGS)), (range(1, GROUPS - 1), (0,)))
UNKNOWN = (((0, GROUPS - 1), (0,)),)


def pieces_of(areas):
    for groups, segs in areas:
        for group in groups:
            for chunk in range(CHUNKS):
                lanes = pl.ds(group * HALO + chunk * LANE, LANE)
                for seg in segs:
                    for tracer in range(TRACERS):
                        for level in range(0, LEV, 8):
                            yield group, chunk, seg, tracer, level, pl.ds(level, 8), lanes


def residual_at(place, state_ref, wet_ref, before):
    group, chunk, seg, tracer, level, rows, lanes = place
    wet = jnp.broadcast_to(wet_ref[pl.ds(group * CHUNKS + chunk, 1), :], (8, LANE))
    here = wet > lax.broadcasted_iota(jnp.int32, (8, LANE), 0) + level
    return jnp.where(here, state_ref[seg, tracer, rows, lanes] - before, 0.0)


def basis_at(place, basis_ref):
    _, _, seg, tracer, _, rows, lanes = place
    return [basis_ref[i, seg, tracer, rows, lanes] for i in range(BASIS)]


def add_products(sums, vectors):
    for at, (i, j) in enumerate(PAIRS):
        sums[at] = sums[at] + vectors[i] * vectors[j]


def add_rest(sums, vectors, value, guess):
    for i in range(BASIS):
        value = value - guess[i] * vectors[i]
    for i in range(BASIS):
        sums[i] = sums[i] + vectors[i] * value
    sums[BASIS] = sums[BASIS] + value * value


def symmetric(values):
    matrix = [[None] * BASIS for _ in range(BASIS)]
    for (i, j), value in zip(PAIRS, values):
        matrix[i][j] = matrix[j][i] = value
    return matrix


def whole_sum(value):
    return jnp.sum(jnp.sum(value, axis=0, keepdims=True), axis=1, keepdims=True)


def least_squares(products, right):
    gram = symmetric(products)
    factor = [[None] * BASIS for _ in range(BASIS)]
    pivots, inverses, weights = [], [], []
    for i in range(BASIS):
        for j in range(i):
            value = gram[i][j]
            for k in range(j):
                value = value - factor[i][k] * pivots[k] * factor[j][k]
            factor[i][j] = value * inverses[j]
        pivot = gram[i][i]
        for k in range(i):
            pivot = pivot - factor[i][k] * factor[i][k] * pivots[k]
        usable = (pivot > 1e-3 * gram[i][i]) & (pivot > 1e-30)
        pivots.append(pivot)
        inverses.append(jnp.where(usable, 1.0 / jnp.where(usable, pivot, 1.0), 0.0))
        value = right[i]
        for k in range(i):
            value = value - factor[i][k] * weights[k]
        weights.append(value)
    for i in range(BASIS - 1, -1, -1):
        value = weights[i] * inverses[i]
        for k in range(i + 1, BASIS):
            value = value - factor[k][i] * weights[k]
        weights[i] = value
    return weights


def early_kernel(
    state_ref, wet_ref, basis_ref, head_ref, middle_ref, tail_ref, came_ref,
    out_ref, residual_ref, sums_ref, guess_ref, sems,
):
    refs = [(head_ref, 0)] + [(middle_ref, i) for i in range(GROUPS - 2)] + [(tail_ref, 0)]
    zero = jnp.zeros((8, LANE), f32)
    first = [zero] * BASIS
    products = [zero] * len(PAIRS)
    for place in pieces_of(KNOWN):
        group, chunk, seg, tracer, level, rows, lanes = place
        if seg:
            ref, at = refs[group]
            before = ref[at, pl.ds(group_row(tracer, chunk, seg - 1) + level, 8), :]
        else:
            before = came_ref[group - 1, pl.ds((tracer * CHUNKS + chunk) * LEV + level, 8), :]
        value = residual_at(place, state_ref, wet_ref, before)
        residual_ref[seg, tracer, rows, lanes] = value
        vectors = basis_at(place, basis_ref)
        for i in range(BASIS):
            first[i] = first[i] + vectors[i] * value
        add_products(products, vectors)
    parts = [(slice(1, SEGS),), (slice(0, 1), slice(None), slice(None), pl.ds(HALO, WIDTH - 2 * HALO))]
    copies = [pltpu.make_async_copy(residual_ref.at[part], out_ref.at[part], sems.at[i]) for i, part in enumerate(parts)]
    for copy in copies:
        copy.start()
    weights = least_squares([whole_sum(one) for one in products], [whole_sum(one) for one in first])
    guess = [jnp.broadcast_to(weight, (8, LANE)) for weight in weights]
    sums = [zero] * (BASIS + 1)
    for place in pieces_of(KNOWN):
        _, _, seg, tracer, _, rows, lanes = place
        add_rest(sums, basis_at(place, basis_ref), residual_ref[seg, tracer, rows, lanes], guess)
    for place in pieces_of(UNKNOWN):
        add_products(products, basis_at(place, basis_ref))
    for i, one in enumerate(sums + products):
        sums_ref[i] = one
    for i, one in enumerate(guess):
        guess_ref[i] = one
    for copy in copies:
        copy.wait()


def late_kernel(state_ref, wet_ref, basis_ref, came_ref, early_ref, guess_ref, pieces_ref, sums_ref):
    guess = [guess_ref[i] for i in range(BASIS)]
    sums = [early_ref[i] for i in range(SUMS)]
    for place in pieces_of(UNKNOWN):
        group, chunk, seg, tracer, level, rows, lanes = place
        before = came_ref[EDGE_PLACES[group], pl.ds((tracer * CHUNKS + chunk) * LEV + level, 8), :]
        value = residual_at(place, state_ref, wet_ref, before)
        pieces_ref[EDGE_PLACES[group], tracer, rows, pl.ds(chunk * LANE, LANE)] = value
        add_rest(sums, basis_at(place, basis_ref), value, guess)
    lane = lax.broadcasted_iota(jnp.int32, (8, LANE), 1)
    row = jnp.zeros((8, LANE), f32)
    for i, one in enumerate([whole_sum(one) for one in sums] + guess):
        row = jnp.where(lane == i, one, row)
    for i in range(sums_ref.shape[0] // 8):
        sums_ref[pl.ds(8 * i, 8), :] = row


def early(state, wet, basis, head, middle, tail, came):
    whole = shape(SEGS, TRACERS, LEV, WIDTH)
    return pl.pallas_call(
        early_kernel,
        out_shape=(whole, whole, shape(SUMS, 8, LANE), shape(BASIS, 8, LANE)),
        in_specs=[VMEM] * 7,
        out_specs=(HBM, VMEM, VMEM, VMEM),
        scratch_shapes=[pltpu.SemaphoreType.DMA((2,))],
        compiler_params=PARAMS,
        cost_estimate=pl.CostEstimate(flops=10_000_000, bytes_accessed=4_000_000, transcendentals=0),
        name="residual_known",
    )(state, wet, basis, head, middle, tail, came)


def late(devices, state, wet, basis, came, sums, guess):
    return call(
        late_kernel, "residual_last", 3_000_000, (shape(2, TRACERS, LEV, HALO), shape(devices, LANE)), [],
        state, wet, basis, came, sums, guess,
    )


def scaled_kernel(
    count, residual_ref, pieces_ref, basis_ref, sums_ref, unused_ref,
    out_ref, new_out_ref, coefficients_ref, new_ref, sems,
):
    copies = []

    def send(from_ref, to_ref):
        copies.append(pltpu.make_async_copy(from_ref, to_ref, sems.at[len(copies)]))
        copies[-1].start()

    for group, place in EDGE_PLACES.items():
        send(pieces_ref.at[place], out_ref.at[0, :, :, pl.ds(group * HALO, HALO)])
    sums = sums_ref[...]
    if sums.shape[0] < LANE:
        sums = jnp.concatenate([sums, jnp.zeros((LANE - sums.shape[0], LANE), f32)], axis=0)
    sums = sums.T
    row = [sums[i : i + 1] for i in range(SUMS + BASIS)]
    of_rest, squares, products, guess = row[:BASIS], row[BASIS], row[BASIS + 1 : SUMS], row[SUMS:]
    gram = symmetric(products)
    first = [of_rest[i] + sum(gram[i][j] * guess[j] for j in range(BASIS)) for i in range(BASIS)]
    totals = jnp.concatenate(first + products + [jnp.zeros((2, LANE), f32)], axis=0)
    totals = jnp.sum(totals, axis=1, keepdims=True)
    one = [totals[i : i + 1] for i in range(SUMS)]
    first, products = one[:BASIS], one[BASIS : SUMS - 1]
    whole_gram = symmetric(products)
    second = [first[i] - sum(whole_gram[i][j] * first[j] for j in range(BASIS)) for i in range(BASIS)]
    both = [first[i] + second[i] for i in range(BASIS)]
    away = [both[i] - guess[i] for i in range(BASIS)]
    for i in range(BASIS):
        squares = squares + away[i] * (sum(gram[i][j] * away[j] for j in range(BASIS)) - 2.0 * of_rest[i])
    square = jnp.maximum(jnp.sum(squares, axis=1, keepdims=True), 0.0)
    spread = jnp.sqrt(square / count + epsilon)
    lane = lax.broadcasted_iota(jnp.int32, (8, LANE), 1)
    result = jnp.zeros((8, LANE), f32)
    for i, value in enumerate(both + [spread]):
        result = jnp.where(lane == i, value, result)
    coefficients_ref[...] = result[0, : BASIS + 1]
    scale = 1.0 / spread
    weights = [jnp.broadcast_to(-value * scale, (LEV, LANE)) for value in both]
    scale = jnp.broadcast_to(scale, (LEV, LANE))
    for seg in range(SEGS):
        for tracer in range(TRACERS):
            for chunk in range(WIDTH // LANE):
                lanes = pl.ds(chunk * LANE, LANE)
                group = chunk // CHUNKS
                if seg == 0 and group in EDGE_PLACES:
                    here = pieces_ref[EDGE_PLACES[group], tracer, :, pl.ds(chunk % CHUNKS * LANE, LANE)]
                else:
                    here = residual_ref[seg, tracer, :, lanes]
                total = here * scale
                for i in range(BASIS):
                    total = total + weights[i] * basis_ref[i, seg, tracer, :, lanes]
                new_ref[seg, tracer, :, lanes] = total
            send(new_ref.at[seg, tracer], new_out_ref.at[seg, tracer])
    for copy in copies:
        copy.wait()


def scaled(count, residual, pieces, basis, sums, out):
    whole = (SEGS, TRACERS, LEV, WIDTH)
    return pl.pallas_call(
        functools.partial(scaled_kernel, count),
        out_shape=(shape(*whole), shape(*whole), shape(BASIS + 1)),
        in_specs=[VMEM] * 4 + [HBM],
        out_specs=(HBM, HBM, VMEM),
        scratch_shapes=[pltpu.VMEM(whole, f32), pltpu.SemaphoreType.DMA((2 + SEGS * TRACERS,))],
        input_output_aliases={4: 0},
        compiler_params=PARAMS,
        cost_estimate=pl.CostEstimate(flops=4_000_000, bytes_accessed=4_000_000, transcendentals=0),
        name="orthogonal_and_scaled",
    )(residual, pieces, basis, sums, out)


def shifted(block, axis, distance):
    count = lax.axis_size(axis)
    return lax.ppermute(block, axis, [(i, (i + distance) % count) for i in range(count)])


def per_device(segment_state, light, mixing, kappa, neighbour_columns, wet_levels, basis):
    every_column = lax.axis_size("col") * WIDTH
    table = neighbour_columns.T
    wet = wet_levels.reshape(WIDTH // LANE, LANE)
    head, tail, state, table = halves(segment_state, table)
    left = shifted(tail, "col", 1)
    right = shifted(head, "col", -1)
    edge, middle, *factors, light, mixing, wet = first_own(every_column, state, table, light, mixing, kappa, wet)
    head, tail = edges(True, every_column, left, right, table, mixing, edge, factors)
    left = shifted(tail, "col", 1)
    right = shifted(head, "col", -1)
    end_middle, sent, xs = second_middle(every_column, head, middle, tail, table, mixing, light, factors)
    came_middle = shifted(sent, "seg", 1)
    edge = second_edge(every_column, head, middle, tail, table, mixing, light, xs)
    head, tail, sent = edges(False, every_column, left, right, table, mixing, edge, factors)
    came_edge = shifted(sent, "seg", 1)
    residual, held, sums, guess = early(state, wet, basis, head, end_middle, tail, came_middle)
    devices = lax.axis_size("seg") * lax.axis_size("col")
    pieces, sums = late(devices, state, wet, basis, came_edge, sums, guess)
    sums = lax.all_to_all(sums, ("seg", "col"), 0, 0, tiled=True)
    count = lax.axis_size("seg") * SEGS * TRACERS * LEV * every_column
    return scaled(count, held, pieces, basis, sums, residual)


def solution(mesh):
    return jax.shard_map(
        per_device,
        mesh=mesh,
        in_specs=(
            P("seg", None, None, "col"),
            P("seg", None, "col"),
            P("seg", None, None, "col"),
            P("seg", None, "col"),
            P("col", None),
            P("col"),
            P(None, "seg", None, None, "col"),
        ),
        out_specs=(P("seg", None, None, "col"), P("seg", None, None, "col"), P()),
        check_vma=False,
    )
```
